128 devices in a mesh: group: 4 (over z), dev: 32 (over x, y, core).
Axes of the slice: x: 4, y: 4, z: 4, core: 2. Of those that a mesh axis runs over, the one named last changes fastest.
Arguments:
- prompt_cache: bfloat16 [128, 2048, 576], P('group', 'dev'), may hold values from -6 to 6
- assignment: int32 [4, 32], P('group'), may hold values from 0 to 31, each once within a row
- resident_cache: bfloat16 [384, 512, 576], P(('group', 'dev')), may hold values from -6 to 6
- resident_len: int32 [128, 3], P(('group', 'dev')), may hold values from 1 to 512, 1024 in all within a row
- queries: bfloat16 [512, 128, 576], P(('group', 'dev')), may hold values from -240 to 240
- new_latent: bfloat16 [512, 576], P(('group', 'dev')), may hold values from -6 to 6
- residual: bfloat16 [512, 7168], P(('group', 'dev')), may hold values from -4 to 4
- w_uv: bfloat16 [128, 512, 128], P('dev'), may hold values from -0.25 to 0.25
- w_out: bfloat16 [16384, 7168], P('dev'), may hold values from -0.125 to 0.125
- norm_gain: bfloat16 [7168], replicated, may hold values from 0.25 to 1.75
- w_router: bfloat16 [7168, 32], replicated, may hold values from -0.125 to 0.125
- expert_ids: int32 [512, 8], replicated, may hold values from 0 to 31, all different within a row; in each aligned block of 512 rows (0 to 511, 512 to 1023, ...) at most 192 rows name the same one
- w_gate: bfloat16 [128, 7168, 256], P(('group', 'dev')), may hold values from -0.0625 to 0.0625
- w_up: bfloat16 [128, 7168, 256], P(('group', 'dev')), may hold values from -0.0625 to 0.0625
- w_down: bfloat16 [128, 256, 7168], P(('group', 'dev')), may hold values from -0.375 to 0.375
Outputs:
- layer_out: bfloat16 [512, 7168], P(('group', 'dev'))
The draws below stay inside these ranges and needn't reach their ends.
Inputs may be any that keep to these rules, and one draw needn't show every extreme that they name: Each group's row of assignment names each of the 32 decode devices of that group once. `resident_len`: each device's 3 lengths sum to 1024. `expert_ids`: each row names 8 different experts; no expert is named by more than 192 rows.
All inputs are finite; a program needn't handle non-finite values.
Results may differ from the reference program's by a relative error of at most 0.033.
Values may be sent and summed in bfloat16 or wider, within the bound.
No kernel may reach another device: no remote copies, remote signals or barrier semaphores. Data moves between devices by JAX's collectives and lax.ppermute only.
A program may use at most 128 MiB of HBM per device.

```python
import math
import jax
import jax.numpy as jnp
import numpy as np
from jax import lax

D = 7168
H = 128
LAT = 512
ROPE = 64
NOPE = 128
VH = 128
FF_EXP = 1024
TOPK = 8
PLEN = 2048
RES = 3
RCAP = 512
KV = 576
PROMPTS = 128
ROWS_ALL = 512
EXPERTS = 32
SLICES = 4
FF_SLICE = 256
CAP = 192
N_GROUP = 4
N_DEV = 32
DEVICES = 128


def draw_queries(key, part):
    key = jax.random.fold_in(key, 7)
    first_key, second_key = jax.random.split(key)
    base = jnp.clip(jax.random.normal(first_key, (ROWS_ALL, H, KV), jnp.float32), -6.0, 6.0)
    spread = 1.5 * jnp.exp(jax.random.uniform(second_key, (ROWS_ALL, H, 1), jnp.float32, -0.5, 0.5))
    return (base * spread).astype(jnp.bfloat16)


def level_of(key, extent, cuts, smallest, top_value):
    def one(axis_at, shards_of):
        heights = jax.random.uniform(jax.random.fold_in(jax.random.fold_in(key, 6), axis_at), (shards_of,), jnp.float32, smallest / len(cuts), top_value / len(cuts))
        return jnp.repeat(jnp.exp(heights), extent[axis_at] // shards_of).reshape((-1,) + (1,) * (len(extent) - axis_at - 1))

    level = one(*cuts[0])
    for cut in cuts[1:]:
        level = level * one(*cut)
    return level


def split_up(number_of, total, most, lean):
    loads = [(1 << 20) // math.isqrt(rank ** lean) + 1 for rank in range(2, number_of + 1)]
    rest, counts = total - most - (number_of - 1), [1] * (number_of - 1)
    while rest > 0:
        movable = [i for i in range(number_of - 1) if counts[i] < most]
        pool, budget = sum([loads[i] for i in movable]), rest
        for i in movable:
            addition = min(most - counts[i], max(1, budget * loads[i] // pool), rest)
            counts[i] = counts[i] + addition
            rest = rest - addition
    return np.array([most] + counts)


def ragged(stream_key, count, total, bound, slope):
    if count == 2:
        one = jax.random.randint(stream_key, (), max(1, total - bound), min(bound, total - 1) + 1)
        return jnp.stack([one, total - one])
    sizes = jnp.asarray(split_up(count, total, bound, slope), jnp.int32)
    twos = (count - 1) // 2
    donor, receiver = sizes[1:1 + 2 * twos:2], sizes[2:2 + 2 * twos:2]
    margin = jnp.minimum(donor - 1, bound - receiver)
    moved = jax.random.randint(jax.random.fold_in(stream_key, 1), (twos,), 0, 1 << 20) % (margin + 1)
    sizes = sizes.at[1:1 + 2 * twos:2].set(donor - moved).at[2:2 + 2 * twos:2].set(receiver + moved)
    return sizes[jax.random.permutation(jax.random.fold_in(stream_key, 2), count)]


def assign_block(rng, own, number, rows, amount, top, limit, skew):
    ranking = jax.random.permutation(rng, amount)
    crowded, common = portions_of(amount, rows * top, limit, skew, True), portions_of(amount, rows * top, limit, skew, False)
    places = jnp.arange(amount)

    def named(tallies, turn):
        used = int((tallies > 0).sum())
        fixed = max(1, used // 4)
        passed = fixed + (places - fixed + turn * (used - fixed)) % max(1, amount - fixed)
        return jnp.zeros((amount,), jnp.int32).at[ranking[jnp.where(places < fixed, places, passed)]].set(jnp.asarray(tallies, jnp.int32))

    tallies = jnp.where(number % 4 == 0, named(crowded, number // 4), named(common, number - number // 4 - 1))
    mixed = jax.random.permutation(jax.random.fold_in(own, 3), amount)
    source_of, receiver = mixed[0:amount // 2 * 2:2], mixed[1:amount // 2 * 2:2]
    slack = jnp.minimum(tallies[source_of] - 1, limit - tallies[receiver]) // 2
    slack = jnp.where((source_of == ranking[0]) | (receiver == ranking[0]) | (tallies[receiver] == 0), 0, jnp.maximum(slack, 0))
    passed = jax.random.randint(jax.random.fold_in(own, 4), (amount // 2,), 0, 1 << 20) % (slack + 1)
    tallies = tallies.at[source_of].add(-passed).at[receiver].add(passed)
    members = jnp.searchsorted(jnp.cumsum(tallies), jnp.arange(rows * top), side="right").astype(jnp.int32)
    table = members.reshape(top, rows).T
    table = table[jax.random.permutation(jax.random.fold_in(own, 1), rows)]
    turn = jax.random.randint(jax.random.fold_in(own, 2), (rows, 1), 0, top)
    return jnp.take_along_axis(table, (jnp.arange(top)[None, :] + turn) % top, axis=1)


def portions_of(amount, total, bound, slope, full):
    portions = [(1 << 20) // math.isqrt(rank ** slope) + 1 for rank in range(1, amount + 1)]
    largest = bound if full else min(bound, max(-(-total // amount), total * portions[0] // sum(portions)))
    least = 1 if total - largest >= amount - 1 else 0
    given, surplus = [largest] + [least] * (amount - 1), total - largest - least * (amount - 1)
    while surplus > 0:
        free = [i for i in range(1, amount) if given[i] < largest] or [i for i in range(1, amount) if given[i] < bound]
        pool, remaining = sum([portions[i] for i in free]), surplus
        for i in free:
            extra = min(bound - given[i], max(1, remaining * portions[i] // pool), surplus)
            given[i] = given[i] + extra
            surplus = surplus - extra
    return np.array(given)


def centred(rng, shape, scale, bound, cuts=(), kind=jnp.bfloat16):
    result = scale * jax.random.normal(rng, shape, jnp.float32)
    if cuts:
        result = result * level_of(rng, shape, cuts, -0.22, 0.18)
    return jnp.clip(result, -bound, bound).astype(kind)


def setup_inputs(seed: int = 0) -> dict:
    seeds = jax.random.split(jax.random.key(seed), 16)
    prompt_cache = centred(seeds[0], (PROMPTS, PLEN, KV), 1.0, 6.0, ((0, 4), (1, 32)))
    assignment = jax.vmap(lambda own: jax.random.permutation(own, N_DEV))(jax.random.split(seeds[1], N_GROUP)).reshape((N_GROUP, N_DEV)).astype(jnp.int32)
    resident_cache = centred(seeds[2], (DEVICES * RES, RCAP, KV), 1.0, 6.0, ((0, 128),))
    resident_len = jax.vmap(lambda own: ragged(own, RES, RCAP + (RES - 1) * RCAP // 2, RCAP, 2))(jax.random.split(seeds[3], DEVICES)).reshape((DEVICES, RES)).astype(jnp.int32)
    queries = draw_queries(jax.random.fold_in(seeds[15], 71), 0)
    new_latent = centred(seeds[5], (ROWS_ALL, KV), 1.0, 6.0, ((0, 128),))
    residual = centred(seeds[6], (ROWS_ALL, D), 0.3, 4.0, ((0, 128),))
    w_uv = centred(seeds[7], (H, LAT, VH), LAT ** -0.5, 0.25, ((0, 32),))
    w_out = centred(seeds[8], (H * VH, D), (H * VH // 8) ** -0.5, 0.125, ((0, 32),))
    norm_gain = jnp.clip(1.0 + 0.15 * jax.random.normal(seeds[9], (D,), jnp.float32), 0.25, 1.75).astype(jnp.bfloat16)
    w_router = centred(seeds[10], (D, EXPERTS), (D // 4) ** -0.5, 0.125)
    expert_ids_keys = jax.random.split(jax.random.fold_in(seeds[11], 1), ROWS_ALL // ROWS_ALL)
    expert_ids_turns = jax.random.permutation(jax.random.fold_in(seeds[11], 3), ROWS_ALL // ROWS_ALL)
    expert_ids = jax.vmap(lambda own, number: assign_block(jax.random.fold_in(seeds[11], 2), own, number, ROWS_ALL, EXPERTS, TOPK, CAP, 2))(expert_ids_keys, expert_ids_turns).reshape((ROWS_ALL, TOPK))
    w_gate = centred(seeds[12], (DEVICES, D, FF_SLICE), D ** -0.5, 0.0625, ((0, 128),))
    w_up = centred(seeds[13], (DEVICES, D, FF_SLICE), D ** -0.5, 0.0625, ((0, 128),))
    w_down = centred(seeds[14], (DEVICES, FF_SLICE, D), (FF_EXP // 4) ** -0.5, 0.375, ((0, 128),))
    return dict(prompt_cache=prompt_cache, assignment=assignment, resident_cache=resident_cache, resident_len=resident_len, queries=queries, new_latent=new_latent, residual=residual, w_uv=w_uv, w_out=w_out, norm_gain=norm_gain, w_router=w_router, expert_ids=expert_ids, w_gate=w_gate, w_up=w_up, w_down=w_down)


def attend(query_row, cache_block, valid_mask, own_entry):
    scale_factor = (NOPE + ROPE) ** (-0.5)
    query_wide = query_row.astype(jnp.float32)
    scores = jnp.einsum('hc,kc->hk', query_wide, cache_block.astype(jnp.float32)) * scale_factor
    scores = jnp.where(valid_mask[None, :], scores, -jnp.inf)
    own_score = jnp.einsum('hc,c->h', query_wide, own_entry.astype(jnp.float32)) * scale_factor
    maximum = jnp.maximum(lax.optimization_barrier(jnp.max(scores, axis=1)), own_score)
    exponent = jnp.exp(scores - maximum[:, None])
    own_exponent = jnp.exp(own_score - maximum)
    totals = lax.optimization_barrier(jnp.sum(exponent, axis=1)) + own_exponent
    weights = (exponent / totals[:, None]).astype(jnp.bfloat16)
    own_weight = (own_exponent / totals).astype(jnp.bfloat16)
    context = jnp.einsum('hk,kl->hl', weights.astype(jnp.float32), cache_block[:, :LAT].astype(jnp.float32))
    context = context + own_weight.astype(jnp.float32)[:, None] * own_entry[:LAT].astype(jnp.float32)[None, :]
    return context.astype(jnp.bfloat16)

def norm_rows(hidden, norm_gain):
    hidden_wide = hidden.astype(jnp.float32)
    scale_rows = lax.rsqrt(lax.optimization_barrier(jnp.mean(hidden_wide * hidden_wide, axis=1, keepdims=True)) + 1e-06)
    return (hidden_wide * scale_rows * norm_gain.astype(jnp.float32)[None, :]).astype(jnp.bfloat16)

def route_gates(normed, w_router, expert_ids):
    logits = jnp.dot(normed, w_router, preferred_element_type=jnp.float32)
    affinity = jax.nn.sigmoid(logits)
    picked = jnp.take_along_axis(affinity, expert_ids, axis=1)
    return (2.5 * picked / lax.optimization_barrier(jnp.sum(picked, axis=1, keepdims=True))).astype(jnp.bfloat16)

def reference(prompt_cache, assignment, resident_cache, resident_len, queries, new_latent, residual, w_uv, w_out, norm_gain, w_router, expert_ids, w_gate, w_up, w_down):
    rows_dev = RES + 1
    owner_match = (assignment[:, None, :] == jnp.arange(N_DEV, dtype=jnp.int32)[None, :, None]).astype(jnp.int32)
    chosen = lax.optimization_barrier(jnp.sum(owner_match * jnp.arange(N_DEV, dtype=jnp.int32)[None, None, :], axis=2))
    prompt_index = (jnp.arange(N_GROUP, dtype=jnp.int32)[:, None] * N_DEV + chosen).reshape(DEVICES)
    query_grid = queries.reshape(DEVICES, rows_dev, H, KV)
    latent_grid = new_latent.reshape(DEVICES, rows_dev, KV)

    def new_row(device):
        valid_mask = jnp.arange(PLEN, dtype=jnp.int32) >= 0
        return attend(query_grid[device, 0], prompt_cache[prompt_index[device]], valid_mask, latent_grid[device, 0])
    context_new = lax.map(new_row, jnp.arange(DEVICES, dtype=jnp.int32))
    lengths_flat = resident_len.reshape(DEVICES * RES)
    old_queries = query_grid[:, 1:].reshape(DEVICES * RES, H, KV)
    old_latent = latent_grid[:, 1:].reshape(DEVICES * RES, KV)

    def old_row(member):
        valid_mask = jnp.arange(RCAP, dtype=jnp.int32) < lengths_flat[member]
        return attend(old_queries[member], resident_cache[member], valid_mask, old_latent[member])
    context_old = lax.map(old_row, jnp.arange(DEVICES * RES, dtype=jnp.int32)).reshape(DEVICES, RES, H, LAT)
    context = jnp.concatenate([context_new[:, None], context_old], axis=1).reshape(ROWS_ALL, H, LAT)
    attn_values = jnp.einsum('rhl,hlv->rhv', context.astype(jnp.float32), w_uv.astype(jnp.float32)).astype(jnp.bfloat16)
    attention = jnp.dot(attn_values.reshape(ROWS_ALL, H * VH), w_out, preferred_element_type=jnp.float32)
    hidden = (residual.astype(jnp.float32) + attention).astype(jnp.bfloat16)
    normed = norm_rows(hidden, norm_gain)
    gate_values = route_gates(normed, w_router, expert_ids)
    flat_ids = expert_ids.reshape(ROWS_ALL * TOPK)
    one_hot = (flat_ids[:, None] == jnp.arange(EXPERTS, dtype=jnp.int32)[None, :]).astype(jnp.int32)
    slot_ranks = jnp.cumsum(one_hot, axis=0) - one_hot
    slot_flat = lax.optimization_barrier(jnp.sum(slot_ranks * one_hot, axis=1))
    row_flat = jnp.arange(ROWS_ALL * TOPK, dtype=jnp.int32) // TOPK
    slot_rows = jnp.full((EXPERTS, CAP), ROWS_ALL, jnp.int32).at[flat_ids, slot_flat].set(row_flat)
    slot_gates = jnp.zeros((EXPERTS, CAP), jnp.float32).at[flat_ids, slot_flat].set(gate_values.reshape(ROWS_ALL * TOPK).astype(jnp.float32))
    padded = jnp.concatenate([normed, jnp.zeros((1, D), jnp.bfloat16)], axis=0)

    def expert_term(expert):
        inputs = padded[slot_rows[expert]].astype(jnp.float32)
        gate_block = lax.dynamic_slice_in_dim(w_gate, expert * SLICES, SLICES, 0).astype(jnp.float32)
        up_block = lax.dynamic_slice_in_dim(w_up, expert * SLICES, SLICES, 0).astype(jnp.float32)
        down_block = lax.dynamic_slice_in_dim(w_down, expert * SLICES, SLICES, 0).astype(jnp.float32)
        gate_proj = jnp.einsum('cd,sdf->csf', inputs, gate_block)
        up_proj = jnp.einsum('cd,sdf->csf', inputs, up_block)
        activation = (jax.nn.silu(gate_proj) * up_proj).astype(jnp.bfloat16)
        expert_out = jnp.einsum('csf,sfd->cd', activation.astype(jnp.float32), down_block)
        return expert_out * slot_gates[expert][:, None]
    terms = lax.map(expert_term, jnp.arange(EXPERTS, dtype=jnp.int32))
    moe = jnp.zeros((ROWS_ALL + 1, D), jnp.float32).at[slot_rows.reshape(EXPERTS * CAP)].add(terms.reshape(EXPERTS * CAP, D))[:ROWS_ALL]
    return (hidden.astype(jnp.float32) + moe).astype(jnp.bfloat16)
```

```python
import functools

import jax
import jax.numpy as jnp
from jax import lax
from jax.experimental import pallas as pl
from jax.experimental.pallas import tpu as pltpu
from jax.sharding import Mesh, PartitionSpec as P

LAT = 512
ROPE = 64
NOPE = 128
D = 7168
CAP = 192
NZ, NX, NY, NC = 4, 4, 4, 2
NXY = NX * NY
NDEV = NXY * NC
EXP_G = 8
CHUNK = D // NDEV
LANES = 256
GROUP = 4
BLK = CHUNK * GROUP
STEPS = NXY // GROUP
ROWS = 128
ALL_ROWS = ROWS * NZ
F32 = jnp.float32
BF16 = jnp.bfloat16
VMEM = 48 * 1024 * 1024


def attend(query_row, cache_block, valid_mask, own_entry):
    scale_factor = (NOPE + ROPE) ** (-0.5)
    scores = jnp.einsum("hc,kc->hk", query_row, cache_block, preferred_element_type=F32) * scale_factor
    if valid_mask is not None:
        scores = jnp.where(valid_mask[None, :], scores, -jnp.inf)
    own_score = jnp.einsum("hc,c->h", query_row, own_entry, preferred_element_type=F32) * scale_factor
    maximum = jnp.maximum(jnp.max(scores, axis=1), own_score)
    exponent = jnp.exp(scores - maximum[:, None])
    own_exponent = jnp.exp(own_score - maximum)
    totals = jnp.sum(exponent, axis=1) + own_exponent
    weights = (exponent / totals[:, None]).astype(BF16)
    own_weight = (own_exponent / totals).astype(BF16)
    context = jnp.einsum("hk,kl->hl", weights, cache_block[:, :LAT], preferred_element_type=F32)
    context = context + own_weight.astype(F32)[:, None] * own_entry[:LAT].astype(F32)[None, :]
    return context.astype(BF16)


def project_kernel(half_ref, attn_ref, place_ref, res_ref, w_ref, out_ref):
    acc = jnp.dot(attn_ref[...], w_ref[...], preferred_element_type=F32)
    acc = acc + jnp.dot(place_ref[...], res_ref[...], preferred_element_type=F32)
    for g in range(GROUP):
        part = acc[:, g * CHUNK : (g + 1) * CHUNK]
        out_ref[g, :, :CHUNK] = part.astype(out_ref.dtype)
        out_ref[g, :, CHUNK:] = jnp.zeros((ROWS, LANES - CHUNK), out_ref.dtype)


def project(half, attn, place, res, w_out, dtype):
    depth = attn.shape[1]
    return pl.pallas_call(
        project_kernel,
        grid_spec=pltpu.PrefetchScalarGridSpec(
            num_scalar_prefetch=1,
            grid=(STEPS,),
            in_specs=[
                pl.BlockSpec((ROWS, depth), lambda i, h: (0, 0)),
                pl.BlockSpec((ROWS, 16), lambda i, h: (0, 0)),
                pl.BlockSpec((16, BLK), lambda i, h: (0, h[0] * STEPS + i)),
                pl.BlockSpec((depth, BLK), lambda i, h: (0, h[0] * STEPS + i)),
            ],
            out_specs=pl.BlockSpec((GROUP, ROWS, LANES), lambda i, h: (i, 0, 0)),
        ),
        out_shape=jax.ShapeDtypeStruct((NXY, ROWS, LANES), dtype),
        compiler_params=pltpu.CompilerParams(vmem_limit_bytes=VMEM),
        cost_estimate=pl.CostEstimate(
            flops=2 * ROWS * depth * D // 2, bytes_accessed=depth * D + 2 * ROWS * D, transcendentals=0
        ),
        name="project",
    )(half, attn, place, res, w_out)


def gate_up_step(y_ref, wg_ref, wu_ref, gate, up, stats):
    for g in range(GROUP):
        rows = y_ref[g, :, :CHUNK]
        gate = gate + jnp.dot(rows, wg_ref[g * CHUNK : (g + 1) * CHUNK, :], preferred_element_type=F32)
        up = up + jnp.dot(rows, wu_ref[g * CHUNK : (g + 1) * CHUNK, :], preferred_element_type=F32)
        stats = stats + y_ref[g, :, CHUNK:].astype(F32)
    return gate, up, stats


def first_kernel(half_ref, y_ref, wg_ref, wu_ref, gate_ref, up_ref, stats_ref):
    @pl.when(pl.program_id(0) == 0)
    def _():
        gate_ref[...] = jnp.zeros_like(gate_ref)
        up_ref[...] = jnp.zeros_like(up_ref)
        stats_ref[...] = jnp.zeros_like(stats_ref)

    gate, up, stats = gate_up_step(y_ref, wg_ref, wu_ref, gate_ref[...], up_ref[...], stats_ref[...])
    gate_ref[...] = gate
    up_ref[...] = up
    stats_ref[...] = stats


def first_half(half, y, w_gate, w_up):
    hidden = w_gate.shape[1]
    acc = pl.BlockSpec((CAP, hidden), lambda i, h: (0, 0))
    return pl.pallas_call(
        first_kernel,
        grid_spec=pltpu.PrefetchScalarGridSpec(
            num_scalar_prefetch=1,
            grid=(STEPS,),
            in_specs=[
                pl.BlockSpec((GROUP, CAP, LANES), lambda i, h: (i, 0, 0)),
                pl.BlockSpec((BLK, hidden), lambda i, h: (h[0] * STEPS + i, 0)),
                pl.BlockSpec((BLK, hidden), lambda i, h: (h[0] * STEPS + i, 0)),
            ],
            out_specs=[acc, acc, pl.BlockSpec((CAP, LANES - CHUNK), lambda i, h: (0, 0))],
        ),
        out_shape=[
            jax.ShapeDtypeStruct((CAP, hidden), F32),
            jax.ShapeDtypeStruct((CAP, hidden), F32),
            jax.ShapeDtypeStruct((CAP, LANES - CHUNK), F32),
        ],
        compiler_params=pltpu.CompilerParams(vmem_limit_bytes=VMEM),
        cost_estimate=pl.CostEstimate(
            flops=2 * CAP * D * hidden, bytes_accessed=2 * D * hidden + CAP * D, transcendentals=0
        ),
        name="gate_up_first",
    )(half, y, w_gate, w_up)


def down_step(act, gates, wd_ref, out_ref):
    acc = jnp.dot(act, wd_ref[...], preferred_element_type=F32) * gates
    for g in range(GROUP):
        out_ref[g, :, :CHUNK] = acc[:, g * CHUNK : (g + 1) * CHUNK].astype(out_ref.dtype)
        out_ref[g, :, CHUNK:] = jnp.zeros((CAP, LANES - CHUNK), out_ref.dtype)


def second_kernel(
    half_ref, y_ref, wg_ref, wu_ref, wd_ref, gate0_ref, up0_ref, stats0_ref, mine_ref,
    act_ref, gates_ref, out_ref, gate_acc, up_acc, stats_acc,
):
    step = pl.program_id(0)

    @pl.when(step == 0)
    def _():
        gate_acc[...] = gate0_ref[...]
        up_acc[...] = up0_ref[...]
        stats_acc[...] = stats0_ref[...]

    @pl.when(step < STEPS)
    def _():
        gate, up, stats = gate_up_step(y_ref, wg_ref, wu_ref, gate_acc[...], up_acc[...], stats_acc[...])
        gate_acc[...] = gate
        up_acc[...] = up
        stats_acc[...] = stats

    @pl.when(step == STEPS - 1)
    def _():
        stats = stats_acc[...]
        square = stats[:, 16:17] + stats[:, 17:18]
        scale = lax.rsqrt(square * (1.0 / D) + 1e-6)
        affinity = jax.nn.sigmoid((stats[:, 0:8] + stats[:, 8:16]) * scale)
        own = jnp.sum(affinity * mine_ref[...], axis=1, keepdims=True)
        gates = 2.5 * own / jnp.sum(affinity, axis=1, keepdims=True)
        gates_ref[...] = jnp.broadcast_to(gates.astype(BF16).astype(F32), gates_ref.shape)
        gate = gate_acc[...] * scale
        up = up_acc[...] * scale
        act_ref[...] = (gate * jax.nn.sigmoid(gate) * up).astype(BF16)

    @pl.when(step >= STEPS)
    def _():
        down_step(act_ref[...], gates_ref[:, :1], wd_ref, out_ref)


def second_half(half, y, w_gate, w_up, w_down, gate, up, stats, mine):
    hidden = w_gate.shape[1]
    fixed = lambda i, h: (0, 0)
    return pl.pallas_call(
        second_kernel,
        grid_spec=pltpu.PrefetchScalarGridSpec(
            num_scalar_prefetch=1,
            grid=(2 * STEPS,),
            in_specs=[
                pl.BlockSpec((GROUP, CAP, LANES), lambda i, h: (jnp.minimum(i, STEPS - 1), 0, 0)),
                pl.BlockSpec((BLK, hidden), lambda i, h: (h[0] * STEPS + jnp.minimum(i, STEPS - 1), 0)),
                pl.BlockSpec((BLK, hidden), lambda i, h: (h[0] * STEPS + jnp.minimum(i, STEPS - 1), 0)),
                pl.BlockSpec((hidden, BLK), lambda i, h: (0, h[0] * STEPS + jnp.maximum(i - STEPS, 0))),
                pl.BlockSpec((CAP, hidden), fixed),
                pl.BlockSpec((CAP, hidden), fixed),
                pl.BlockSpec((CAP, LANES - CHUNK), fixed),
                pl.BlockSpec((CAP, EXP_G), fixed),
            ],
            out_specs=[
                pl.BlockSpec((CAP, hidden), fixed),
                pl.BlockSpec((CAP, 128), fixed),
                pl.BlockSpec((GROUP, CAP, LANES), lambda i, h: (jnp.maximum(i - STEPS, 0), 0, 0)),
            ],
            scratch_shapes=[
                pltpu.VMEM((CAP, hidden), F32),
                pltpu.VMEM((CAP, hidden), F32),
                pltpu.VMEM((CAP, LANES - CHUNK), F32),
            ],
        ),
        out_shape=[
            jax.ShapeDtypeStruct((CAP, hidden), BF16),
            jax.ShapeDtypeStruct((CAP, 128), F32),
            jax.ShapeDtypeStruct((NXY, CAP, LANES), BF16),
        ],
        compiler_params=pltpu.CompilerParams(vmem_limit_bytes=VMEM),
        cost_estimate=pl.CostEstimate(
            flops=3 * CAP * D * hidden, bytes_accessed=3 * D * hidden + 2 * CAP * D, transcendentals=0
        ),
        name="gate_up_second",
    )(half, y, w_gate, w_up, w_down, gate, up, stats, mine)


def down_kernel(half_ref, act_ref, gates_ref, wd_ref, out_ref):
    down_step(act_ref[...], gates_ref[:, :1], wd_ref, out_ref)


def down_half(half, act, gates, w_down):
    hidden = act.shape[1]
    return pl.pallas_call(
        down_kernel,
        grid_spec=pltpu.PrefetchScalarGridSpec(
            num_scalar_prefetch=1,
            grid=(STEPS,),
            in_specs=[
                pl.BlockSpec((CAP, hidden), lambda i, h: (0, 0)),
                pl.BlockSpec((CAP, 128), lambda i, h: (0, 0)),
                pl.BlockSpec((hidden, BLK), lambda i, h: (0, h[0] * STEPS + i)),
            ],
            out_specs=pl.BlockSpec((GROUP, CAP, LANES), lambda i, h: (i, 0, 0)),
        ),
        out_shape=jax.ShapeDtypeStruct((NXY, CAP, LANES), F32),
        compiler_params=pltpu.CompilerParams(vmem_limit_bytes=VMEM),
        cost_estimate=pl.CostEstimate(
            flops=CAP * D * hidden, bytes_accessed=D * hidden + 2 * CAP * D, transcendentals=0
        ),
        name="down_own",
    )(half, act, gates, w_down)


def split_pair(values):
    high = lax.reduce_precision(values, 8, 7)
    low = lax.reduce_precision(values - high, 8, 7)
    return high.astype(BF16), low.astype(BF16)


def swap_cores(values):
    return lax.ppermute(values, "c", [(0, 1), (1, 0)])


def per_device(
    prompt_cache,
    assignment,
    resident_cache,
    resident_len,
    queries,
    new_latent,
    residual,
    w_uv,
    w_out,
    norm_gain,
    w_router,
    expert_ids,
    w_gate,
    w_up,
    w_down,
):
    plane = lax.axis_index("z")
    core = lax.axis_index("c")
    place_xy = lax.axis_index("x") * NY + lax.axis_index("y")
    dev_index = place_xy * NC + core
    rows_dev = queries.shape[0]
    own_half = jnp.reshape(core, (1,)).astype(jnp.int32)
    other_half = 1 - own_half
    chunk = core * NXY + place_xy

    owners = assignment[0]
    dev_iota = jnp.arange(NDEV, dtype=jnp.int32)
    inverse = jnp.sum((owners[None, :] == dev_iota[:, None]).astype(jnp.int32) * dev_iota[None, :], axis=1)
    outgoing = prompt_cache.at[inverse].get(mode="promise_in_bounds")
    received = lax.all_to_all(outgoing, ("x", "y", "c"), 0, 0, tiled=True)

    ids_plane = expert_ids - plane * EXP_G
    named = jnp.any(expert_ids[:, :, None] == jnp.arange(NZ * EXP_G, dtype=jnp.int32)[None, None, :], axis=1)
    lower = (jnp.arange(ALL_ROWS)[:, None] > jnp.arange(ALL_ROWS)[None, :]).astype(BF16)
    ranks = jnp.dot(lower, named.astype(BF16), preferred_element_type=F32).astype(jnp.int32)
    ranks = jnp.where(named, ranks, -1)
    plane_ranks = lax.dynamic_slice_in_dim(ranks, plane * EXP_G, EXP_G, 1)
    slots = (plane_ranks.T[:, None, :] == jnp.arange(CAP, dtype=jnp.int32)[None, :, None]).astype(BF16)
    table = jnp.broadcast_to(slots[:, None], (EXP_G, 2, CAP, ALL_ROWS)).reshape(NXY * CAP, ALL_ROWS)
    own_expert = place_xy // 2
    own_slots = lax.dynamic_index_in_dim(slots, own_expert, 0, keepdims=False)
    slot_ids = jnp.dot(own_slots, ids_plane.astype(BF16), preferred_element_type=F32)
    mine = (slot_ids == own_expert.astype(F32)).astype(F32)
    group_ids = lax.dynamic_slice_in_dim(expert_ids, plane * ROWS, ROWS, 0)
    picks = (group_ids[:, :, None] == jnp.arange(NZ * EXP_G, dtype=jnp.int32)[None, None, :]).astype(F32)
    gain_chunk = lax.dynamic_slice_in_dim(norm_gain, chunk * CHUNK, CHUNK, 0).astype(F32)
    router_chunk = lax.dynamic_slice_in_dim(w_router, chunk * CHUNK, CHUNK, 0)
    row_iota = jnp.arange(ROWS, dtype=jnp.int32)
    place = (row_iota[:, None] == dev_index * rows_dev + jnp.arange(16, dtype=jnp.int32)[None, :]) & (
        jnp.arange(16) < rows_dev
    )[None, :]
    place = place.astype(BF16)
    res = jnp.pad(residual, ((0, 16 - rows_dev), (0, 0)))

    slot_iota = jnp.arange(resident_cache.shape[1], dtype=jnp.int32)
    old_masks = slot_iota[None, :] < resident_len[0][:, None]
    context_old = jax.vmap(attend)(queries[1:], resident_cache, old_masks, new_latent[1:])
    prompt = received.reshape(-1, received.shape[-1])
    context_new = attend(queries[0], prompt, None, new_latent[0])
    context = jnp.concatenate([context_new[None], context_old], axis=0)

    heads = w_uv.shape[0]
    context = context.reshape(rows_dev, NDEV, heads, LAT).transpose(1, 2, 0, 3)
    context = context.reshape(NDEV, heads * rows_dev, LAT)
    context = lax.all_to_all(context, ("x", "y", "c"), 0, 0, tiled=True)
    context = context.reshape(NDEV, heads, rows_dev, LAT)
    attn = jnp.einsum("shrl,hlv->srhv", context, w_uv, preferred_element_type=F32).astype(BF16)
    attn = attn.reshape(ROWS, -1)

    partial_other = project(other_half, attn, place, res, w_out, BF16)
    partial_got = swap_cores(partial_other)
    partial_own = project(own_half, attn, place, res, w_out, F32)
    partial = (partial_own + partial_got.astype(F32)).astype(BF16)
    partial = lax.all_to_all(partial, ("x", "y"), 0, 0, tiled=True)
    hidden = jnp.sum(partial[:, :, :CHUNK].astype(F32), axis=0).astype(BF16)

    hidden_wide = hidden.astype(F32)
    square = jnp.sum(hidden_wide * hidden_wide, axis=1, keepdims=True)
    scaled = (hidden_wide * gain_chunk[None, :]).astype(BF16)
    logits = jnp.dot(scaled, router_chunk, preferred_element_type=F32)
    picked = jnp.sum(picks * logits[:, None, :], axis=2)
    picked_high, picked_low = split_pair(picked)
    square_high, square_low = split_pair(square)
    spare = jnp.zeros((ROWS, LANES - CHUNK - 18), BF16)
    packed = jnp.concatenate([scaled, picked_high, picked_low, square_high, square_low, spare], axis=1)

    packed = jnp.broadcast_to(packed[None], (NZ, ROWS, LANES))
    packed = lax.all_to_all(packed, "z", 0, 0, tiled=True).reshape(ALL_ROWS, LANES)
    slotted = jnp.dot(table, packed, preferred_element_type=F32).astype(BF16).reshape(NXY, CAP, LANES)
    slotted = lax.all_to_all(slotted, ("x", "y"), 0, 0, tiled=True)

    slotted_other = swap_cores(slotted)
    gate, up, stats = first_half(own_half, slotted, w_gate[0], w_up[0])
    act, gates, out_other = second_half(
        other_half, slotted_other, w_gate[0], w_up[0], w_down[0], gate, up, stats, mine
    )
    out_got = swap_cores(out_other)
    out_own = down_half(own_half, act, gates, w_down[0])
    out = (out_own + out_got.astype(F32)).astype(BF16)
    out = lax.all_to_all(out, ("x", "y"), 0, 0, tiled=True)

    moe = lax.dot_general(
        table, out.reshape(NXY * CAP, LANES), (((0,), (0,)), ((), ())), preferred_element_type=F32
    )[:, :CHUNK].reshape(NZ, ROWS, CHUNK)
    mask = (jnp.arange(NZ) == plane).astype(F32)
    total = (moe + mask[:, None, None] * hidden_wide[None]).astype(BF16)
    total = total.reshape(NZ * NDEV, rows_dev, CHUNK)
    total = lax.all_to_all(total, ("z", "x", "y", "c"), 0, 0, tiled=True)
    total = jnp.sum(total.reshape(NZ, NXY, NC, rows_dev, CHUNK).astype(F32), axis=0)
    return total.transpose(2, 1, 0, 3).reshape(rows_dev, D).astype(BF16)


def solution(mesh):
    grid = Mesh(mesh.devices.reshape(NZ, NX, NY, NC), ("z", "x", "y", "c"))
    dev = ("x", "y", "c")
    every = ("z", "x", "y", "c")
    return jax.shard_map(
        per_device,
        mesh=grid,
        in_specs=(
            P("z", dev, None),
            P("z", None),
            P(every, None, None),
            P(every, None),
            P(every, None, None),
            P(every, None),
            P(every, None),
            P(dev, None, None),
            P(dev, None),
            P(),
            P(),
            P(),
            P(every, None, None),
            P(every, None, None),
            P(every, None, None),
        ),
        out_specs=P(every, None),
        check_vma=False,
    )
```

```python
import functools

import jax
import jax.numpy as jnp
from jax import lax
from jax.experimental import pallas as pl
from jax.experimental.pallas import tpu as pltpu
from jax.sharding import Mesh, PartitionSpec as P

LAT = 512
ROPE = 64
NOPE = 128
D = 7168
CAP = 192
NZ, NX, NY, NC = 4, 4, 4, 2
NXY = NX * NY
NDEV = NXY * NC
EXP_G = 8
CHUNK = D // NDEV
LANES = 256
GROUP = 4
BLK = CHUNK * GROUP
STEPS = NXY // GROUP
ROWS = 128
ALL_ROWS = ROWS * NZ
F32 = jnp.float32
BF16 = jnp.bfloat16
SMALL = 16 * 1024 * 1024
LARGE = 20 * 1024 * 1024


def kept(shape, dtype):
    return pltpu.VMEM(shape, dtype)


def in_hbm(array):
    return pltpu.with_memory_space_constraint(array, pltpu.HBM)


def start_all(copies):
    for copy in copies:
        copy.start()
    return copies


WHOLE = pl.BlockSpec(memory_space=pltpu.VMEM)
SCALAR = pl.BlockSpec(memory_space=pltpu.SMEM)
ANYWHERE = pl.BlockSpec(memory_space=pl.ANY)


def attend(query_row, cache_block, valid_mask, own_entry):
    scale_factor = (NOPE + ROPE) ** (-0.5)
    scores = jnp.einsum("hc,kc->hk", query_row, cache_block, preferred_element_type=F32) * scale_factor
    if valid_mask is not None:
        scores = jnp.where(valid_mask[None, :], scores, -jnp.inf)
    own_score = jnp.einsum("hc,c->h", query_row, own_entry, preferred_element_type=F32) * scale_factor
    maximum = jnp.maximum(jnp.max(scores, axis=1), own_score)
    exponent = jnp.exp(scores - maximum[:, None])
    own_exponent = jnp.exp(own_score - maximum)
    totals = jnp.sum(exponent, axis=1) + own_exponent
    weights = (exponent / totals[:, None]).astype(BF16)
    own_weight = (own_exponent / totals).astype(BF16)
    context = jnp.einsum("hk,kl->hl", weights, cache_block[:, :LAT], preferred_element_type=F32)
    context = context + own_weight.astype(F32)[:, None] * own_entry[:LAT].astype(F32)[None, :]
    return context.astype(BF16)


def spread_kernel(owners_ref, cache_ref, out_ref, held_ref, in_sem, out_sem):
    arrive = [pltpu.make_async_copy(cache_ref.at[p], held_ref.at[p], in_sem.at[p]) for p in range(NDEV)]
    leave = [
        pltpu.make_async_copy(held_ref.at[p], out_ref.at[owners_ref[0, p]], out_sem.at[p]) for p in range(NDEV)
    ]
    start_all(arrive)
    for p in range(NDEV):
        arrive[p].wait()
        leave[p].start()
    for p in range(NDEV):
        leave[p].wait()


def spread(owners, cache):
    return pl.pallas_call(
        spread_kernel,
        in_specs=[SCALAR, ANYWHERE],
        out_specs=ANYWHERE,
        scratch_shapes=[
            pltpu.VMEM(cache.shape, cache.dtype),
            pltpu.SemaphoreType.DMA((NDEV,)),
            pltpu.SemaphoreType.DMA((NDEV,)),
        ],
        out_shape=pltpu.HBM(cache.shape, cache.dtype),
        compiler_params=pltpu.CompilerParams(vmem_limit_bytes=SMALL),
        name="spread",
    )(owners, in_hbm(cache))


def prompt_kernel(
    query_hbm, cache_ref, entry_ref, old_hbm, uv_hbm, w_hbm, out_ref, uv_ref, w_ref, all_ref, query_ref, sems
):
    heads_all = query_hbm.shape[1]
    query_copy = pltpu.make_async_copy(query_hbm, query_ref, sems.at[0])
    old_copy = pltpu.make_async_copy(old_hbm, all_ref.at[pl.ds(heads_all, old_hbm.shape[0]), :], sems.at[1])
    uv_copy = pltpu.make_async_copy(uv_hbm, uv_ref, sems.at[2])
    w_copy = pltpu.make_async_copy(w_hbm, w_ref, sems.at[3])
    start_all((query_copy, old_copy, uv_copy, w_copy))
    scale_factor = (NOPE + ROPE) ** (-0.5)
    cache = cache_ref[...].reshape(-1, cache_ref.shape[-1])
    entry = entry_ref[:1, :]
    query_copy.wait()
    query = query_ref[...]
    scores = jnp.dot(cache, query, preferred_element_type=F32) * scale_factor
    own_score = jnp.dot(entry, query, preferred_element_type=F32) * scale_factor
    maximum = jnp.maximum(jnp.max(scores, axis=0, keepdims=True), own_score)
    exponent = jnp.exp(scores - maximum)
    own_exponent = jnp.exp(own_score - maximum)
    totals = jnp.sum(exponent, axis=0, keepdims=True) + own_exponent
    weights = (exponent / totals).astype(BF16)
    own_weight = (own_exponent / totals).astype(BF16)
    over_rows = (((0,), (0,)), ((), ()))
    context = lax.dot_general(weights, cache[:, :LAT], over_rows, preferred_element_type=F32)
    context = context + lax.dot_general(own_weight, entry[:, :LAT], over_rows, preferred_element_type=F32)
    all_ref[:heads_all, :] = context.astype(BF16)
    rows, block = out_ref.shape[0], out_ref.shape[0] // NDEV
    heads = heads_all // NDEV
    to = lax.broadcasted_iota(jnp.int32, (rows, rows), 0)
    source = (to % block) // heads * heads_all + to // block * heads + to % heads
    order = (lax.broadcasted_iota(jnp.int32, (rows, rows), 1) == source).astype(BF16)
    old_copy.wait()
    out_ref[...] = jnp.dot(order, all_ref[...], preferred_element_type=F32).astype(BF16)
    uv_copy.wait()
    w_copy.wait()


def prompt_attention(query, cache, entry, old, w_uv, w_out):
    rows = query.shape[1] + old.shape[0]
    return pl.pallas_call(
        prompt_kernel,
        in_specs=[ANYWHERE, WHOLE, WHOLE, ANYWHERE, ANYWHERE, ANYWHERE],
        out_specs=[WHOLE, ANYWHERE, ANYWHERE],
        out_shape=[
            kept((rows, LAT), BF16), kept(w_uv.shape, BF16), kept(w_out.shape, BF16),
        ],
        scratch_shapes=[
            pltpu.VMEM((rows, LAT), BF16),
            pltpu.VMEM(query.shape, BF16),
            pltpu.SemaphoreType.DMA((4,)),
        ],
        compiler_params=pltpu.CompilerParams(vmem_limit_bytes=LARGE),
        name="prompt_attention",
    )(in_hbm(query), cache, entry, in_hbm(old), in_hbm(w_uv), in_hbm(w_out))


def project_half(half, attn, place_ref, res_ref, w_ref, out_ref):
    for i in range(STEPS):
        at = pl.ds(pl.multiple_of((half * STEPS + i) * BLK, 128), BLK)
        acc = jnp.dot(attn, w_ref[:, at], preferred_element_type=F32)
        acc = acc + jnp.dot(place_ref[...], res_ref[:, at], preferred_element_type=F32)
        for g in range(GROUP):
            part = acc[:, g * CHUNK : (g + 1) * CHUNK]
            out_ref[i * GROUP + g, :, :CHUNK] = part.astype(out_ref.dtype)
            out_ref[i * GROUP + g, :, CHUNK:] = jnp.zeros((ROWS, LANES - CHUNK), out_ref.dtype)


def project_first_kernel(half_ref, context_ref, uv_ref, place_ref, res_ref, w_ref, out_ref, attn_ref):
    heads, rows = uv_ref.shape[0], context_ref.shape[0]
    context = context_ref[...]
    pick = lax.broadcasted_iota(jnp.int32, (ROWS, rows), 1) // heads
    pick = (pick == lax.broadcasted_iota(jnp.int32, (ROWS, rows), 0)).astype(BF16)
    head = lax.broadcasted_iota(jnp.int32, (rows, uv_ref.shape[2]), 0) % heads
    for h in range(heads):
        values = jnp.dot(context, uv_ref[h], preferred_element_type=F32)
        values = jnp.where(head == h, values, 0.0).astype(BF16)
        values = jnp.dot(pick, values, preferred_element_type=F32).astype(BF16)
        attn_ref[:, h * values.shape[1] : (h + 1) * values.shape[1]] = values
    project_half(half_ref[0], attn_ref[...], place_ref, res_ref, w_ref, out_ref)


def project_second_kernel(half_ref, attn_ref, place_ref, res_ref, w_ref, out_ref):
    project_half(half_ref[0], attn_ref[...], place_ref, res_ref, w_ref, out_ref)


def project_call(kernel, name, out_shape, args, depth):
    return pl.pallas_call(
        kernel,
        in_specs=[SCALAR] + [WHOLE] * (len(args) - 1),
        out_specs=[WHOLE] * len(out_shape),
        out_shape=out_shape,
        compiler_params=pltpu.CompilerParams(vmem_limit_bytes=SMALL),
        cost_estimate=pl.CostEstimate(
            flops=2 * ROWS * depth * D // 2, bytes_accessed=depth * D + 2 * ROWS * D, transcendentals=0
        ),
        name=name,
    )(*args)


def project_first(half, context, w_uv, place, res, w_out):
    depth = w_out.shape[0]
    return project_call(
        project_first_kernel,
        "project_first",
        [kept((NXY, ROWS, LANES), BF16), kept((ROWS, depth), BF16)],
        (half, context, w_uv, place, res, w_out),
        depth,
    )


def project_second(half, attn, place, res, w_out):
    return project_call(
        project_second_kernel,
        "project_second",
        [kept((NXY, ROWS, LANES), F32)],
        (half, attn, place, res, w_out),
        w_out.shape[0],
    )[0]


def rows_kernel(rows_dev, part_ref, gain_ref, router_ref, ids_ref, packed_ref, hidden_ref):
    total = part_ref[0].astype(F32)
    for source in range(1, part_ref.shape[0]):
        total = total + part_ref[source].astype(F32)
    total = total.astype(BF16)
    to = lax.broadcasted_iota(jnp.int32, (ROWS, ROWS), 0)
    order = to % (ROWS // rows_dev) * rows_dev + to // (ROWS // rows_dev)
    order = (lax.broadcasted_iota(jnp.int32, (ROWS, ROWS), 1) == order).astype(BF16)
    hidden_ref[...] = jnp.dot(order, total, preferred_element_type=F32)
    hidden = total[:, :CHUNK].astype(F32)
    square = jnp.sum(hidden * hidden, axis=1, keepdims=True)
    scaled = (hidden * gain_ref[...]).astype(BF16)
    logits = jnp.dot(scaled, router_ref[...], preferred_element_type=F32)
    expert = lax.broadcasted_iota(jnp.int32, logits.shape, 1)
    lane = lax.broadcasted_iota(jnp.int32, (ROWS, LANES - CHUNK), 1)
    top = ids_ref.shape[1]
    spare = jnp.zeros((ROWS, LANES - CHUNK), F32)
    for k in range(top + 1):
        value = square
        if k < top:
            value = jnp.sum(jnp.where(expert == ids_ref[:, k : k + 1], logits, 0.0), axis=1, keepdims=True)
        high = value.astype(BF16).astype(F32)
        at_high, at_low = (k, top + k) if k < top else (2 * top, 2 * top + 1)
        spare = jnp.where(lane == at_high, high, jnp.where(lane == at_low, value - high, spare))
    packed_ref[:, :CHUNK] = scaled
    packed_ref[:, CHUNK:] = spare.astype(BF16)


def pack_rows(part, gain, router, ids, rows_dev):
    return pl.pallas_call(
        functools.partial(rows_kernel, rows_dev),
        out_shape=[kept((ROWS, LANES), BF16), kept((ROWS, LANES), F32)],
        compiler_params=pltpu.CompilerParams(vmem_limit_bytes=SMALL),
        name="pack_rows",
    )(part, gain, router, ids)


def slot_kernel(after_ref, ranks_ref, *refs):
    packed_refs, out_ref, rows_ref = refs[:NZ], refs[NZ], refs[NZ + 1]
    for k in range(NZ):
        rows_ref[k * ROWS : (k + 1) * ROWS, :] = packed_refs[k][...]
    slot = lax.broadcasted_iota(jnp.int32, (CAP, ALL_ROWS), 0)
    for e in range(EXP_G):
        table = (ranks_ref[e : e + 1, :] == slot).astype(BF16)
        slotted = jnp.dot(table, rows_ref[...], preferred_element_type=F32).astype(BF16)
        out_ref[2 * e] = slotted
        out_ref[2 * e + 1] = slotted


def slot_rows(after, ranks, packed):
    return pl.pallas_call(
        slot_kernel,
        in_specs=[ANYWHERE] + [WHOLE] * (1 + NZ),
        out_specs=WHOLE,
        out_shape=kept((NXY, CAP, LANES), BF16),
        scratch_shapes=[pltpu.VMEM((ALL_ROWS, LANES), BF16)],
        compiler_params=pltpu.CompilerParams(vmem_limit_bytes=SMALL),
        name="slot_rows",
    )(after, ranks, *packed)


def combine_kernel(plane_ref, out_ref, ranks_ref, hidden_ref, rows_ref, acc_ref):
    slot = lax.broadcasted_iota(jnp.int32, (ALL_ROWS, CAP), 1)
    acc = jnp.zeros((ALL_ROWS, LANES), F32)
    for e in range(EXP_G):
        table = (ranks_ref[:, e : e + 1] == slot).astype(BF16)
        acc = acc + jnp.dot(table, out_ref[2 * e], preferred_element_type=F32)
        acc = acc + jnp.dot(table, out_ref[2 * e + 1], preferred_element_type=F32)
    acc_ref[...] = acc
    span, count = rows_ref.shape[0], rows_ref.shape[1]
    own = ROWS // count
    for r in range(count):
        at = pl.multiple_of(r * span + plane_ref[0] * own, 8)
        acc_ref[pl.ds(at, own), :] += hidden_ref[r * own : (r + 1) * own, :]
    for r in range(count):
        rows_ref[:, r, :] = acc_ref[r * span : (r + 1) * span, :].astype(BF16)


def combine_rows(plane, out, ranks, hidden, count):
    vmem = pl.BlockSpec(memory_space=pltpu.VMEM)
    return pl.pallas_call(
        combine_kernel,
        in_specs=[pl.BlockSpec(memory_space=pltpu.SMEM), vmem, vmem, vmem],
        out_specs=vmem,
        out_shape=kept((ALL_ROWS // count, count, LANES), BF16),
        scratch_shapes=[pltpu.VMEM((ALL_ROWS, LANES), F32)],
        compiler_params=pltpu.CompilerParams(vmem_limit_bytes=SMALL),
        name="combine_rows",
    )(plane, out, ranks, hidden)


def fetch_kernel(after_ref, *refs):
    count = len(refs) // 2
    sems = refs[2 * count]
    copies = [pltpu.make_async_copy(refs[i], refs[count + i], sems.at[i]) for i in range(count)]
    for copy in start_all(copies):
        copy.wait()


def fetch(after, arrays):
    return pl.pallas_call(
        fetch_kernel,
        in_specs=[ANYWHERE] * (1 + len(arrays)),
        out_specs=[ANYWHERE] * len(arrays),
        scratch_shapes=[pltpu.SemaphoreType.DMA((len(arrays),))],
        out_shape=[kept(a.shape, a.dtype) for a in arrays],
        compiler_params=pltpu.CompilerParams(vmem_limit_bytes=SMALL),
        cost_estimate=pl.CostEstimate(
            flops=0, bytes_accessed=4 * sum(a.size for a in arrays), transcendentals=0
        ),
        name="fetch",
    )(after, *[in_hbm(a) for a in arrays])


def gate_up_half(half, y_ref, wg_ref, wu_ref, gate_ref, up_ref, stats_ref):
    gate, up, stats = gate_ref[...], up_ref[...], stats_ref[...]
    for p in range(NXY):
        rows = y_ref[p, :, :CHUNK]
        at = pl.ds(pl.multiple_of((half * NXY + p) * CHUNK, 16), CHUNK)
        gate = gate + jnp.dot(rows, wg_ref[0, at, :], preferred_element_type=F32)
        up = up + jnp.dot(rows, wu_ref[0, at, :], preferred_element_type=F32)
        stats = stats + y_ref[p, :, CHUNK:].astype(F32)
    gate_ref[...] = gate
    up_ref[...] = up
    stats_ref[...] = stats


def first_kernel(half_ref, y_ref, wg_ref, wu_ref, gate_ref, up_ref, stats_ref):
    gate_ref[...] = jnp.zeros_like(gate_ref)
    up_ref[...] = jnp.zeros_like(up_ref)
    stats_ref[...] = jnp.zeros_like(stats_ref)
    gate_up_half(half_ref[0], y_ref, wg_ref, wu_ref, gate_ref, up_ref, stats_ref)


def first_half(half, y, w_gate, w_up):
    hidden = w_gate.shape[2]
    return pl.pallas_call(
        first_kernel,
        in_specs=[SCALAR, WHOLE, WHOLE, WHOLE],
        out_specs=[WHOLE] * 3,
        out_shape=[
            kept((CAP, hidden), F32),
            kept((CAP, hidden), F32),
            kept((CAP, LANES - CHUNK), F32),
        ],
        compiler_params=pltpu.CompilerParams(vmem_limit_bytes=SMALL),
        cost_estimate=pl.CostEstimate(
            flops=2 * CAP * D * hidden, bytes_accessed=2 * D * hidden + CAP * D, transcendentals=0
        ),
        name="gate_up_first",
    )(half, y, w_gate, w_up)


def down_step(half, act, gates, wd_ref, out_ref):
    for i in range(STEPS):
        at = pl.ds(pl.multiple_of((half * STEPS + i) * BLK, 128), BLK)
        acc = jnp.dot(act, wd_ref[0, :, at], preferred_element_type=F32) * gates
        for g in range(GROUP):
            out_ref[i * GROUP + g, :, :CHUNK] = acc[:, g * CHUNK : (g + 1) * CHUNK].astype(out_ref.dtype)
            out_ref[i * GROUP + g, :, CHUNK:] = jnp.zeros((CAP, LANES - CHUNK), out_ref.dtype)


def second_kernel(
    half_ref, y_ref, wg_ref, wu_ref, wd_ref, gate0_ref, up0_ref, stats0_ref, mine_ref,
    act_ref, gates_ref, out_ref, gate_acc, up_acc, stats_acc,
):
    gate_acc[...] = gate0_ref[...]
    up_acc[...] = up0_ref[...]
    stats_acc[...] = stats0_ref[...]
    gate_up_half(half_ref[0], y_ref, wg_ref, wu_ref, gate_acc, up_acc, stats_acc)
    stats = stats_acc[...]
    square = stats[:, 16:17] + stats[:, 17:18]
    scale = lax.rsqrt(square * (1.0 / D) + 1e-6)
    affinity = jax.nn.sigmoid((stats[:, 0:8] + stats[:, 8:16]) * scale)
    own = jnp.sum(affinity * mine_ref[...], axis=1, keepdims=True)
    gates = 2.5 * own / jnp.sum(affinity, axis=1, keepdims=True)
    gates_ref[...] = jnp.broadcast_to(gates.astype(BF16).astype(F32), gates_ref.shape)
    gate = gate_acc[...] * scale
    up = up_acc[...] * scale
    act_ref[...] = (gate * jax.nn.sigmoid(gate) * up).astype(BF16)
    down_step(half_ref[0], act_ref[...], gates_ref[:, :1], wd_ref, out_ref)


def second_half(half, y, w_gate, w_up, w_down, gate, up, stats, mine):
    hidden = w_gate.shape[2]
    return pl.pallas_call(
        second_kernel,
        in_specs=[SCALAR] + [WHOLE] * 8,
        out_specs=[WHOLE] * 3,
        out_shape=[kept((CAP, hidden), BF16), kept((CAP, 128), F32), kept((NXY, CAP, LANES), BF16)],
        scratch_shapes=[
            pltpu.VMEM((CAP, hidden), F32),
            pltpu.VMEM((CAP, hidden), F32),
            pltpu.VMEM((CAP, LANES - CHUNK), F32),
        ],
        compiler_params=pltpu.CompilerParams(vmem_limit_bytes=SMALL),
        cost_estimate=pl.CostEstimate(
            flops=3 * CAP * D * hidden, bytes_accessed=3 * D * hidden + 2 * CAP * D, transcendentals=0
        ),
        name="gate_up_second",
    )(half, y, w_gate, w_up, w_down, gate, up, stats, mine)


def down_kernel(half_ref, act_ref, gates_ref, wd_ref, out_ref):
    down_step(half_ref[0], act_ref[...], gates_ref[:, :1], wd_ref, out_ref)


def down_own(half, act, gates, w_down):
    hidden = act.shape[1]
    return pl.pallas_call(
        down_kernel,
        in_specs=[SCALAR] + [WHOLE] * 3,
        out_specs=WHOLE,
        out_shape=kept((NXY, CAP, LANES), F32),
        compiler_params=pltpu.CompilerParams(vmem_limit_bytes=SMALL),
        cost_estimate=pl.CostEstimate(
            flops=CAP * D * hidden, bytes_accessed=D * hidden + 2 * CAP * D, transcendentals=0
        ),
        name="down_own",
    )(half, act, gates, w_down)


def swap_cores(values):
    return lax.ppermute(values, "c", [(0, 1), (1, 0)])


def per_device(
    prompt_cache,
    assignment,
    resident_cache,
    resident_len,
    queries,
    new_latent,
    residual,
    w_uv,
    w_out,
    norm_gain,
    w_router,
    expert_ids,
    w_gate,
    w_up,
    w_down,
):
    plane = lax.axis_index("z")
    core = lax.axis_index("c")
    place_xy = lax.axis_index("x") * NY + lax.axis_index("y")
    dev_index = place_xy * NC + core
    rows_dev = queries.shape[0]
    own_half = jnp.reshape(core, (1,)).astype(jnp.int32)
    other_half = 1 - own_half
    plane_index = jnp.reshape(plane, (1,)).astype(jnp.int32)
    chunk = core * NXY + place_xy

    received = lax.all_to_all(spread(assignment, prompt_cache), ("x", "y", "c"), 0, 0, tiled=True)

    ids_plane = expert_ids - plane * EXP_G
    named = jnp.any(expert_ids[:, :, None] == jnp.arange(NZ * EXP_G, dtype=jnp.int32)[None, None, :], axis=1)
    lower = (jnp.arange(ALL_ROWS)[:, None] > jnp.arange(ALL_ROWS)[None, :]).astype(BF16)
    ranks = jnp.dot(lower, named.astype(BF16), preferred_element_type=F32).astype(jnp.int32)
    ranks = jnp.where(named, ranks, -1)
    plane_ranks = lax.dynamic_slice_in_dim(ranks, plane * EXP_G, EXP_G, 1)
    own_expert = place_xy // 2
    slot_iota = jnp.arange(CAP, dtype=jnp.int32)
    own_ranks = lax.dynamic_index_in_dim(plane_ranks, own_expert, 1, keepdims=False)
    own_slots = (own_ranks[None, :] == slot_iota[:, None]).astype(BF16)
    slot_ids = jnp.dot(own_slots, ids_plane.astype(BF16), preferred_element_type=F32)
    mine = (slot_ids == own_expert.astype(F32)).astype(F32)
    group_ids = lax.dynamic_slice_in_dim(expert_ids, plane * ROWS, ROWS, 0)
    by_group = plane_ranks.reshape(NZ, ROWS, EXP_G)
    step_order = (plane - jnp.arange(NZ, dtype=jnp.int32)) % NZ
    step_ranks = by_group.at[step_order].get(mode="promise_in_bounds").reshape(ALL_ROWS, EXP_G).T
    owner_ranks = plane_ranks.reshape(NZ * NDEV, rows_dev, EXP_G).transpose(1, 0, 2).reshape(ALL_ROWS, EXP_G)
    gain_chunk = lax.dynamic_slice_in_dim(norm_gain, chunk * CHUNK, CHUNK, 0).astype(F32)[None, :]
    router_chunk = lax.dynamic_slice_in_dim(w_router, chunk * CHUNK, CHUNK, 0)
    row_iota = jnp.arange(ROWS, dtype=jnp.int32)
    place = (row_iota[:, None] == dev_index * rows_dev + jnp.arange(16, dtype=jnp.int32)[None, :]) & (
        jnp.arange(16) < rows_dev
    )[None, :]
    place = place.astype(BF16)
    res = jnp.pad(residual, ((0, 16 - rows_dev), (0, 0)))

    cache_iota = jnp.arange(resident_cache.shape[1], dtype=jnp.int32)
    old_masks = cache_iota[None, :] < resident_len[0][:, None]
    context_old = jax.vmap(attend)(queries[1:], resident_cache, old_masks, new_latent[1:])
    context_old = context_old.reshape(-1, LAT)
    held = (
        received, context_old, queries[0].T, step_ranks, owner_ranks, mine, group_ids, gain_chunk,
        router_chunk, place, res, own_half, other_half, plane_index,
    )
    (
        received, context_old, first_query, step_ranks, owner_ranks, mine, group_ids, gain_chunk,
        router_chunk, place, res, own_half, other_half, plane_index,
    ) = lax.optimization_barrier(held)
    context, w_uv, w_out = prompt_attention(first_query, received, new_latent, context_old, w_uv, w_out)

    context = lax.all_to_all(context.reshape(NDEV, -1, LAT), ("x", "y", "c"), 0, 0, tiled=True)
    context = context.reshape(-1, LAT)

    partial_other, attn = project_first(other_half, context, w_uv, place, res, w_out)
    partial_got = swap_cores(partial_other)
    partial_own = project_second(own_half, attn, place, res, w_out)
    partial = (partial_own + partial_got.astype(F32)).astype(BF16)
    partial = lax.all_to_all(partial, ("x", "y"), 0, 0, tiled=True)

    packed, hidden = pack_rows(partial, gain_chunk, router_chunk, group_ids, rows_dev)

    groups = [packed]
    for k in range(1, NZ):
        groups.append(lax.ppermute(packed, "z", [(i, (i + k) % NZ) for i in range(NZ)]))
    w_gate, w_up, w_down = fetch(packed, (w_gate, w_up, w_down))
    slotted = slot_rows(w_down, step_ranks, groups)
    slotted = lax.all_to_all(slotted, ("x", "y"), 0, 0, tiled=True)

    slotted_other = swap_cores(slotted)
    gate, up, stats = first_half(own_half, slotted, w_gate, w_up)
    act, gates, out_other = second_half(
        other_half, slotted_other, w_gate, w_up, w_down, gate, up, stats, mine
    )
    out_got = swap_cores(out_other)
    out_own = down_own(own_half, act, gates, w_down)
    out = (out_own + out_got.astype(F32)).astype(BF16)
    out = lax.all_to_all(out, ("x", "y"), 0, 0, tiled=True)

    total = combine_rows(plane_index, out, owner_ranks, hidden, rows_dev)
    total = lax.all_to_all(total, ("z", "x", "y", "c"), 0, 0, tiled=True)
    total = jnp.sum(total.reshape(NZ, NXY, NC, rows_dev, LANES)[..., :CHUNK].astype(F32), axis=0)
    return total.transpose(2, 1, 0, 3).reshape(rows_dev, D).astype(BF16)


def solution(mesh):
    grid = Mesh(mesh.devices.reshape(NZ, NX, NY, NC), ("z", "x", "y", "c"))
    dev = ("x", "y", "c")
    every = ("z", "x", "y", "c")
    return jax.shard_map(
        per_device,
        mesh=grid,
        in_specs=(
            P("z", dev, None),
            P("z", None),
            P(every, None, None),
            P(every, None),
            P(every, None, None),
            P(every, None),
            P(every, None),
            P(dev, None, None),
            P(dev, None),
            P(),
            P(),
            P(),
            P(every, None, None),
            P(every, None, None),
            P(every, None, None),
        ),
        out_specs=P(every, None),
        check_vma=False,
    )
```

```python
import functools

import jax
import jax.numpy as jnp
from jax import lax
from jax.experimental import pallas as pl
from jax.experimental.pallas import tpu as pltpu
from jax.sharding import Mesh, PartitionSpec as P

LAT = 512
ROPE = 64
NOPE = 128
D = 7168
CAP = 192
NZ, NX, NY, NC = 4, 4, 4, 2
NXY = NX * NY
NDEV = NXY * NC
EXP_G = 8
CHUNK = D // NDEV
HALF = D // 2
LANES = 256
GROUP = 4
BLK = CHUNK * GROUP
STEPS = NXY // GROUP
ROWS = 128
ALL_ROWS = ROWS * NZ
F32 = jnp.float32
BF16 = jnp.bfloat16
SMALL = 16 * 1024 * 1024
LARGE = 20 * 1024 * 1024


def kept(shape, dtype):
    return pltpu.VMEM(shape, dtype)


def in_hbm(array):
    return pltpu.with_memory_space_constraint(array, pltpu.HBM)


def start_all(copies):
    for copy in copies:
        copy.start()
    return copies


WHOLE = pl.BlockSpec(memory_space=pltpu.VMEM)
SCALAR = pl.BlockSpec(memory_space=pltpu.SMEM)
ANYWHERE = pl.BlockSpec(memory_space=pl.ANY)


def attend(query_row, cache_block, valid_mask, own_entry):
    scale_factor = (NOPE + ROPE) ** (-0.5)
    scores = jnp.einsum("hc,kc->hk", query_row, cache_block, preferred_element_type=F32) * scale_factor
    if valid_mask is not None:
        scores = jnp.where(valid_mask[None, :], scores, -jnp.inf)
    own_score = jnp.einsum("hc,c->h", query_row, own_entry, preferred_element_type=F32) * scale_factor
    maximum = jnp.maximum(jnp.max(scores, axis=1), own_score)
    exponent = jnp.exp(scores - maximum[:, None])
    own_exponent = jnp.exp(own_score - maximum)
    totals = jnp.sum(exponent, axis=1) + own_exponent
    weights = (exponent / totals[:, None]).astype(BF16)
    own_weight = (own_exponent / totals).astype(BF16)
    context = jnp.einsum("hk,kl->hl", weights, cache_block[:, :LAT], preferred_element_type=F32)
    context = context + own_weight.astype(F32)[:, None] * own_entry[:LAT].astype(F32)[None, :]
    return context.astype(BF16)


def spread_kernel(owners_ref, cache_ref, out_ref, held_ref, in_sem, out_sem):
    arrive = [pltpu.make_async_copy(cache_ref.at[p], held_ref.at[p], in_sem.at[p]) for p in range(NDEV)]
    leave = [
        pltpu.make_async_copy(held_ref.at[p], out_ref.at[owners_ref[0, p]], out_sem.at[p]) for p in range(NDEV)
    ]
    start_all(arrive)
    for p in range(NDEV):
        arrive[p].wait()
        leave[p].start()
    for p in range(NDEV):
        leave[p].wait()


def spread(owners, cache):
    return pl.pallas_call(
        spread_kernel,
        in_specs=[SCALAR, ANYWHERE],
        out_specs=ANYWHERE,
        scratch_shapes=[
            pltpu.VMEM(cache.shape, cache.dtype),
            pltpu.SemaphoreType.DMA((NDEV,)),
            pltpu.SemaphoreType.DMA((NDEV,)),
        ],
        out_shape=pltpu.HBM(cache.shape, cache.dtype),
        compiler_params=pltpu.CompilerParams(vmem_limit_bytes=SMALL),
        name="spread",
    )(owners, in_hbm(cache))


def prompt_kernel(
    half_ref, query_hbm, cache_ref, entry_ref, old_hbm, uv_hbm, w_hbm, res_hbm, got_hbm,
    out_ref, uv_ref, w_ref, all_ref, query_ref, sems,
):
    heads_all = query_hbm.shape[1]
    query_copy = pltpu.make_async_copy(query_hbm, query_ref, sems.at[0])
    old_copy = pltpu.make_async_copy(old_hbm, all_ref.at[pl.ds(heads_all, old_hbm.shape[0]), :], sems.at[1])
    uv_copy = pltpu.make_async_copy(uv_hbm, uv_ref, sems.at[2])
    depth = w_hbm.shape[0]
    at = pl.ds(pl.multiple_of(half_ref[0] * HALF, 128), HALF)
    w_copies = (
        pltpu.make_async_copy(w_hbm.at[:, at], w_ref.at[pl.ds(0, depth), :], sems.at[3]),
        pltpu.make_async_copy(res_hbm.at[:, at], w_ref.at[pl.ds(depth, 16), :], sems.at[4]),
        pltpu.make_async_copy(got_hbm, w_ref.at[pl.ds(depth + 16, depth + 16), :], sems.at[5]),
    )
    start_all((query_copy, old_copy, uv_copy) + w_copies)
    scale_factor = (NOPE + ROPE) ** (-0.5)
    cache = cache_ref[...].reshape(-1, cache_ref.shape[-1])
    entry = entry_ref[:1, :]
    query_copy.wait()
    query = query_ref[...]
    scores = jnp.dot(cache, query, preferred_element_type=F32) * scale_factor
    own_score = jnp.dot(entry, query, preferred_element_type=F32) * scale_factor
    maximum = jnp.maximum(jnp.max(scores, axis=0, keepdims=True), own_score)
    exponent = jnp.exp(scores - maximum)
    own_exponent = jnp.exp(own_score - maximum)
    totals = jnp.sum(exponent, axis=0, keepdims=True) + own_exponent
    weights = (exponent / totals).astype(BF16)
    own_weight = (own_exponent / totals).astype(BF16)
    over_rows = (((0,), (0,)), ((), ()))
    context = lax.dot_general(weights, cache[:, :LAT], over_rows, preferred_element_type=F32)
    context = context + lax.dot_general(own_weight, entry[:, :LAT], over_rows, preferred_element_type=F32)
    all_ref[:heads_all, :] = context.astype(BF16)
    rows, block = out_ref.shape[0], out_ref.shape[0] // NDEV
    heads = heads_all // NDEV
    to = lax.broadcasted_iota(jnp.int32, (rows, rows), 0)
    source = (to % block) // heads * heads_all + to // block * heads + to % heads
    order = (lax.broadcasted_iota(jnp.int32, (rows, rows), 1) == source).astype(BF16)
    old_copy.wait()
    out_ref[...] = jnp.dot(order, all_ref[...], preferred_element_type=F32).astype(BF16)
    uv_copy.wait()
    for copy in w_copies:
        copy.wait()


def prompt_attention(half, query, cache, entry, old, w_uv, w_out, res, got):
    rows = query.shape[1] + old.shape[0]
    return pl.pallas_call(
        prompt_kernel,
        in_specs=[SCALAR, ANYWHERE, WHOLE, WHOLE] + [ANYWHERE] * 5,
        out_specs=[WHOLE, ANYWHERE, ANYWHERE],
        out_shape=[
            kept((rows, LAT), BF16), kept(w_uv.shape, BF16), kept((2 * got.shape[0], HALF), BF16),
        ],
        scratch_shapes=[
            pltpu.VMEM((rows, LAT), BF16),
            pltpu.VMEM(query.shape, BF16),
            pltpu.SemaphoreType.DMA((6,)),
        ],
        compiler_params=pltpu.CompilerParams(vmem_limit_bytes=LARGE),
        name="prompt_attention",
    )(half, in_hbm(query), cache, entry, *[in_hbm(a) for a in (old, w_uv, w_out, res, got)])


def values_kernel(context_ref, uv_ref, attn_ref):
    heads, rows = uv_ref.shape[0], context_ref.shape[0]
    context = context_ref[...]
    pick = lax.broadcasted_iota(jnp.int32, (ROWS, rows), 1) // heads
    pick = (pick == lax.broadcasted_iota(jnp.int32, (ROWS, rows), 0)).astype(BF16)
    head = lax.broadcasted_iota(jnp.int32, (rows, uv_ref.shape[2]), 0) % heads
    for h in range(heads):
        values = jnp.dot(context, uv_ref[h], preferred_element_type=F32)
        values = jnp.where(head == h, values, 0.0).astype(BF16)
        values = jnp.dot(pick, values, preferred_element_type=F32).astype(BF16)
        attn_ref[:, h * values.shape[1] : (h + 1) * values.shape[1]] = values


def head_values(context, w_uv):
    return pl.pallas_call(
        values_kernel,
        in_specs=[WHOLE, WHOLE],
        out_specs=WHOLE,
        out_shape=kept((ROWS, w_uv.shape[0] * w_uv.shape[2]), BF16),
        compiler_params=pltpu.CompilerParams(vmem_limit_bytes=SMALL),
        name="head_values",
    )(context, w_uv)


def project_kernel(own_ref, got_ref, place_ref, w_ref, out_ref):
    depth = own_ref.shape[1]
    lhs = (own_ref[...], place_ref[0], got_ref[...], place_ref[1])
    for i in range(STEPS):
        at, acc = 0, jnp.zeros((ROWS, BLK), F32)
        for left in lhs:
            acc = acc + jnp.dot(
                left, w_ref[at : at + left.shape[1], i * BLK : (i + 1) * BLK], preferred_element_type=F32
            )
            at += left.shape[1]
        for g in range(GROUP):
            out_ref[i * GROUP + g, :, :CHUNK] = acc[:, g * CHUNK : (g + 1) * CHUNK].astype(BF16)
            out_ref[i * GROUP + g, :, CHUNK:] = jnp.zeros((ROWS, LANES - CHUNK), BF16)


def project(own, got, place, w_out):
    return pl.pallas_call(
        project_kernel,
        in_specs=[WHOLE] * 4,
        out_specs=WHOLE,
        out_shape=kept((NXY, ROWS, LANES), BF16),
        compiler_params=pltpu.CompilerParams(vmem_limit_bytes=SMALL),
        name="project",
    )(own, got, place, w_out)


def rows_kernel(rows_dev, part_ref, gain_ref, router_ref, ids_ref, packed_ref, hidden_ref):
    total = part_ref[0].astype(F32)
    for source in range(1, part_ref.shape[0]):
        total = total + part_ref[source].astype(F32)
    total = total.astype(BF16)
    to = lax.broadcasted_iota(jnp.int32, (ROWS, ROWS), 0)
    order = to % (ROWS // rows_dev) * rows_dev + to // (ROWS // rows_dev)
    order = (lax.broadcasted_iota(jnp.int32, (ROWS, ROWS), 1) == order).astype(BF16)
    hidden_ref[...] = jnp.dot(order, total, preferred_element_type=F32)
    hidden = total[:, :CHUNK].astype(F32)
    square = jnp.sum(hidden * hidden, axis=1, keepdims=True)
    scaled = (hidden * gain_ref[...]).astype(BF16)
    logits = jnp.dot(scaled, router_ref[...], preferred_element_type=F32)
    expert = lax.broadcasted_iota(jnp.int32, logits.shape, 1)
    lane = lax.broadcasted_iota(jnp.int32, (ROWS, LANES - CHUNK), 1)
    top = ids_ref.shape[1]
    spare = jnp.zeros((ROWS, LANES - CHUNK), F32)
    for k in range(top + 1):
        value = square
        if k < top:
            value = jnp.sum(jnp.where(expert == ids_ref[:, k : k + 1], logits, 0.0), axis=1, keepdims=True)
        high = value.astype(BF16).astype(F32)
        at_high, at_low = (k, top + k) if k < top else (2 * top, 2 * top + 1)
        spare = jnp.where(lane == at_high, high, jnp.where(lane == at_low, value - high, spare))
    packed_ref[:, :CHUNK] = scaled
    packed_ref[:, CHUNK:] = spare.astype(BF16)


def pack_rows(part, gain, router, ids, rows_dev):
    return pl.pallas_call(
        functools.partial(rows_kernel, rows_dev),
        out_shape=[kept((ROWS, LANES), BF16), kept((ROWS, LANES), F32)],
        compiler_params=pltpu.CompilerParams(vmem_limit_bytes=SMALL),
        name="pack_rows",
    )(part, gain, router, ids)


def slot_kernel(after_ref, ranks_ref, *refs):
    packed_refs, out_ref, rows_ref = refs[:NZ], refs[NZ], refs[NZ + 1]
    for k in range(NZ):
        rows_ref[k * ROWS : (k + 1) * ROWS, :] = packed_refs[k][...]
    slot = lax.broadcasted_iota(jnp.int32, (CAP, ALL_ROWS), 0)
    for e in range(EXP_G):
        table = (ranks_ref[e : e + 1, :] == slot).astype(BF16)
        slotted = jnp.dot(table, rows_ref[...], preferred_element_type=F32).astype(BF16)
        out_ref[2 * e] = slotted
        out_ref[2 * e + 1] = slotted


def slot_rows(after, ranks, packed):
    return pl.pallas_call(
        slot_kernel,
        in_specs=[ANYWHERE] + [WHOLE] * (1 + NZ),
        out_specs=WHOLE,
        out_shape=kept((NXY, CAP, LANES), BF16),
        scratch_shapes=[pltpu.VMEM((ALL_ROWS, LANES), BF16)],
        compiler_params=pltpu.CompilerParams(vmem_limit_bytes=SMALL),
        name="slot_rows",
    )(after, ranks, *packed)


def combine_kernel(plane_ref, out_ref, ranks_ref, hidden_ref, rows_ref, acc_ref):
    slot = lax.broadcasted_iota(jnp.int32, (ALL_ROWS, CAP), 1)
    acc = jnp.zeros((ALL_ROWS, LANES), F32)
    for e in range(EXP_G):
        table = (ranks_ref[:, e : e + 1] == slot).astype(BF16)
        acc = acc + jnp.dot(table, out_ref[2 * e], preferred_element_type=F32)
        acc = acc + jnp.dot(table, out_ref[2 * e + 1], preferred_element_type=F32)
    acc_ref[...] = acc
    span, count = rows_ref.shape[0], rows_ref.shape[1]
    own = ROWS // count
    for r in range(count):
        at = pl.multiple_of(r * span + plane_ref[0] * own, 8)
        acc_ref[pl.ds(at, own), :] += hidden_ref[r * own : (r + 1) * own, :]
    for r in range(count):
        rows_ref[:, r, :] = acc_ref[r * span : (r + 1) * span, :].astype(BF16)


def combine_rows(plane, out, ranks, hidden, count):
    vmem = pl.BlockSpec(memory_space=pltpu.VMEM)
    return pl.pallas_call(
        combine_kernel,
        in_specs=[pl.BlockSpec(memory_space=pltpu.SMEM), vmem, vmem, vmem],
        out_specs=vmem,
        out_shape=kept((ALL_ROWS // count, count, LANES), BF16),
        scratch_shapes=[pltpu.VMEM((ALL_ROWS, LANES), F32)],
        compiler_params=pltpu.CompilerParams(vmem_limit_bytes=SMALL),
        name="combine_rows",
    )(plane, out, ranks, hidden)


def give_kernel(
    half_ref, out_hbm, res_hbm, gate_hbm, up_hbm, down_hbm, to_out, to_in, to_down,
    out_ref, in_ref, down_ref, in_sems, out_sems,
):
    depth = out_hbm.shape[0]
    columns = pl.ds(pl.multiple_of(half_ref[0] * HALF, 128), HALF)
    rows = pl.ds(pl.multiple_of(half_ref[0] * HALF, 16), HALF)
    sources = (
        (out_hbm.at[:, columns], out_ref.at[pl.ds(0, depth), :], to_out.at[pl.ds(0, depth), :]),
        (res_hbm.at[:, columns], out_ref.at[pl.ds(depth, 16), :], to_out.at[pl.ds(depth, 16), :]),
        (gate_hbm.at[0, rows, :], in_ref.at[0], to_in.at[0]),
        (up_hbm.at[0, rows, :], in_ref.at[1], to_in.at[1]),
        (down_hbm.at[0, :, columns], down_ref, to_down),
    )
    arrive = [pltpu.make_async_copy(a, b, in_sems.at[n]) for n, (a, b, _) in enumerate(sources)]
    leave = [pltpu.make_async_copy(b, c, out_sems.at[n]) for n, (_, b, c) in enumerate(sources)]
    start_all(arrive)
    for first, second in zip(arrive, leave):
        first.wait()
        second.start()
    for copy in leave:
        copy.wait()


def give_weights(half, w_out, res, w_gate, w_up, w_down):
    hidden = w_gate.shape[2]
    arrays = (w_out, res, w_gate, w_up, w_down)
    return pl.pallas_call(
        give_kernel,
        in_specs=[SCALAR] + [ANYWHERE] * 5,
        out_specs=[ANYWHERE] * 3,
        out_shape=[
            pltpu.HBM((w_out.shape[0] + 16, HALF), BF16),
            pltpu.HBM((2, HALF, hidden), BF16),
            pltpu.HBM((hidden, HALF), BF16),
        ],
        scratch_shapes=[
            pltpu.VMEM((w_out.shape[0] + 16, HALF), BF16),
            pltpu.VMEM((2, HALF, hidden), BF16),
            pltpu.VMEM((hidden, HALF), BF16),
            pltpu.SemaphoreType.DMA((5,)),
            pltpu.SemaphoreType.DMA((5,)),
        ],
        compiler_params=pltpu.CompilerParams(vmem_limit_bytes=SMALL),
        name="give_weights",
    )(half, *[in_hbm(a) for a in arrays])


def fetch_kernel(
    after_ref, half_ref, gate_hbm, up_hbm, down_hbm, got_in_hbm, got_down_hbm, in_ref, down_ref, sems
):
    hidden = gate_hbm.shape[2]
    columns = pl.ds(pl.multiple_of(half_ref[0] * HALF, 128), HALF)
    rows = pl.ds(pl.multiple_of(half_ref[0] * HALF, 16), HALF)
    sources = (gate_hbm.at[0, rows, :], up_hbm.at[0, rows, :], got_in_hbm.at[0], got_in_hbm.at[1])
    copies = [
        pltpu.make_async_copy(source, in_ref.at[:, pl.ds(j * hidden, hidden)], sems.at[j])
        for j, source in enumerate(sources)
    ]
    copies.append(
        pltpu.make_async_copy(down_hbm.at[0, :, columns], down_ref.at[pl.ds(0, hidden), :], sems.at[4])
    )
    copies.append(pltpu.make_async_copy(got_down_hbm, down_ref.at[pl.ds(hidden, hidden), :], sems.at[5]))
    for copy in start_all(copies):
        copy.wait()


def fetch_experts(after, half, w_gate, w_up, w_down, got_in, got_down):
    hidden = w_gate.shape[2]
    return pl.pallas_call(
        fetch_kernel,
        in_specs=[ANYWHERE, SCALAR] + [ANYWHERE] * 5,
        out_specs=[ANYWHERE] * 2,
        out_shape=[kept((HALF, 4 * hidden), BF16), kept((2 * hidden, HALF), BF16)],
        scratch_shapes=[pltpu.SemaphoreType.DMA((6,))],
        compiler_params=pltpu.CompilerParams(vmem_limit_bytes=SMALL),
        cost_estimate=pl.CostEstimate(flops=0, bytes_accessed=12 * D * hidden, transcendentals=0),
        name="fetch_experts",
    )(after, half, *[in_hbm(a) for a in (w_gate, w_up, w_down, got_in, got_down)])


def gate_up_kernel(y_ref, w_ref, own_ref, send_ref):
    width = w_ref.shape[1]
    acc = jnp.zeros((CAP, width), F32)
    stats = jnp.zeros((CAP, LANES - CHUNK), F32)
    for p in range(NXY):
        acc = acc + jnp.dot(
            y_ref[p, :, :CHUNK], w_ref[p * CHUNK : (p + 1) * CHUNK, :], preferred_element_type=F32
        )
        stats = stats + y_ref[p, :, CHUNK:].astype(F32)
    own_ref[:, :width] = acc
    send_ref[:, :width] = acc.astype(BF16)
    high = stats.astype(BF16).astype(F32)
    spare = jnp.zeros((CAP, 128 - 2 * stats.shape[1]), F32)
    own_ref[:, width:] = jnp.concatenate([stats, jnp.zeros_like(stats), spare], axis=1)
    send_ref[:, width:] = jnp.concatenate([high, stats - high, spare], axis=1).astype(BF16)


def gate_up(y, w):
    width = w.shape[1] + 128
    return pl.pallas_call(
        gate_up_kernel,
        in_specs=[WHOLE] * 2,
        out_specs=[WHOLE] * 2,
        out_shape=[kept((CAP, width), F32), kept((CAP, width), BF16)],
        compiler_params=pltpu.CompilerParams(vmem_limit_bytes=SMALL),
        name="gate_up",
    )(y, w)


def down_kernel(own_ref, got_ref, mine_ref, w_ref, out_ref):
    slices = w_ref.shape[0]
    hidden = slices // 2
    width = 2 * slices
    lanes = LANES - CHUNK
    stats = own_ref[:, width : width + lanes]
    stats = stats + got_ref[:, width : width + lanes].astype(F32)
    stats = stats + got_ref[:, width + lanes : width + 2 * lanes].astype(F32)
    square = stats[:, 16:17] + stats[:, 17:18]
    scale = lax.rsqrt(square * (1.0 / D) + 1e-6)
    affinity = jax.nn.sigmoid((stats[:, 0:8] + stats[:, 8:16]) * scale)
    own = jnp.sum(affinity * mine_ref[...], axis=1, keepdims=True)
    gates = 2.5 * own / jnp.sum(affinity, axis=1, keepdims=True)
    gates = gates.astype(BF16).astype(F32)
    acts = []
    for j in range(2):
        here, there = j * slices, (1 - j) * slices
        both = own_ref[:, here : here + slices] + got_ref[:, there : there + slices].astype(F32)
        gate = both[:, :hidden] * scale
        acts.append((gate * jax.nn.sigmoid(gate) * (both[:, hidden:] * scale)).astype(BF16))
    act = jnp.concatenate(acts, axis=1)
    for i in range(STEPS):
        acc = jnp.dot(act, w_ref[:, i * BLK : (i + 1) * BLK], preferred_element_type=F32) * gates
        for g in range(GROUP):
            out_ref[i * GROUP + g, :, :CHUNK] = acc[:, g * CHUNK : (g + 1) * CHUNK].astype(BF16)
            out_ref[i * GROUP + g, :, CHUNK:] = jnp.zeros((CAP, LANES - CHUNK), BF16)


def down(own, got, mine, w):
    return pl.pallas_call(
        down_kernel,
        in_specs=[WHOLE] * 4,
        out_specs=WHOLE,
        out_shape=kept((NXY, CAP, LANES), BF16),
        compiler_params=pltpu.CompilerParams(vmem_limit_bytes=SMALL),
        name="down",
    )(own, got, mine, w)


def swap_cores(values):
    return lax.ppermute(values, "c", [(0, 1), (1, 0)])


def per_device(
    prompt_cache,
    assignment,
    resident_cache,
    resident_len,
    queries,
    new_latent,
    residual,
    w_uv,
    w_out,
    norm_gain,
    w_router,
    expert_ids,
    w_gate,
    w_up,
    w_down,
):
    plane = lax.axis_index("z")
    core = lax.axis_index("c")
    place_xy = lax.axis_index("x") * NY + lax.axis_index("y")
    rows_dev = queries.shape[0]
    own_half = jnp.reshape(core, (1,)).astype(jnp.int32)
    other_half = 1 - own_half
    plane_index = jnp.reshape(plane, (1,)).astype(jnp.int32)
    chunk = core * NXY + place_xy

    received = lax.all_to_all(spread(assignment, prompt_cache), ("x", "y", "c"), 0, 0, tiled=True)

    ids_plane = expert_ids - plane * EXP_G
    named = jnp.any(expert_ids[:, :, None] == jnp.arange(NZ * EXP_G, dtype=jnp.int32)[None, None, :], axis=1)
    lower = (jnp.arange(ALL_ROWS)[:, None] > jnp.arange(ALL_ROWS)[None, :]).astype(BF16)
    ranks = jnp.dot(lower, named.astype(BF16), preferred_element_type=F32).astype(jnp.int32)
    ranks = jnp.where(named, ranks, -1)
    plane_ranks = lax.dynamic_slice_in_dim(ranks, plane * EXP_G, EXP_G, 1)
    own_expert = place_xy // 2
    slot_iota = jnp.arange(CAP, dtype=jnp.int32)
    own_ranks = lax.dynamic_index_in_dim(plane_ranks, own_expert, 1, keepdims=False)
    own_slots = (own_ranks[None, :] == slot_iota[:, None]).astype(BF16)
    slot_ids = jnp.dot(own_slots, ids_plane.astype(BF16), preferred_element_type=F32)
    mine = (slot_ids == own_expert.astype(F32)).astype(F32)
    group_ids = lax.dynamic_slice_in_dim(expert_ids, plane * ROWS, ROWS, 0)
    by_group = plane_ranks.reshape(NZ, ROWS, EXP_G)
    step_order = (plane - jnp.arange(NZ, dtype=jnp.int32)) % NZ
    step_ranks = by_group.at[step_order].get(mode="promise_in_bounds").reshape(ALL_ROWS, EXP_G).T
    owner_ranks = plane_ranks.reshape(NZ * NDEV, rows_dev, EXP_G).transpose(1, 0, 2).reshape(ALL_ROWS, EXP_G)
    gain_chunk = lax.dynamic_slice_in_dim(norm_gain, chunk * CHUNK, CHUNK, 0).astype(F32)[None, :]
    router_chunk = lax.dynamic_slice_in_dim(w_router, chunk * CHUNK, CHUNK, 0)
    row_iota = jnp.arange(ROWS, dtype=jnp.int32)
    pair = jnp.arange(2, dtype=jnp.int32)
    first_rows = (place_xy * NC + core + pair * (1 - 2 * core)) * rows_dev
    place = row_iota[None, :, None] == (first_rows[:, None] + jnp.arange(16, dtype=jnp.int32)[None, :])[:, None, :]
    place = (place & (jnp.arange(16) < rows_dev)[None, None, :]).astype(BF16)
    res = jnp.pad(residual, ((0, 16 - rows_dev), (0, 0)))

    given = give_weights(other_half, w_out, res, w_gate, w_up, w_down)
    got_out, got_in, got_down = [swap_cores(a) for a in given]

    cache_iota = jnp.arange(resident_cache.shape[1], dtype=jnp.int32)
    old_masks = cache_iota[None, :] < resident_len[0][:, None]
    context_old = jax.vmap(attend)(queries[1:], resident_cache, old_masks, new_latent[1:])
    context_old = context_old.reshape(-1, LAT)
    held = (
        received, context_old, queries[0].T, step_ranks, owner_ranks, mine, group_ids, gain_chunk,
        router_chunk, place, res, own_half, plane_index, got_out, got_in, got_down,
    )
    (
        received, context_old, first_query, step_ranks, owner_ranks, mine, group_ids, gain_chunk,
        router_chunk, place, res, own_half, plane_index, got_out, got_in, got_down,
    ) = lax.optimization_barrier(held)
    context, w_uv, w_out = prompt_attention(
        own_half, first_query, received, new_latent, context_old, w_uv, w_out, res, got_out
    )

    context = lax.all_to_all(context.reshape(NDEV, -1, LAT), ("x", "y", "c"), 0, 0, tiled=True)
    context = context.reshape(-1, LAT)

    attn = head_values(context, w_uv)
    partial = project(attn, swap_cores(attn), place, w_out)
    partial = lax.all_to_all(partial, ("x", "y"), 0, 0, tiled=True)

    packed, hidden = pack_rows(partial, gain_chunk, router_chunk, group_ids, rows_dev)

    groups = [packed]
    for k in range(1, NZ):
        groups.append(lax.ppermute(packed, "z", [(i, (i + k) % NZ) for i in range(NZ)]))
    w_in, w_down = fetch_experts(packed, own_half, w_gate, w_up, w_down, got_in, got_down)
    slotted = slot_rows(w_down, step_ranks, groups)
    slotted = lax.all_to_all(slotted, ("x", "y"), 0, 0, tiled=True)

    sums, to_send = gate_up(slotted, w_in)
    out = down(sums, swap_cores(to_send), mine, w_down)
    out = lax.all_to_all(out, ("x", "y"), 0, 0, tiled=True)

    total = combine_rows(plane_index, out, owner_ranks, hidden, rows_dev)
    total = lax.all_to_all(total, ("z", "x", "y", "c"), 0, 0, tiled=True)
    total = jnp.sum(total.reshape(NZ, NXY, NC, rows_dev, LANES)[..., :CHUNK].astype(F32), axis=0)
    return total.transpose(2, 1, 0, 3).reshape(rows_dev, D).astype(BF16)


def solution(mesh):
    grid = Mesh(mesh.devices.reshape(NZ, NX, NY, NC), ("z", "x", "y", "c"))
    dev = ("x", "y", "c")
    every = ("z", "x", "y", "c")
    return jax.shard_map(
        per_device,
        mesh=grid,
        in_specs=(
            P("z", dev, None),
            P("z", None),
            P(every, None, None),
            P(every, None),
            P(every, None, None),
            P(every, None),
            P(every, None),
            P(dev, None, None),
            P(dev, None),
            P(),
            P(),
            P(),
            P(every, None, None),
            P(every, None, None),
            P(every, None, None),
        ),
        out_specs=P(every, None),
        check_vma=False,
    )
```

```python
import functools

import jax
import jax.numpy as jnp
from jax import lax
from jax.experimental import pallas as pl
from jax.experimental.pallas import tpu as pltpu
from jax.sharding import Mesh, PartitionSpec as P

LAT = 512
ROPE = 64
NOPE = 128
D = 7168
CAP = 192
NZ, NX, NY, NC = 4, 4, 4, 2
NXY = NX * NY
NDEV = NXY * NC
EXP_G = 8
CHUNK = D // NDEV
HALF = D // 2
LANES = 256
GROUP = 4
BLK = CHUNK * GROUP
STEPS = NXY // GROUP
ROWS = 128
ALL_ROWS = ROWS * NZ
F32 = jnp.float32
BF16 = jnp.bfloat16
SMALL = 16 * 1024 * 1024
LARGE = 20 * 1024 * 1024


def kept(shape, dtype):
    return pltpu.VMEM(shape, dtype)


def in_hbm(array):
    return pltpu.with_memory_space_constraint(array, pltpu.HBM)


def start_all(copies):
    for copy in copies:
        copy.start()
    return copies


WHOLE = pl.BlockSpec(memory_space=pltpu.VMEM)
SCALAR = pl.BlockSpec(memory_space=pltpu.SMEM)
ANYWHERE = pl.BlockSpec(memory_space=pl.ANY)


def attend(query_row, cache_block, valid_mask, own_entry):
    scale_factor = (NOPE + ROPE) ** (-0.5)
    scores = jnp.einsum("hc,kc->hk", query_row, cache_block, preferred_element_type=F32) * scale_factor
    if valid_mask is not None:
        scores = jnp.where(valid_mask[None, :], scores, -jnp.inf)
    own_score = jnp.einsum("hc,c->h", query_row, own_entry, preferred_element_type=F32) * scale_factor
    maximum = jnp.maximum(jnp.max(scores, axis=1), own_score)
    exponent = jnp.exp(scores - maximum[:, None])
    own_exponent = jnp.exp(own_score - maximum)
    totals = jnp.sum(exponent, axis=1) + own_exponent
    weights = (exponent / totals[:, None]).astype(BF16)
    own_weight = (own_exponent / totals).astype(BF16)
    context = jnp.einsum("hk,kl->hl", weights, cache_block[:, :LAT], preferred_element_type=F32)
    context = context + own_weight.astype(F32)[:, None] * own_entry[:LAT].astype(F32)[None, :]
    return context.astype(BF16)


def pack_chunk(ref, at, part):
    rows, most = part.shape[0], part.shape[0] * 3 // 4
    rest = part[:, 128:]
    ref[at, :rows, :] = part[:, :128].astype(ref.dtype)
    ref[at, rows:, :96] = rest[:most].astype(ref.dtype)
    tail = jnp.concatenate([rest[most:, 32 * i : 32 * (i + 1)] for i in range(3)], axis=0)
    ref[at, rows:, 96:] = tail.astype(ref.dtype)


def unpack_chunk(packed):
    rows = packed.shape[0] * 4 // 7
    most, few = rows * 3 // 4, rows // 4
    rest = packed[rows:, :96]
    tail = [packed[rows + few * i : rows + few * (i + 1), 96:] for i in range(3)]
    rest = jnp.concatenate([rest, jnp.concatenate(tail, axis=1)], axis=0)
    return jnp.concatenate([packed[:rows], rest], axis=1)


def spread_kernel(owners_ref, cache_ref, out_ref, held_ref, packed_ref, in_sem, out_sem):
    batch = NDEV // in_sem.shape[0]
    tokens, half = cache_ref.shape[1], cache_ref.shape[1] // 2
    arrive = []
    for b in range(in_sem.shape[0]):
        at = pl.ds(b * batch, batch)
        arrive.append(pltpu.make_async_copy(cache_ref.at[at], held_ref.at[at], in_sem.at[b]))
    leave = [
        pltpu.make_async_copy(packed_ref.at[p], out_ref.at[owners_ref[0, p]], out_sem.at[p])
        for p in range(NDEV)
    ]
    start_all(arrive)
    for p in range(NDEV):
        if p % batch == 0:
            arrive[p // batch].wait()
        for j in range(LAT // 128):
            packed_ref[p, j * tokens : (j + 1) * tokens, :] = held_ref[p, :, j * 128 : (j + 1) * 128]
        tail = jnp.concatenate([held_ref[p, :half, LAT:], held_ref[p, half:, LAT:]], axis=1)
        packed_ref[p, LAT // 128 * tokens :, :] = tail
        leave[p].start()
    for p in range(NDEV):
        leave[p].wait()


def spread(owners, cache):
    packed = (NDEV, cache.shape[1] * cache.shape[2] // 128, 128)
    return pl.pallas_call(
        spread_kernel,
        in_specs=[SCALAR, ANYWHERE],
        out_specs=ANYWHERE,
        scratch_shapes=[
            pltpu.VMEM(cache.shape, cache.dtype),
            pltpu.VMEM(packed, cache.dtype),
            pltpu.SemaphoreType.DMA((8,)),
            pltpu.SemaphoreType.DMA((NDEV,)),
        ],
        out_shape=pltpu.HBM(packed, cache.dtype),
        compiler_params=pltpu.CompilerParams(vmem_limit_bytes=SMALL),
        name="spread",
    )(owners, in_hbm(cache))


def prompt_kernel(
    half_ref, query_hbm, cache_ref, entry_ref, old_hbm, uv_hbm, w_hbm, res_hbm, got_hbm,
    out_ref, uv_ref, w_ref, all_ref, query_ref, sems,
):
    heads_all = query_hbm.shape[1]
    query_copy = pltpu.make_async_copy(query_hbm, query_ref, sems.at[0])
    old_copy = pltpu.make_async_copy(old_hbm, all_ref.at[pl.ds(heads_all, old_hbm.shape[0]), :], sems.at[1])
    uv_copy = pltpu.make_async_copy(uv_hbm, uv_ref, sems.at[2])
    depth = w_hbm.shape[0]
    at = pl.ds(pl.multiple_of(half_ref[0] * HALF, 128), HALF)
    w_copies = (
        pltpu.make_async_copy(w_hbm.at[:, at], w_ref.at[pl.ds(0, depth), :], sems.at[3]),
        pltpu.make_async_copy(res_hbm.at[:, at], w_ref.at[pl.ds(depth, 16), :], sems.at[4]),
        pltpu.make_async_copy(got_hbm, w_ref.at[pl.ds(depth + 16, depth + 16), :], sems.at[5]),
    )
    start_all((query_copy, old_copy, uv_copy) + w_copies)
    scale_factor = (NOPE + ROPE) ** (-0.5)
    sources, tokens = cache_ref.shape[0], cache_ref.shape[1] * 128 // query_ref.shape[0]
    tiles = [cache_ref[:, j * tokens : (j + 1) * tokens, :].reshape(-1, 128) for j in range(LAT // 128)]
    cache = jnp.concatenate(tiles, axis=1)
    rope = cache_ref[:, LAT // 128 * tokens :, :].reshape(-1, 128)
    entry = entry_ref[:1, :]
    query_copy.wait()
    query = query_ref[...]
    tail = query[LAT:, :]
    blank = jnp.zeros_like(tail)
    tail = jnp.concatenate(
        [jnp.concatenate([tail, blank], axis=0), jnp.concatenate([blank, tail], axis=0)], axis=1
    )
    extra = jnp.dot(rope, tail, preferred_element_type=F32)
    extra = [extra[:, h * heads_all : (h + 1) * heads_all].reshape(sources, -1, heads_all) for h in range(2)]
    scores = jnp.dot(cache, query[:LAT, :], preferred_element_type=F32)
    scores = (scores + jnp.concatenate(extra, axis=1).reshape(scores.shape)) * scale_factor
    own_score = jnp.dot(entry, query, preferred_element_type=F32) * scale_factor
    maximum = jnp.maximum(jnp.max(scores, axis=0, keepdims=True), own_score)
    exponent = jnp.exp(scores - maximum)
    own_exponent = jnp.exp(own_score - maximum)
    totals = jnp.sum(exponent, axis=0, keepdims=True) + own_exponent
    weights = (exponent / totals).astype(BF16)
    own_weight = (own_exponent / totals).astype(BF16)
    over_rows = (((0,), (0,)), ((), ()))
    context = lax.dot_general(weights, cache, over_rows, preferred_element_type=F32)
    context = context + lax.dot_general(own_weight, entry[:, :LAT], over_rows, preferred_element_type=F32)
    all_ref[:heads_all, :] = context.astype(BF16)
    rows, block = out_ref.shape[0], out_ref.shape[0] // NDEV
    heads = heads_all // NDEV
    to = lax.broadcasted_iota(jnp.int32, (rows, rows), 0)
    source = (to % block) // heads * heads_all + to // block * heads + to % heads
    order = (lax.broadcasted_iota(jnp.int32, (rows, rows), 1) == source).astype(BF16)
    old_copy.wait()
    out_ref[...] = jnp.dot(order, all_ref[...], preferred_element_type=F32).astype(BF16)
    uv_copy.wait()
    for copy in w_copies:
        copy.wait()


def prompt_attention(half, query, cache, entry, old, w_uv, w_out, res, got):
    rows = query.shape[1] + old.shape[0]
    return pl.pallas_call(
        prompt_kernel,
        in_specs=[SCALAR, ANYWHERE, WHOLE, WHOLE] + [ANYWHERE] * 5,
        out_specs=[WHOLE, ANYWHERE, ANYWHERE],
        out_shape=[
            kept((rows, LAT), BF16), kept(w_uv.shape, BF16), kept((2 * got.shape[0], HALF), BF16),
        ],
        scratch_shapes=[
            pltpu.VMEM((rows, LAT), BF16),
            pltpu.VMEM(query.shape, BF16),
            pltpu.SemaphoreType.DMA((6,)),
        ],
        compiler_params=pltpu.CompilerParams(vmem_limit_bytes=LARGE),
        name="prompt_attention",
    )(half, in_hbm(query), cache, entry, *[in_hbm(a) for a in (old, w_uv, w_out, res, got)])


def values_kernel(context_ref, uv_ref, attn_ref):
    heads, rows = uv_ref.shape[0], context_ref.shape[0]
    context = context_ref[...]
    pick = lax.broadcasted_iota(jnp.int32, (ROWS, rows), 1) // heads
    pick = (pick == lax.broadcasted_iota(jnp.int32, (ROWS, rows), 0)).astype(BF16)
    head = lax.broadcasted_iota(jnp.int32, (rows, uv_ref.shape[2]), 0) % heads
    for h in range(heads):
        values = jnp.dot(context, uv_ref[h], preferred_element_type=F32)
        values = jnp.where(head == h, values, 0.0).astype(BF16)
        values = jnp.dot(pick, values, preferred_element_type=F32).astype(BF16)
        attn_ref[:, h * values.shape[1] : (h + 1) * values.shape[1]] = values


def head_values(context, w_uv):
    return pl.pallas_call(
        values_kernel,
        in_specs=[WHOLE, WHOLE],
        out_specs=WHOLE,
        out_shape=kept((ROWS, w_uv.shape[0] * w_uv.shape[2]), BF16),
        compiler_params=pltpu.CompilerParams(vmem_limit_bytes=SMALL),
        name="head_values",
    )(context, w_uv)


def project_kernel(own_ref, got_ref, place_ref, w_ref, out_ref):
    depth = own_ref.shape[1]
    lhs = (own_ref[...], place_ref[0], got_ref[...], place_ref[1])
    for i in range(STEPS):
        at, acc = 0, jnp.zeros((ROWS, BLK), F32)
        for left in lhs:
            acc = acc + jnp.dot(
                left, w_ref[at : at + left.shape[1], i * BLK : (i + 1) * BLK], preferred_element_type=F32
            )
            at += left.shape[1]
        for g in range(GROUP):
            pack_chunk(out_ref, i * GROUP + g, acc[:, g * CHUNK : (g + 1) * CHUNK])


def project(own, got, place, w_out):
    return pl.pallas_call(
        project_kernel,
        in_specs=[WHOLE] * 4,
        out_specs=WHOLE,
        out_shape=kept((NXY, ROWS * CHUNK // 128, 128), BF16),
        compiler_params=pltpu.CompilerParams(vmem_limit_bytes=SMALL),
        name="project",
    )(own, got, place, w_out)


def rows_kernel(rows_dev, part_ref, gain_ref, router_ref, ids_ref, packed_ref, hidden_ref):
    total = part_ref[0].astype(F32)
    for source in range(1, part_ref.shape[0]):
        total = total + part_ref[source].astype(F32)
    total = unpack_chunk(total.astype(BF16))
    to = lax.broadcasted_iota(jnp.int32, (ROWS, ROWS), 0)
    order = to % (ROWS // rows_dev) * rows_dev + to // (ROWS // rows_dev)
    order = (lax.broadcasted_iota(jnp.int32, (ROWS, ROWS), 1) == order).astype(BF16)
    hidden_ref[...] = jnp.dot(order, total, preferred_element_type=F32)
    hidden = total.astype(F32)
    square = jnp.sum(hidden * hidden, axis=1, keepdims=True)
    scaled = (hidden * gain_ref[...]).astype(BF16)
    logits = jnp.dot(scaled, router_ref[...], preferred_element_type=F32)
    expert = lax.broadcasted_iota(jnp.int32, logits.shape, 1)
    lane = lax.broadcasted_iota(jnp.int32, (ROWS, LANES - CHUNK), 1)
    top = ids_ref.shape[1]
    spare = jnp.zeros((ROWS, LANES - CHUNK), F32)
    for k in range(top + 1):
        value = square
        if k < top:
            value = jnp.sum(jnp.where(expert == ids_ref[:, k : k + 1], logits, 0.0), axis=1, keepdims=True)
        high = value.astype(BF16).astype(F32)
        at_high, at_low = (k, top + k) if k < top else (2 * top, 2 * top + 1)
        spare = jnp.where(lane == at_high, high, jnp.where(lane == at_low, value - high, spare))
    packed_ref[:, :CHUNK] = scaled
    packed_ref[:, CHUNK:] = spare.astype(BF16)


def pack_rows(part, gain, router, ids, rows_dev):
    return pl.pallas_call(
        functools.partial(rows_kernel, rows_dev),
        out_shape=[kept((ROWS, LANES), BF16), kept((ROWS, CHUNK), F32)],
        compiler_params=pltpu.CompilerParams(vmem_limit_bytes=SMALL),
        name="pack_rows",
    )(part, gain, router, ids)


def slot_kernel(after_ref, ranks_ref, *refs):
    packed_refs, out_ref, rows_ref = refs[:NZ], refs[NZ], refs[NZ + 1]
    for k in range(NZ):
        rows_ref[k * ROWS : (k + 1) * ROWS, :] = packed_refs[k][...]
    slot = lax.broadcasted_iota(jnp.int32, (CAP, ALL_ROWS), 0)
    for e in range(EXP_G):
        table = (ranks_ref[e : e + 1, :] == slot).astype(BF16)
        slotted = jnp.dot(table, rows_ref[...], preferred_element_type=F32).astype(BF16)
        out_ref[2 * e] = slotted
        out_ref[2 * e + 1] = slotted


def slot_rows(after, ranks, packed):
    return pl.pallas_call(
        slot_kernel,
        in_specs=[ANYWHERE] + [WHOLE] * (1 + NZ),
        out_specs=WHOLE,
        out_shape=kept((NXY, CAP, LANES), BF16),
        scratch_shapes=[pltpu.VMEM((ALL_ROWS, LANES), BF16)],
        compiler_params=pltpu.CompilerParams(vmem_limit_bytes=SMALL),
        name="slot_rows",
    )(after, ranks, *packed)


def combine_kernel(plane_ref, out_ref, ranks_ref, hidden_ref, rows_ref, acc_ref):
    slot = lax.broadcasted_iota(jnp.int32, (ALL_ROWS, CAP), 1)
    acc = jnp.zeros((ALL_ROWS, CHUNK), F32)
    for e in range(EXP_G):
        table = (ranks_ref[:, e : e + 1] == slot).astype(BF16)
        for source in (2 * e, 2 * e + 1):
            acc = acc + jnp.dot(table, unpack_chunk(out_ref[source]), preferred_element_type=F32)
    acc_ref[...] = acc
    span, count = rows_ref.shape[0], rows_ref.shape[1]
    own = ROWS // count
    for r in range(count):
        at = pl.multiple_of(r * span + plane_ref[0] * own, 8)
        acc_ref[pl.ds(at, own), :] += hidden_ref[r * own : (r + 1) * own, :]
    for r in range(count):
        rows_ref[:, r, :] = acc_ref[r * span : (r + 1) * span, :].astype(BF16)


def combine_rows(plane, out, ranks, hidden, count):
    vmem = pl.BlockSpec(memory_space=pltpu.VMEM)
    return pl.pallas_call(
        combine_kernel,
        in_specs=[pl.BlockSpec(memory_space=pltpu.SMEM), vmem, vmem, vmem],
        out_specs=vmem,
        out_shape=kept((ALL_ROWS // count, count, CHUNK), BF16),
        scratch_shapes=[pltpu.VMEM((ALL_ROWS, CHUNK), F32)],
        compiler_params=pltpu.CompilerParams(vmem_limit_bytes=SMALL),
        name="combine_rows",
    )(plane, out, ranks, hidden)


def give_kernel(
    half_ref, out_hbm, res_hbm, gate_hbm, up_hbm, down_hbm, to_out, to_in, to_down,
    out_ref, in_ref, down_ref, in_sems, out_sems,
):
    depth = out_hbm.shape[0]
    columns = pl.ds(pl.multiple_of(half_ref[0] * HALF, 128), HALF)
    rows = pl.ds(pl.multiple_of(half_ref[0] * HALF, 16), HALF)
    sources = (
        (out_hbm.at[:, columns], out_ref.at[pl.ds(0, depth), :], to_out.at[pl.ds(0, depth), :]),
        (res_hbm.at[:, columns], out_ref.at[pl.ds(depth, 16), :], to_out.at[pl.ds(depth, 16), :]),
        (gate_hbm.at[0, rows, :], in_ref.at[0], to_in.at[0]),
        (up_hbm.at[0, rows, :], in_ref.at[1], to_in.at[1]),
        (down_hbm.at[0, :, columns], down_ref, to_down),
    )
    arrive = [pltpu.make_async_copy(a, b, in_sems.at[n]) for n, (a, b, _) in enumerate(sources)]
    leave = [pltpu.make_async_copy(b, c, out_sems.at[n]) for n, (_, b, c) in enumerate(sources)]
    start_all(arrive)
    for first, second in zip(arrive, leave):
        first.wait()
        second.start()
    for copy in leave:
        copy.wait()


def give_weights(half, w_out, res, w_gate, w_up, w_down):
    hidden = w_gate.shape[2]
    arrays = (w_out, res, w_gate, w_up, w_down)
    return pl.pallas_call(
        give_kernel,
        in_specs=[SCALAR] + [ANYWHERE] * 5,
        out_specs=[ANYWHERE] * 3,
        out_shape=[
            pltpu.HBM((w_out.shape[0] + 16, HALF), BF16),
            pltpu.HBM((2, HALF, hidden), BF16),
            pltpu.HBM((hidden, HALF), BF16),
        ],
        scratch_shapes=[
            pltpu.VMEM((w_out.shape[0] + 16, HALF), BF16),
            pltpu.VMEM((2, HALF, hidden), BF16),
            pltpu.VMEM((hidden, HALF), BF16),
            pltpu.SemaphoreType.DMA((5,)),
            pltpu.SemaphoreType.DMA((5,)),
        ],
        compiler_params=pltpu.CompilerParams(vmem_limit_bytes=SMALL),
        name="give_weights",
    )(half, *[in_hbm(a) for a in arrays])


def fetch_kernel(
    after_ref, half_ref, gate_hbm, up_hbm, down_hbm, got_in_hbm, got_down_hbm, in_ref, down_ref, sems
):
    hidden = gate_hbm.shape[2]
    columns = pl.ds(pl.multiple_of(half_ref[0] * HALF, 128), HALF)
    rows = pl.ds(pl.multiple_of(half_ref[0] * HALF, 16), HALF)
    sources = (gate_hbm.at[0, rows, :], up_hbm.at[0, rows, :], got_in_hbm.at[0], got_in_hbm.at[1])
    copies = [
        pltpu.make_async_copy(source, in_ref.at[:, pl.ds(j * hidden, hidden)], sems.at[j])
        for j, source in enumerate(sources)
    ]
    copies.append(
        pltpu.make_async_copy(down_hbm.at[0, :, columns], down_ref.at[pl.ds(0, hidden), :], sems.at[4])
    )
    copies.append(pltpu.make_async_copy(got_down_hbm, down_ref.at[pl.ds(hidden, hidden), :], sems.at[5]))
    for copy in start_all(copies):
        copy.wait()


def fetch_experts(after, half, w_gate, w_up, w_down, got_in, got_down):
    hidden = w_gate.shape[2]
    return pl.pallas_call(
        fetch_kernel,
        in_specs=[ANYWHERE, SCALAR] + [ANYWHERE] * 5,
        out_specs=[ANYWHERE] * 2,
        out_shape=[kept((HALF, 4 * hidden), BF16), kept((2 * hidden, HALF), BF16)],
        scratch_shapes=[pltpu.SemaphoreType.DMA((6,))],
        compiler_params=pltpu.CompilerParams(vmem_limit_bytes=SMALL),
        cost_estimate=pl.CostEstimate(flops=0, bytes_accessed=12 * D * hidden, transcendentals=0),
        name="fetch_experts",
    )(after, half, *[in_hbm(a) for a in (w_gate, w_up, w_down, got_in, got_down)])


def gate_up_kernel(y_ref, w_ref, own_ref, send_ref):
    width = w_ref.shape[1]
    acc = jnp.zeros((CAP, width), F32)
    stats = jnp.zeros((CAP, LANES - CHUNK), F32)
    for p in range(NXY):
        acc = acc + jnp.dot(
            y_ref[p, :, :CHUNK], w_ref[p * CHUNK : (p + 1) * CHUNK, :], preferred_element_type=F32
        )
        stats = stats + y_ref[p, :, CHUNK:].astype(F32)
    own_ref[:, :width] = acc
    send_ref[:, :width] = acc.astype(BF16)
    high = stats.astype(BF16).astype(F32)
    spare = jnp.zeros((CAP, 128 - 2 * stats.shape[1]), F32)
    own_ref[:, width:] = jnp.concatenate([stats, jnp.zeros_like(stats), spare], axis=1)
    send_ref[:, width:] = jnp.concatenate([high, stats - high, spare], axis=1).astype(BF16)


def gate_up(y, w):
    width = w.shape[1] + 128
    return pl.pallas_call(
        gate_up_kernel,
        in_specs=[WHOLE] * 2,
        out_specs=[WHOLE] * 2,
        out_shape=[kept((CAP, width), F32), kept((CAP, width), BF16)],
        compiler_params=pltpu.CompilerParams(vmem_limit_bytes=SMALL),
        name="gate_up",
    )(y, w)


def down_kernel(own_ref, got_ref, mine_ref, w_ref, out_ref):
    slices = w_ref.shape[0]
    hidden = slices // 2
    width = 2 * slices
    lanes = LANES - CHUNK
    stats = own_ref[:, width : width + lanes]
    stats = stats + got_ref[:, width : width + lanes].astype(F32)
    stats = stats + got_ref[:, width + lanes : width + 2 * lanes].astype(F32)
    square = stats[:, 16:17] + stats[:, 17:18]
    scale = lax.rsqrt(square * (1.0 / D) + 1e-6)
    affinity = jax.nn.sigmoid((stats[:, 0:8] + stats[:, 8:16]) * scale)
    own = jnp.sum(affinity * mine_ref[...], axis=1, keepdims=True)
    gates = 2.5 * own / jnp.sum(affinity, axis=1, keepdims=True)
    gates = gates.astype(BF16).astype(F32)
    acts = []
    for j in range(2):
        here, there = j * slices, (1 - j) * slices
        both = own_ref[:, here : here + slices] + got_ref[:, there : there + slices].astype(F32)
        gate = both[:, :hidden] * scale
        acts.append((gate * jax.nn.sigmoid(gate) * (both[:, hidden:] * scale)).astype(BF16))
    act = jnp.concatenate(acts, axis=1)
    for i in range(STEPS):
        acc = jnp.dot(act, w_ref[:, i * BLK : (i + 1) * BLK], preferred_element_type=F32) * gates
        for g in range(GROUP):
            pack_chunk(out_ref, i * GROUP + g, acc[:, g * CHUNK : (g + 1) * CHUNK])


def down(own, got, mine, w):
    return pl.pallas_call(
        down_kernel,
        in_specs=[WHOLE] * 4,
        out_specs=WHOLE,
        out_shape=kept((NXY, CAP * CHUNK // 128, 128), BF16),
        compiler_params=pltpu.CompilerParams(vmem_limit_bytes=SMALL),
        name="down",
    )(own, got, mine, w)


def swap_cores(values):
    return lax.ppermute(values, "c", [(0, 1), (1, 0)])


def per_device(
    prompt_cache,
    assignment,
    resident_cache,
    resident_len,
    queries,
    new_latent,
    residual,
    w_uv,
    w_out,
    norm_gain,
    w_router,
    expert_ids,
    w_gate,
    w_up,
    w_down,
):
    plane = lax.axis_index("z")
    core = lax.axis_index("c")
    place_xy = lax.axis_index("x") * NY + lax.axis_index("y")
    rows_dev = queries.shape[0]
    own_half = jnp.reshape(core, (1,)).astype(jnp.int32)
    other_half = 1 - own_half
    plane_index = jnp.reshape(plane, (1,)).astype(jnp.int32)
    chunk = core * NXY + place_xy

    received = lax.all_to_all(spread(assignment, prompt_cache), ("x", "y", "c"), 0, 0, tiled=True)

    ids_plane = expert_ids - plane * EXP_G
    named = jnp.any(expert_ids[:, :, None] == jnp.arange(NZ * EXP_G, dtype=jnp.int32)[None, None, :], axis=1)
    lower = (jnp.arange(ALL_ROWS)[:, None] > jnp.arange(ALL_ROWS)[None, :]).astype(BF16)
    ranks = jnp.dot(lower, named.astype(BF16), preferred_element_type=F32).astype(jnp.int32)
    ranks = jnp.where(named, ranks, -1)
    plane_ranks = lax.dynamic_slice_in_dim(ranks, plane * EXP_G, EXP_G, 1)
    own_expert = place_xy // 2
    slot_iota = jnp.arange(CAP, dtype=jnp.int32)
    own_ranks = lax.dynamic_index_in_dim(plane_ranks, own_expert, 1, keepdims=False)
    own_slots = (own_ranks[None, :] == slot_iota[:, None]).astype(BF16)
    slot_ids = jnp.dot(own_slots, ids_plane.astype(BF16), preferred_element_type=F32)
    mine = (slot_ids == own_expert.astype(F32)).astype(F32)
    group_ids = lax.dynamic_slice_in_dim(expert_ids, plane * ROWS, ROWS, 0)
    by_group = plane_ranks.reshape(NZ, ROWS, EXP_G)
    step_order = (plane - jnp.arange(NZ, dtype=jnp.int32)) % NZ
    step_ranks = by_group.at[step_order].get(mode="promise_in_bounds").reshape(ALL_ROWS, EXP_G).T
    owner_ranks = plane_ranks.reshape(NZ * NDEV, rows_dev, EXP_G).transpose(1, 0, 2).reshape(ALL_ROWS, EXP_G)
    gain_chunk = lax.dynamic_slice_in_dim(norm_gain, chunk * CHUNK, CHUNK, 0).astype(F32)[None, :]
    router_chunk = lax.dynamic_slice_in_dim(w_router, chunk * CHUNK, CHUNK, 0)
    row_iota = jnp.arange(ROWS, dtype=jnp.int32)
    pair = jnp.arange(2, dtype=jnp.int32)
    first_rows = (place_xy * NC + core + pair * (1 - 2 * core)) * rows_dev
    place = row_iota[None, :, None] == (first_rows[:, None] + jnp.arange(16, dtype=jnp.int32)[None, :])[:, None, :]
    place = (place & (jnp.arange(16) < rows_dev)[None, None, :]).astype(BF16)
    res = jnp.pad(residual, ((0, 16 - rows_dev), (0, 0)))

    given = give_weights(other_half, w_out, res, w_gate, w_up, w_down)
    got_out, got_in, got_down = [swap_cores(a) for a in given]

    cache_iota = jnp.arange(resident_cache.shape[1], dtype=jnp.int32)
    old_masks = cache_iota[None, :] < resident_len[0][:, None]
    context_old = jax.vmap(attend)(queries[1:], resident_cache, old_masks, new_latent[1:])
    context_old = context_old.reshape(-1, LAT)
    held = (
        received, context_old, queries[0].T, step_ranks, owner_ranks, mine, group_ids, gain_chunk,
        router_chunk, place, res, own_half, plane_index, got_out, got_in, got_down,
    )
    (
        received, context_old, first_query, step_ranks, owner_ranks, mine, group_ids, gain_chunk,
        router_chunk, place, res, own_half, plane_index, got_out, got_in, got_down,
    ) = lax.optimization_barrier(held)
    context, w_uv, w_out = prompt_attention(
        own_half, first_query, received, new_latent, context_old, w_uv, w_out, res, got_out
    )

    context = lax.all_to_all(context.reshape(NDEV, -1, LAT), ("x", "y", "c"), 0, 0, tiled=True)
    context = context.reshape(-1, LAT)

    attn = head_values(context, w_uv)
    partial = project(attn, swap_cores(attn), place, w_out)
    partial = lax.all_to_all(partial, ("x", "y"), 0, 0, tiled=True)

    packed, hidden = pack_rows(partial, gain_chunk, router_chunk, group_ids, rows_dev)

    groups = [packed]
    for k in range(1, NZ):
        groups.append(lax.ppermute(packed, "z", [(i, (i + k) % NZ) for i in range(NZ)]))
    w_in, w_down = fetch_experts(packed, own_half, w_gate, w_up, w_down, got_in, got_down)
    slotted = slot_rows(w_down, step_ranks, groups)
    slotted = lax.all_to_all(slotted, ("x", "y"), 0, 0, tiled=True)

    sums, to_send = gate_up(slotted, w_in)
    out = down(sums, swap_cores(to_send), mine, w_down)
    out = lax.all_to_all(out, ("x", "y"), 0, 0, tiled=True)

    total = combine_rows(plane_index, out, owner_ranks, hidden, rows_dev)
    total = lax.all_to_all(total, ("z", "x", "y", "c"), 0, 0, tiled=True)
    total = jnp.sum(total.reshape(NZ, NXY, NC, rows_dev, CHUNK).astype(F32), axis=0)
    return total.transpose(2, 1, 0, 3).reshape(rows_dev, D).astype(BF16)


def solution(mesh):
    grid = Mesh(mesh.devices.reshape(NZ, NX, NY, NC), ("z", "x", "y", "c"))
    dev = ("x", "y", "c")
    every = ("z", "x", "y", "c")
    return jax.shard_map(
        per_device,
        mesh=grid,
        in_specs=(
            P("z", dev, None),
            P("z", None),
            P(every, None, None),
            P(every, None),
            P(every, None, None),
            P(every, None),
            P(every, None),
            P(dev, None, None),
            P(dev, None),
            P(),
            P(),
            P(),
            P(every, None, None),
            P(every, None, None),
            P(every, None, None),
        ),
        out_specs=P(every, None),
        check_vma=False,
    )
```

```python
import functools

import jax
import jax.numpy as jnp
from jax import lax
from jax.experimental import pallas as pl
from jax.experimental.pallas import tpu as pltpu
from jax.sharding import Mesh, PartitionSpec as P

LAT = 512
ROPE = 64
NOPE = 128
D = 7168
CAP = 192
NZ, NX, NY, NC = 4, 4, 4, 2
NXY = NX * NY
NDEV = NXY * NC
EXP_G = 8
CHUNK = D // NDEV
HALF = D // 2
PARTS = 4
LANES = 256
GROUP = 4
BLK = CHUNK * GROUP
STEPS = NXY // GROUP
ROWS = 128
ALL_ROWS = ROWS * NZ
F32 = jnp.float32
BF16 = jnp.bfloat16
SMALL = 16 * 1024 * 1024
LARGE = 20 * 1024 * 1024


def kept(shape, dtype):
    return pltpu.VMEM(shape, dtype)


def in_hbm(array):
    return pltpu.with_memory_space_constraint(array, pltpu.HBM)


def start_all(copies):
    for copy in copies:
        copy.start()
    return copies


WHOLE = pl.BlockSpec(memory_space=pltpu.VMEM)
SCALAR = pl.BlockSpec(memory_space=pltpu.SMEM)
ANYWHERE = pl.BlockSpec(memory_space=pl.ANY)


def attend(query_row, cache_block, valid_mask, own_entry):
    scale_factor = (NOPE + ROPE) ** (-0.5)
    scores = jnp.einsum("hc,kc->hk", query_row, cache_block, preferred_element_type=F32) * scale_factor
    if valid_mask is not None:
        scores = jnp.where(valid_mask[None, :], scores, -jnp.inf)
    own_score = jnp.einsum("hc,c->h", query_row, own_entry, preferred_element_type=F32) * scale_factor
    maximum = jnp.maximum(jnp.max(scores, axis=1), own_score)
    exponent = jnp.exp(scores - maximum[:, None])
    own_exponent = jnp.exp(own_score - maximum)
    totals = jnp.sum(exponent, axis=1) + own_exponent
    weights = (exponent / totals[:, None]).astype(BF16)
    own_weight = (own_exponent / totals).astype(BF16)
    context = jnp.einsum("hk,kl->hl", weights, cache_block[:, :LAT], preferred_element_type=F32)
    context = context + own_weight.astype(F32)[:, None] * own_entry[:LAT].astype(F32)[None, :]
    return context.astype(BF16)


def pack_chunk(ref, at, part):
    rows, most = part.shape[0], part.shape[0] * 3 // 4
    rest = part[:, 128:]
    ref[at, :rows, :] = part[:, :128].astype(ref.dtype)
    ref[at, rows:, :96] = rest[:most].astype(ref.dtype)
    tail = jnp.concatenate([rest[most:, 32 * i : 32 * (i + 1)] for i in range(3)], axis=0)
    ref[at, rows:, 96:] = tail.astype(ref.dtype)


def unpack_chunk(packed):
    rows = packed.shape[0] * 4 // 7
    most, few = rows * 3 // 4, rows // 4
    rest = packed[rows:, :96]
    tail = [packed[rows + few * i : rows + few * (i + 1), 96:] for i in range(3)]
    rest = jnp.concatenate([rest, jnp.concatenate(tail, axis=1)], axis=0)
    return jnp.concatenate([packed[:rows], rest], axis=1)


def spread_kernel(owners_hbm, cache_ref, out_ref, owners_ref, held_ref, packed_ref, owner_sem, in_sem, out_sem):
    owners_copy = pltpu.make_async_copy(owners_hbm, owners_ref, owner_sem)
    owners_copy.start()
    batch = NDEV // in_sem.shape[0]
    tokens, half = cache_ref.shape[1], cache_ref.shape[1] // 2
    arrive = []
    for b in range(in_sem.shape[0]):
        at = pl.ds(b * batch, batch)
        arrive.append(pltpu.make_async_copy(cache_ref.at[at], held_ref.at[at], in_sem.at[b]))
    start_all(arrive)
    owners_copy.wait()
    leave = [
        pltpu.make_async_copy(packed_ref.at[p], out_ref.at[owners_ref[0, p]], out_sem.at[p])
        for p in range(NDEV)
    ]
    for p in range(NDEV):
        if p % batch == 0:
            arrive[p // batch].wait()
        for j in range(LAT // 128):
            packed_ref[p, j * tokens : (j + 1) * tokens, :] = held_ref[p, :, j * 128 : (j + 1) * 128]
        tail = jnp.concatenate([held_ref[p, :half, LAT:], held_ref[p, half:, LAT:]], axis=1)
        packed_ref[p, LAT // 128 * tokens :, :] = tail
        leave[p].start()
    for p in range(NDEV):
        leave[p].wait()


def spread(owners, cache):
    packed = (NDEV, cache.shape[1] * cache.shape[2] // 128, 128)
    return pl.pallas_call(
        spread_kernel,
        in_specs=[ANYWHERE, ANYWHERE],
        out_specs=ANYWHERE,
        scratch_shapes=[
            pltpu.SMEM(owners.shape, owners.dtype),
            pltpu.VMEM(cache.shape, cache.dtype),
            pltpu.VMEM(packed, cache.dtype),
            pltpu.SemaphoreType.DMA,
            pltpu.SemaphoreType.DMA((8,)),
            pltpu.SemaphoreType.DMA((NDEV,)),
        ],
        out_shape=pltpu.HBM(packed, cache.dtype),
        compiler_params=pltpu.CompilerParams(vmem_limit_bytes=SMALL),
        name="spread",
    )(in_hbm(owners), in_hbm(cache))


def prompt_kernel(
    half_ref, query_hbm, cache_ref, entry_ref, old_hbm, uv_hbm, w_hbm, res_hbm, got_hbm,
    out_ref, uv_ref, w_ref, old_ref, query_ref, sems,
):
    heads_all = query_hbm.shape[1]
    query_copy = pltpu.make_async_copy(query_hbm, query_ref, sems.at[0])
    old_copy = pltpu.make_async_copy(old_hbm, old_ref, sems.at[1])
    uv_copy = pltpu.make_async_copy(uv_hbm, uv_ref, sems.at[2])
    depth = w_hbm.shape[0]
    at = pl.ds(pl.multiple_of(half_ref[0] * HALF, 128), HALF)
    w_copies = [pltpu.make_async_copy(res_hbm.at[:, at], w_ref.at[pl.ds(depth, 16), :], sems.at[3])]
    span = depth // PARTS
    for n in range(PARTS):
        rows = pl.ds(n * span, span)
        w_copies.append(pltpu.make_async_copy(w_hbm.at[rows, at], w_ref.at[rows, :], sems.at[4 + n]))
        span_got = span + 16 if n == PARTS - 1 else span
        w_copies.append(
            pltpu.make_async_copy(
                got_hbm.at[pl.ds(n * span, span_got), :],
                w_ref.at[pl.ds(depth + 16 + n * span, span_got), :],
                sems.at[4 + PARTS + n],
            )
        )
    start_all([query_copy, old_copy, uv_copy] + w_copies)
    scale_factor = (NOPE + ROPE) ** (-0.5)
    sources, tokens = cache_ref.shape[0], cache_ref.shape[1] * 128 // query_ref.shape[0]
    tiles = [cache_ref[:, j * tokens : (j + 1) * tokens, :].reshape(-1, 128) for j in range(LAT // 128)]
    cache = jnp.concatenate(tiles, axis=1)
    rope = cache_ref[:, LAT // 128 * tokens :, :].reshape(-1, 128)
    entry = entry_ref[:1, :]
    query_copy.wait()
    query = query_ref[...]
    tail = query[LAT:, :]
    blank = jnp.zeros_like(tail)
    tail = jnp.concatenate(
        [jnp.concatenate([tail, blank], axis=0), jnp.concatenate([blank, tail], axis=0)], axis=1
    )
    extra = jnp.dot(rope, tail, preferred_element_type=F32)
    extra = [extra[:, h * heads_all : (h + 1) * heads_all].reshape(sources, -1, heads_all) for h in range(2)]
    scores = jnp.dot(cache, query[:LAT, :], preferred_element_type=F32)
    scores = (scores + jnp.concatenate(extra, axis=1).reshape(scores.shape)) * scale_factor
    own_score = jnp.dot(entry, query, preferred_element_type=F32) * scale_factor
    maximum = jnp.maximum(jnp.max(scores, axis=0, keepdims=True), own_score)
    exponent = jnp.exp(scores - maximum)
    own_exponent = jnp.exp(own_score - maximum)
    totals = jnp.sum(exponent, axis=0, keepdims=True) + own_exponent
    inverse = 1.0 / totals
    weights = (exponent * inverse).astype(BF16)
    own_weight = (own_exponent * inverse).astype(BF16)
    over_rows = (((0,), (0,)), ((), ()))
    context = lax.dot_general(weights, cache, over_rows, preferred_element_type=F32)
    context = context + lax.dot_general(own_weight, entry[:, :LAT], over_rows, preferred_element_type=F32)
    rows, block = out_ref.shape[0], out_ref.shape[0] // NDEV
    heads = heads_all // NDEV
    to = lax.broadcasted_iota(jnp.int32, (rows, heads_all), 0)
    source = jnp.where(to % block < heads, to // block * heads + to % block, -1)
    order = (lax.broadcasted_iota(jnp.int32, (rows, heads_all), 1) == source).astype(BF16)
    placed = jnp.dot(order, context.astype(BF16), preferred_element_type=F32)
    old_copy.wait()
    out_ref[...] = (placed + old_ref[...].astype(F32)).astype(BF16)
    uv_copy.wait()
    for copy in w_copies:
        copy.wait()


def prompt_attention(half, query, cache, entry, old, w_uv, w_out, res, got):
    rows = old.shape[0]
    return pl.pallas_call(
        prompt_kernel,
        in_specs=[SCALAR, ANYWHERE, WHOLE, WHOLE] + [ANYWHERE] * 5,
        out_specs=[WHOLE, ANYWHERE, ANYWHERE],
        out_shape=[
            kept((rows, LAT), BF16), kept(w_uv.shape, BF16), kept((2 * got.shape[0], HALF), BF16),
        ],
        scratch_shapes=[
            pltpu.VMEM((rows, LAT), BF16),
            pltpu.VMEM(query.shape, BF16),
            pltpu.SemaphoreType.DMA((4 + 2 * PARTS,)),
        ],
        compiler_params=pltpu.CompilerParams(vmem_limit_bytes=LARGE),
        name="prompt_attention",
    )(half, in_hbm(query), cache, entry, *[in_hbm(a) for a in (old, w_uv, w_out, res, got)])


def values_kernel(context_ref, uv_ref, attn_ref):
    heads, rows = uv_ref.shape[0], context_ref.shape[0]
    context = context_ref[...]
    pick = lax.broadcasted_iota(jnp.int32, (ROWS, rows), 1) // heads
    pick = (pick == lax.broadcasted_iota(jnp.int32, (ROWS, rows), 0)).astype(BF16)
    head = lax.broadcasted_iota(jnp.int32, (rows, uv_ref.shape[2]), 0) % heads
    for h in range(heads):
        values = jnp.dot(context, uv_ref[h], preferred_element_type=F32)
        values = jnp.where(head == h, values, 0.0).astype(BF16)
        values = jnp.dot(pick, values, preferred_element_type=F32).astype(BF16)
        attn_ref[:, h * values.shape[1] : (h + 1) * values.shape[1]] = values


def head_values(context, w_uv):
    return pl.pallas_call(
        values_kernel,
        in_specs=[WHOLE, WHOLE],
        out_specs=WHOLE,
        out_shape=kept((ROWS, w_uv.shape[0] * w_uv.shape[2]), BF16),
        compiler_params=pltpu.CompilerParams(vmem_limit_bytes=SMALL),
        name="head_values",
    )(context, w_uv)


def project_kernel(own_ref, got_ref, place_ref, w_ref, out_ref):
    depth = own_ref.shape[1]
    lhs = (own_ref[...], place_ref[0], got_ref[...], place_ref[1])
    for i in range(STEPS):
        at, acc = 0, jnp.zeros((ROWS, BLK), F32)
        for left in lhs:
            acc = acc + jnp.dot(
                left, w_ref[at : at + left.shape[1], i * BLK : (i + 1) * BLK], preferred_element_type=F32
            )
            at += left.shape[1]
        for g in range(GROUP):
            pack_chunk(out_ref, i * GROUP + g, acc[:, g * CHUNK : (g + 1) * CHUNK])


def project(own, got, place, w_out):
    return pl.pallas_call(
        project_kernel,
        in_specs=[WHOLE] * 4,
        out_specs=WHOLE,
        out_shape=kept((NXY, ROWS * CHUNK // 128, 128), BF16),
        compiler_params=pltpu.CompilerParams(vmem_limit_bytes=SMALL),
        name="project",
    )(own, got, place, w_out)


def rows_kernel(rows_dev, part_ref, gain_ref, router_ref, ids_ref, packed_ref, hidden_ref):
    total = part_ref[0].astype(F32)
    for source in range(1, part_ref.shape[0]):
        total = total + part_ref[source].astype(F32)
    total = unpack_chunk(total.astype(BF16))
    to = lax.broadcasted_iota(jnp.int32, (ROWS, ROWS), 0)
    order = to % (ROWS // rows_dev) * rows_dev + to // (ROWS // rows_dev)
    order = (lax.broadcasted_iota(jnp.int32, (ROWS, ROWS), 1) == order).astype(BF16)
    hidden_ref[...] = jnp.dot(order, total, preferred_element_type=F32)
    hidden = total.astype(F32)
    square = jnp.sum(hidden * hidden, axis=1, keepdims=True)
    scaled = (hidden * gain_ref[...]).astype(BF16)
    logits = jnp.dot(scaled, router_ref[...], preferred_element_type=F32)
    expert = lax.broadcasted_iota(jnp.int32, logits.shape, 1)
    lane = lax.broadcasted_iota(jnp.int32, (ROWS, LANES - CHUNK), 1)
    top = ids_ref.shape[1]
    spare = jnp.zeros((ROWS, LANES - CHUNK), F32)
    for k in range(top + 1):
        value = square
        if k < top:
            value = jnp.sum(jnp.where(expert == ids_ref[:, k : k + 1], logits, 0.0), axis=1, keepdims=True)
        high = value.astype(BF16).astype(F32)
        at_high, at_low = (k, top + k) if k < top else (2 * top, 2 * top + 1)
        spare = jnp.where(lane == at_high, high, jnp.where(lane == at_low, value - high, spare))
    packed_ref[:, :CHUNK] = scaled
    packed_ref[:, CHUNK:] = spare.astype(BF16)


def pack_rows(part, gain, router, ids, rows_dev):
    return pl.pallas_call(
        functools.partial(rows_kernel, rows_dev),
        out_shape=[kept((ROWS, LANES), BF16), kept((ROWS, CHUNK), F32)],
        compiler_params=pltpu.CompilerParams(vmem_limit_bytes=SMALL),
        name="pack_rows",
    )(part, gain, router, ids)


def slot_kernel(after_ref, ranks_ref, *refs):
    packed_refs, out_ref, rows_ref = refs[:NZ], refs[NZ], refs[NZ + 1]
    for k in range(NZ):
        rows_ref[k * ROWS : (k + 1) * ROWS, :] = packed_refs[k][...]
    slot = lax.broadcasted_iota(jnp.int32, (CAP, ALL_ROWS), 0)
    for e in range(EXP_G):
        table = (ranks_ref[e : e + 1, :] == slot).astype(BF16)
        slotted = jnp.dot(table, rows_ref[...], preferred_element_type=F32).astype(BF16)
        out_ref[2 * e] = slotted
        out_ref[2 * e + 1] = slotted


def slot_rows(after, ranks, packed):
    return pl.pallas_call(
        slot_kernel,
        in_specs=[ANYWHERE] + [WHOLE] * (1 + NZ),
        out_specs=WHOLE,
        out_shape=kept((NXY, CAP, LANES), BF16),
        scratch_shapes=[pltpu.VMEM((ALL_ROWS, LANES), BF16)],
        compiler_params=pltpu.CompilerParams(vmem_limit_bytes=SMALL),
        name="slot_rows",
    )(after, ranks, *packed)


def combine_kernel(plane_ref, out_ref, ranks_ref, hidden_ref, rows_ref, acc_ref):
    slot = lax.broadcasted_iota(jnp.int32, (ALL_ROWS, CAP), 1)
    acc = jnp.zeros((ALL_ROWS, CHUNK), F32)
    for e in range(EXP_G):
        table = (ranks_ref[:, e : e + 1] == slot).astype(BF16)
        for source in (2 * e, 2 * e + 1):
            acc = acc + jnp.dot(table, unpack_chunk(out_ref[source]), preferred_element_type=F32)
    acc_ref[...] = acc
    span, count = rows_ref.shape[0], rows_ref.shape[1]
    own = ROWS // count
    for r in range(count):
        at = pl.multiple_of(r * span + plane_ref[0] * own, 8)
        acc_ref[pl.ds(at, own), :] += hidden_ref[r * own : (r + 1) * own, :]
    for r in range(count):
        rows_ref[:, r, :] = acc_ref[r * span : (r + 1) * span, :].astype(BF16)


def combine_rows(plane, out, ranks, hidden, count):
    vmem = pl.BlockSpec(memory_space=pltpu.VMEM)
    return pl.pallas_call(
        combine_kernel,
        in_specs=[pl.BlockSpec(memory_space=pltpu.SMEM), vmem, vmem, vmem],
        out_specs=vmem,
        out_shape=kept((ALL_ROWS // count, count, CHUNK), BF16),
        scratch_shapes=[pltpu.VMEM((ALL_ROWS, CHUNK), F32)],
        compiler_params=pltpu.CompilerParams(vmem_limit_bytes=SMALL),
        name="combine_rows",
    )(plane, out, ranks, hidden)


def give_kernel(
    half_ref, out_hbm, res_hbm, gate_hbm, up_hbm, down_hbm, to_out, to_in, to_down,
    out_ref, in_ref, down_ref, in_sems, out_sems,
):
    depth = out_hbm.shape[0]
    columns = pl.ds(pl.multiple_of(half_ref[0] * HALF, 128), HALF)
    rows = pl.ds(pl.multiple_of(half_ref[0] * HALF, 16), HALF)
    sources = (
        (out_hbm.at[:, columns], out_ref.at[pl.ds(0, depth), :], to_out.at[pl.ds(0, depth), :]),
        (res_hbm.at[:, columns], out_ref.at[pl.ds(depth, 16), :], to_out.at[pl.ds(depth, 16), :]),
        (gate_hbm.at[0, rows, :], in_ref.at[0], to_in.at[0]),
        (up_hbm.at[0, rows, :], in_ref.at[1], to_in.at[1]),
        (down_hbm.at[0, :, columns], down_ref, to_down),
    )
    arrive = [pltpu.make_async_copy(a, b, in_sems.at[n]) for n, (a, b, _) in enumerate(sources)]
    leave = [pltpu.make_async_copy(b, c, out_sems.at[n]) for n, (_, b, c) in enumerate(sources)]
    start_all(arrive)
    for first, second in zip(arrive, leave):
        first.wait()
        second.start()
    for copy in leave:
        copy.wait()


def give_weights(half, w_out, res, w_gate, w_up, w_down):
    hidden = w_gate.shape[2]
    arrays = (w_out, res, w_gate, w_up, w_down)
    return pl.pallas_call(
        give_kernel,
        in_specs=[SCALAR] + [ANYWHERE] * 5,
        out_specs=[ANYWHERE] * 3,
        out_shape=[
            pltpu.HBM((w_out.shape[0] + 16, HALF), BF16),
            pltpu.HBM((2, HALF, hidden), BF16),
            pltpu.HBM((hidden, HALF), BF16),
        ],
        scratch_shapes=[
            pltpu.VMEM((w_out.shape[0] + 16, HALF), BF16),
            pltpu.VMEM((2, HALF, hidden), BF16),
            pltpu.VMEM((hidden, HALF), BF16),
            pltpu.SemaphoreType.DMA((5,)),
            pltpu.SemaphoreType.DMA((5,)),
        ],
        compiler_params=pltpu.CompilerParams(vmem_limit_bytes=SMALL),
        name="give_weights",
    )(half, *[in_hbm(a) for a in arrays])


def fetch_kernel(
    after_ref, half_ref, gate_hbm, up_hbm, down_hbm, got_in_hbm, got_down_hbm, in_ref, down_ref, sems
):
    hidden = gate_hbm.shape[2]
    columns = pl.ds(pl.multiple_of(half_ref[0] * HALF, 128), HALF)
    rows = pl.ds(pl.multiple_of(half_ref[0] * HALF, 16), HALF)
    sources = (gate_hbm.at[0, rows, :], up_hbm.at[0, rows, :], got_in_hbm.at[0], got_in_hbm.at[1])
    copies = [
        pltpu.make_async_copy(source, in_ref.at[:, pl.ds(j * hidden, hidden)], sems.at[j])
        for j, source in enumerate(sources)
    ]
    copies.append(
        pltpu.make_async_copy(down_hbm.at[0, :, columns], down_ref.at[pl.ds(0, hidden), :], sems.at[4])
    )
    copies.append(pltpu.make_async_copy(got_down_hbm, down_ref.at[pl.ds(hidden, hidden), :], sems.at[5]))
    for copy in start_all(copies):
        copy.wait()


def fetch_experts(after, half, w_gate, w_up, w_down, got_in, got_down):
    hidden = w_gate.shape[2]
    return pl.pallas_call(
        fetch_kernel,
        in_specs=[ANYWHERE, SCALAR] + [ANYWHERE] * 5,
        out_specs=[ANYWHERE] * 2,
        out_shape=[kept((HALF, 4 * hidden), BF16), kept((2 * hidden, HALF), BF16)],
        scratch_shapes=[pltpu.SemaphoreType.DMA((6,))],
        compiler_params=pltpu.CompilerParams(vmem_limit_bytes=SMALL),
        cost_estimate=pl.CostEstimate(flops=0, bytes_accessed=12 * D * hidden, transcendentals=0),
        name="fetch_experts",
    )(after, half, *[in_hbm(a) for a in (w_gate, w_up, w_down, got_in, got_down)])


def gate_up_kernel(y_ref, w_ref, own_ref, send_ref):
    width = w_ref.shape[1]
    acc = jnp.zeros((CAP, width), F32)
    stats = jnp.zeros((CAP, LANES - CHUNK), F32)
    for p in range(NXY):
        acc = acc + jnp.dot(
            y_ref[p, :, :CHUNK], w_ref[p * CHUNK : (p + 1) * CHUNK, :], preferred_element_type=F32
        )
        stats = stats + y_ref[p, :, CHUNK:].astype(F32)
    own_ref[:, :width] = acc
    send_ref[:, :width] = acc.astype(BF16)
    high = stats.astype(BF16).astype(F32)
    spare = jnp.zeros((CAP, 128 - 2 * stats.shape[1]), F32)
    own_ref[:, width:] = jnp.concatenate([stats, jnp.zeros_like(stats), spare], axis=1)
    send_ref[:, width:] = jnp.concatenate([high, stats - high, spare], axis=1).astype(BF16)


def gate_up(y, w):
    width = w.shape[1] + 128
    return pl.pallas_call(
        gate_up_kernel,
        in_specs=[WHOLE] * 2,
        out_specs=[WHOLE] * 2,
        out_shape=[kept((CAP, width), F32), kept((CAP, width), BF16)],
        compiler_params=pltpu.CompilerParams(vmem_limit_bytes=SMALL),
        name="gate_up",
    )(y, w)


def down_kernel(own_ref, got_ref, mine_ref, w_ref, out_ref):
    slices = w_ref.shape[0]
    hidden = slices // 2
    width = 2 * slices
    lanes = LANES - CHUNK
    stats = own_ref[:, width : width + lanes]
    stats = stats + got_ref[:, width : width + lanes].astype(F32)
    stats = stats + got_ref[:, width + lanes : width + 2 * lanes].astype(F32)
    square = stats[:, 16:17] + stats[:, 17:18]
    scale = lax.rsqrt(square * (1.0 / D) + 1e-6)
    affinity = jax.nn.sigmoid((stats[:, 0:8] + stats[:, 8:16]) * scale)
    own = jnp.sum(affinity * mine_ref[...], axis=1, keepdims=True)
    gates = 2.5 * own / jnp.sum(affinity, axis=1, keepdims=True)
    gates = gates.astype(BF16).astype(F32)
    acts = []
    for j in range(2):
        here, there = j * slices, (1 - j) * slices
        both = own_ref[:, here : here + slices] + got_ref[:, there : there + slices].astype(F32)
        gate = both[:, :hidden] * scale
        acts.append((gate * jax.nn.sigmoid(gate) * (both[:, hidden:] * scale)).astype(BF16))
    act = jnp.concatenate(acts, axis=1)
    for i in range(STEPS):
        acc = jnp.dot(act, w_ref[:, i * BLK : (i + 1) * BLK], preferred_element_type=F32) * gates
        for g in range(GROUP):
            pack_chunk(out_ref, i * GROUP + g, acc[:, g * CHUNK : (g + 1) * CHUNK])


def down(own, got, mine, w):
    return pl.pallas_call(
        down_kernel,
        in_specs=[WHOLE] * 4,
        out_specs=WHOLE,
        out_shape=kept((NXY, CAP * CHUNK // 128, 128), BF16),
        compiler_params=pltpu.CompilerParams(vmem_limit_bytes=SMALL),
        name="down",
    )(own, got, mine, w)


def finish_kernel(total_ref, out_ref):
    for c in range(NC):
        for p in range(NXY):
            row = sum(total_ref[z * NDEV + p * NC + c].astype(F32) for z in range(NZ))
            at = (c * NXY + p) * CHUNK
            out_ref[:, at : at + CHUNK] = row.astype(BF16)


def finish(total):
    return pl.pallas_call(
        finish_kernel,
        in_specs=[WHOLE],
        out_specs=WHOLE,
        out_shape=jax.ShapeDtypeStruct((total.shape[1], D), BF16),
        compiler_params=pltpu.CompilerParams(vmem_limit_bytes=SMALL),
        name="finish",
    )(total)


def swap_cores(values):
    return lax.ppermute(values, "c", [(0, 1), (1, 0)])


def per_device(
    prompt_cache,
    assignment,
    resident_cache,
    resident_len,
    queries,
    new_latent,
    residual,
    w_uv,
    w_out,
    norm_gain,
    w_router,
    expert_ids,
    w_gate,
    w_up,
    w_down,
):
    plane = lax.axis_index("z")
    core = lax.axis_index("c")
    place_xy = lax.axis_index("x") * NY + lax.axis_index("y")
    rows_dev = queries.shape[0]
    own_half = jnp.reshape(core, (1,)).astype(jnp.int32)
    other_half = 1 - own_half
    plane_index = jnp.reshape(plane, (1,)).astype(jnp.int32)
    chunk = core * NXY + place_xy

    received = lax.all_to_all(spread(assignment, prompt_cache), ("x", "y", "c"), 0, 0, tiled=True)

    ids_plane = expert_ids - plane * EXP_G
    named = jnp.any(expert_ids[:, :, None] == jnp.arange(NZ * EXP_G, dtype=jnp.int32)[None, None, :], axis=1)
    lower = (jnp.arange(ALL_ROWS)[:, None] > jnp.arange(ALL_ROWS)[None, :]).astype(BF16)
    ranks = jnp.dot(lower, named.astype(BF16), preferred_element_type=F32).astype(jnp.int32)
    ranks = jnp.where(named, ranks, -1)
    plane_ranks = lax.dynamic_slice_in_dim(ranks, plane * EXP_G, EXP_G, 1)
    own_expert = place_xy // 2
    slot_iota = jnp.arange(CAP, dtype=jnp.int32)
    own_ranks = lax.dynamic_index_in_dim(plane_ranks, own_expert, 1, keepdims=False)
    own_slots = (own_ranks[None, :] == slot_iota[:, None]).astype(BF16)
    slot_ids = jnp.dot(own_slots, ids_plane.astype(BF16), preferred_element_type=F32)
    mine = (slot_ids == own_expert.astype(F32)).astype(F32)
    group_ids = lax.dynamic_slice_in_dim(expert_ids, plane * ROWS, ROWS, 0)
    by_group = plane_ranks.reshape(NZ, ROWS, EXP_G)
    step_order = (plane - jnp.arange(NZ, dtype=jnp.int32)) % NZ
    step_ranks = by_group.at[step_order].get(mode="promise_in_bounds").reshape(ALL_ROWS, EXP_G).T
    owner_ranks = plane_ranks.reshape(NZ * NDEV, rows_dev, EXP_G).transpose(1, 0, 2).reshape(ALL_ROWS, EXP_G)
    gain_chunk = lax.dynamic_slice_in_dim(norm_gain, chunk * CHUNK, CHUNK, 0).astype(F32)[None, :]
    router_chunk = lax.dynamic_slice_in_dim(w_router, chunk * CHUNK, CHUNK, 0)
    row_iota = jnp.arange(ROWS, dtype=jnp.int32)
    pair = jnp.arange(2, dtype=jnp.int32)
    first_rows = (place_xy * NC + core + pair * (1 - 2 * core)) * rows_dev
    place = row_iota[None, :, None] == (first_rows[:, None] + jnp.arange(16, dtype=jnp.int32)[None, :])[:, None, :]
    place = (place & (jnp.arange(16) < rows_dev)[None, None, :]).astype(BF16)
    res = jnp.pad(residual, ((0, 16 - rows_dev), (0, 0)))

    given = give_weights(other_half, w_out, res, w_gate, w_up, w_down)
    got_out, got_in, got_down = [swap_cores(a) for a in given]

    cache_iota = jnp.arange(resident_cache.shape[1], dtype=jnp.int32)
    old_masks = cache_iota[None, :] < resident_len[0][:, None]
    context_old = jax.vmap(attend)(queries[1:], resident_cache, old_masks, new_latent[1:])
    context_old = context_old.reshape(rows_dev - 1, NDEV, -1, LAT).transpose(1, 0, 2, 3)
    context_old = jnp.pad(context_old, ((0, 0), (1, 0), (0, 0), (0, 0))).reshape(-1, LAT)
    held = (
        received, context_old, queries[0].T, step_ranks, owner_ranks, mine, group_ids, gain_chunk,
        router_chunk, place, res, own_half, plane_index, got_out, got_in, got_down,
    )
    (
        received, context_old, first_query, step_ranks, owner_ranks, mine, group_ids, gain_chunk,
        router_chunk, place, res, own_half, plane_index, got_out, got_in, got_down,
    ) = lax.optimization_barrier(held)
    context, w_uv, w_out = prompt_attention(
        own_half, first_query, received, new_latent, context_old, w_uv, w_out, res, got_out
    )

    context = lax.all_to_all(context.reshape(NDEV, -1, LAT), ("x", "y", "c"), 0, 0, tiled=True)
    context = context.reshape(-1, LAT)

    attn = head_values(context, w_uv)
    partial = project(attn, swap_cores(attn), place, w_out)
    partial = lax.all_to_all(partial, ("x", "y"), 0, 0, tiled=True)

    packed, hidden = pack_rows(partial, gain_chunk, router_chunk, group_ids, rows_dev)

    groups = [packed]
    for k in range(1, NZ):
        groups.append(lax.ppermute(packed, "z", [(i, (i + k) % NZ) for i in range(NZ)]))
    w_in, w_down = fetch_experts(packed, own_half, w_gate, w_up, w_down, got_in, got_down)
    slotted = slot_rows(w_down, step_ranks, groups)
    slotted = lax.all_to_all(slotted, ("x", "y"), 0, 0, tiled=True)

    sums, to_send = gate_up(slotted, w_in)
    out = down(sums, swap_cores(to_send), mine, w_down)
    out = lax.all_to_all(out, ("x", "y"), 0, 0, tiled=True)

    total = combine_rows(plane_index, out, owner_ranks, hidden, rows_dev)
    total = lax.all_to_all(total, ("z", "x", "y", "c"), 0, 0, tiled=True)
    return finish(total)


def solution(mesh):
    grid = Mesh(mesh.devices.reshape(NZ, NX, NY, NC), ("z", "x", "y", "c"))
    dev = ("x", "y", "c")
    every = ("z", "x", "y", "c")
    return jax.shard_map(
        per_device,
        mesh=grid,
        in_specs=(
            P("z", dev, None),
            P("z", None),
            P(every, None, None),
            P(every, None),
            P(every, None, None),
            P(every, None),
            P(every, None),
            P(dev, None, None),
            P(dev, None),
            P(),
            P(),
            P(),
            P(every, None, None),
            P(every, None, None),
            P(every, None, None),
        ),
        out_specs=P(every, None),
        check_vma=False,
    )
```

```python
import functools

import jax
import jax.numpy as jnp
from jax import lax
from jax.experimental import pallas as pl
from jax.experimental.pallas import tpu as pltpu
from jax.sharding import Mesh, PartitionSpec as P

LAT = 512
ROPE = 64
NOPE = 128
D = 7168
CAP = 192
NZ, NX, NY, NC = 4, 4, 4, 2
NXY = NX * NY
NDEV = NXY * NC
EXP_G = 8
CHUNK = D // NDEV
HALF = D // 2
PARTS = 4
LANES = 256
GROUP = 4
BLK = CHUNK * GROUP
STEPS = NXY // GROUP
ROWS = 128
ALL_ROWS = ROWS * NZ
F32 = jnp.float32
BF16 = jnp.bfloat16
SMALL = 16 * 1024 * 1024
LARGE = 20 * 1024 * 1024


def kept(shape, dtype):
    return pltpu.VMEM(shape, dtype)


def in_hbm(array):
    return pltpu.with_memory_space_constraint(array, pltpu.HBM)


def start_all(copies):
    for copy in copies:
        copy.start()
    return copies


WHOLE = pl.BlockSpec(memory_space=pltpu.VMEM)
SCALAR = pl.BlockSpec(memory_space=pltpu.SMEM)
ANYWHERE = pl.BlockSpec(memory_space=pl.ANY)


def attend(query_row, cache_block, valid_mask, own_entry):
    scale_factor = (NOPE + ROPE) ** (-0.5)
    scores = jnp.einsum("hc,kc->hk", query_row, cache_block, preferred_element_type=F32) * scale_factor
    if valid_mask is not None:
        scores = jnp.where(valid_mask[None, :], scores, -jnp.inf)
    own_score = jnp.einsum("hc,c->h", query_row, own_entry, preferred_element_type=F32) * scale_factor
    maximum = jnp.maximum(jnp.max(scores, axis=1), own_score)
    exponent = jnp.exp(scores - maximum[:, None])
    own_exponent = jnp.exp(own_score - maximum)
    totals = jnp.sum(exponent, axis=1) + own_exponent
    weights = (exponent / totals[:, None]).astype(BF16)
    own_weight = (own_exponent / totals).astype(BF16)
    context = jnp.einsum("hk,kl->hl", weights, cache_block[:, :LAT], preferred_element_type=F32)
    context = context + own_weight.astype(F32)[:, None] * own_entry[:LAT].astype(F32)[None, :]
    return context.astype(BF16)


def pack_chunk(ref, at, part):
    rows, most = part.shape[0], part.shape[0] * 3 // 4
    rest = part[:, 128:]
    ref[at, :rows, :] = part[:, :128].astype(ref.dtype)
    ref[at, rows:, :96] = rest[:most].astype(ref.dtype)
    tail = jnp.concatenate([rest[most:, 32 * i : 32 * (i + 1)] for i in range(3)], axis=0)
    ref[at, rows:, 96:] = tail.astype(ref.dtype)


def unpack_chunk(packed):
    rows = packed.shape[0] * 4 // 7
    most, few = rows * 3 // 4, rows // 4
    rest = packed[rows:, :96]
    tail = [packed[rows + few * i : rows + few * (i + 1), 96:] for i in range(3)]
    rest = jnp.concatenate([rest, jnp.concatenate(tail, axis=1)], axis=0)
    return jnp.concatenate([packed[:rows], rest], axis=1)


def spread_kernel(owners_hbm, cache_ref, out_ref, owners_ref, held_ref, packed_ref, owner_sem, in_sem, out_sem):
    owners_copy = pltpu.make_async_copy(owners_hbm, owners_ref, owner_sem)
    owners_copy.start()
    batch = NDEV // in_sem.shape[0]
    tokens, half = cache_ref.shape[1], cache_ref.shape[1] // 2
    arrive = []
    for b in range(in_sem.shape[0]):
        at = pl.ds(b * batch, batch)
        arrive.append(pltpu.make_async_copy(cache_ref.at[at], held_ref.at[at], in_sem.at[b]))
    start_all(arrive)
    owners_copy.wait()
    leave = [
        pltpu.make_async_copy(packed_ref.at[p], out_ref.at[owners_ref[0, p]], out_sem.at[p])
        for p in range(NDEV)
    ]
    for p in range(NDEV):
        if p % batch == 0:
            arrive[p // batch].wait()
        for j in range(LAT // 128):
            packed_ref[p, j * tokens : (j + 1) * tokens, :] = held_ref[p, :, j * 128 : (j + 1) * 128]
        tail = jnp.concatenate([held_ref[p, :half, LAT:], held_ref[p, half:, LAT:]], axis=1)
        packed_ref[p, LAT // 128 * tokens :, :] = tail
        leave[p].start()
    for p in range(NDEV):
        leave[p].wait()


def spread(owners, cache):
    packed = (NDEV, cache.shape[1] * cache.shape[2] // 128, 128)
    return pl.pallas_call(
        spread_kernel,
        in_specs=[ANYWHERE, ANYWHERE],
        out_specs=ANYWHERE,
        scratch_shapes=[
            pltpu.SMEM(owners.shape, owners.dtype),
            pltpu.VMEM(cache.shape, cache.dtype),
            pltpu.VMEM(packed, cache.dtype),
            pltpu.SemaphoreType.DMA,
            pltpu.SemaphoreType.DMA((8,)),
            pltpu.SemaphoreType.DMA((NDEV,)),
        ],
        out_shape=pltpu.HBM(packed, cache.dtype),
        compiler_params=pltpu.CompilerParams(vmem_limit_bytes=SMALL),
        name="spread",
    )(in_hbm(owners), in_hbm(cache))


def prompt_kernel(
    half_ref, query_hbm, cache_ref, entry_ref, old_hbm, uv_hbm, w_hbm, res_hbm, got_hbm,
    out_ref, uv_ref, w_ref, old_ref, query_ref, sems,
):
    heads_all = query_hbm.shape[1]
    query_copy = pltpu.make_async_copy(query_hbm, query_ref, sems.at[0])
    old_copy = pltpu.make_async_copy(old_hbm, old_ref, sems.at[1])
    uv_copy = pltpu.make_async_copy(uv_hbm, uv_ref, sems.at[2])
    depth = w_hbm.shape[0]
    at = pl.ds(pl.multiple_of(half_ref[0] * HALF, 128), HALF)
    w_copies = [pltpu.make_async_copy(res_hbm.at[:, at], w_ref.at[pl.ds(depth, 16), :], sems.at[3])]
    span = depth // PARTS
    for n in range(PARTS):
        rows = pl.ds(n * span, span)
        w_copies.append(pltpu.make_async_copy(w_hbm.at[rows, at], w_ref.at[rows, :], sems.at[4 + n]))
        span_got = span + 16 if n == PARTS - 1 else span
        w_copies.append(
            pltpu.make_async_copy(
                got_hbm.at[pl.ds(n * span, span_got), :],
                w_ref.at[pl.ds(depth + 16 + n * span, span_got), :],
                sems.at[4 + PARTS + n],
            )
        )
    start_all([query_copy, old_copy, uv_copy] + w_copies)
    scale_factor = (NOPE + ROPE) ** (-0.5)
    sources, tokens = cache_ref.shape[0], cache_ref.shape[1] * 128 // query_ref.shape[0]
    tiles = [cache_ref[:, j * tokens : (j + 1) * tokens, :].reshape(-1, 128) for j in range(LAT // 128)]
    cache = jnp.concatenate(tiles, axis=1)
    rope = cache_ref[:, LAT // 128 * tokens :, :].reshape(-1, 128)
    entry = entry_ref[:1, :]
    query_copy.wait()
    query = query_ref[...]
    tail = query[LAT:, :]
    blank = jnp.zeros_like(tail)
    tail = jnp.concatenate(
        [jnp.concatenate([tail, blank], axis=0), jnp.concatenate([blank, tail], axis=0)], axis=1
    )
    extra = jnp.dot(rope, tail, preferred_element_type=F32)
    extra = [extra[:, h * heads_all : (h + 1) * heads_all].reshape(sources, -1, heads_all) for h in range(2)]
    scores = jnp.dot(cache, query[:LAT, :], preferred_element_type=F32)
    scores = (scores + jnp.concatenate(extra, axis=1).reshape(scores.shape)) * scale_factor
    own_score = jnp.dot(entry, query, preferred_element_type=F32) * scale_factor
    maximum = jnp.maximum(jnp.max(scores, axis=0, keepdims=True), own_score)
    exponent = jnp.exp(scores - maximum)
    own_exponent = jnp.exp(own_score - maximum)
    totals = jnp.sum(exponent, axis=0, keepdims=True) + own_exponent
    inverse = 1.0 / totals
    weights = (exponent * inverse).astype(BF16)
    own_weight = (own_exponent * inverse).astype(BF16)
    over_rows = (((0,), (0,)), ((), ()))
    context = lax.dot_general(weights, cache, over_rows, preferred_element_type=F32)
    context = context + lax.dot_general(own_weight, entry[:, :LAT], over_rows, preferred_element_type=F32)
    rows, block = out_ref.shape[0], out_ref.shape[0] // NDEV
    heads = heads_all // NDEV
    to = lax.broadcasted_iota(jnp.int32, (rows, heads_all), 0)
    source = jnp.where(to % block < heads, to // block * heads + to % block, -1)
    order = (lax.broadcasted_iota(jnp.int32, (rows, heads_all), 1) == source).astype(BF16)
    placed = jnp.dot(order, context.astype(BF16), preferred_element_type=F32)
    old_copy.wait()
    out_ref[...] = (placed + old_ref[...].astype(F32)).astype(BF16)
    uv_copy.wait()
    for copy in w_copies:
        copy.wait()


def prompt_attention(half, query, cache, entry, old, w_uv, w_out, res, got):
    rows = old.shape[0]
    return pl.pallas_call(
        prompt_kernel,
        in_specs=[SCALAR, ANYWHERE, WHOLE, WHOLE] + [ANYWHERE] * 5,
        out_specs=[WHOLE, ANYWHERE, ANYWHERE],
        out_shape=[
            kept((rows, LAT), BF16), kept(w_uv.shape, BF16), kept((2 * got.shape[0], HALF), BF16),
        ],
        scratch_shapes=[
            pltpu.VMEM((rows, LAT), BF16),
            pltpu.VMEM(query.shape, BF16),
            pltpu.SemaphoreType.DMA((4 + 2 * PARTS,)),
        ],
        compiler_params=pltpu.CompilerParams(vmem_limit_bytes=LARGE),
        name="prompt_attention",
    )(half, in_hbm(query), cache, entry, *[in_hbm(a) for a in (old, w_uv, w_out, res, got)])


def values_kernel(context_ref, uv_ref, attn_ref):
    heads, rows = uv_ref.shape[0], context_ref.shape[0]
    context = context_ref[...]
    pick = lax.broadcasted_iota(jnp.int32, (ROWS, rows), 1) // heads
    pick = (pick == lax.broadcasted_iota(jnp.int32, (ROWS, rows), 0)).astype(BF16)
    width = uv_ref.shape[2]
    row_head = lax.broadcasted_iota(jnp.int32, (rows, 2 * width), 0) % heads
    lane_head = lax.broadcasted_iota(jnp.int32, (rows, 2 * width), 1) // width
    for h in range(0, heads, 2):
        values = jnp.concatenate([uv_ref[h], uv_ref[h + 1]], axis=1)
        values = jnp.dot(context, values, preferred_element_type=F32)
        values = jnp.where(row_head == lane_head + h, values, 0.0).astype(BF16)
        values = jnp.dot(pick, values, preferred_element_type=F32).astype(BF16)
        attn_ref[:, h * width : (h + 2) * width] = values


def head_values(context, w_uv):
    return pl.pallas_call(
        values_kernel,
        in_specs=[WHOLE, WHOLE],
        out_specs=WHOLE,
        out_shape=kept((ROWS, w_uv.shape[0] * w_uv.shape[2]), BF16),
        compiler_params=pltpu.CompilerParams(vmem_limit_bytes=SMALL),
        name="head_values",
    )(context, w_uv)


def project_kernel(own_ref, got_ref, place_ref, w_ref, out_ref):
    depth = own_ref.shape[1]
    lhs = (own_ref[...], place_ref[0], got_ref[...], place_ref[1])
    for i in range(STEPS):
        at, acc = 0, jnp.zeros((ROWS, BLK), F32)
        for left in lhs:
            acc = acc + jnp.dot(
                left, w_ref[at : at + left.shape[1], i * BLK : (i + 1) * BLK], preferred_element_type=F32
            )
            at += left.shape[1]
        for g in range(GROUP):
            pack_chunk(out_ref, i * GROUP + g, acc[:, g * CHUNK : (g + 1) * CHUNK])


def project(own, got, place, w_out):
    return pl.pallas_call(
        project_kernel,
        in_specs=[WHOLE] * 4,
        out_specs=WHOLE,
        out_shape=kept((NXY, ROWS * CHUNK // 128, 128), BF16),
        compiler_params=pltpu.CompilerParams(vmem_limit_bytes=SMALL),
        name="project",
    )(own, got, place, w_out)


def rows_kernel(rows_dev, part_ref, gain_ref, router_ref, ids_ref, packed_ref, hidden_ref):
    total = part_ref[0].astype(F32)
    for source in range(1, part_ref.shape[0]):
        total = total + part_ref[source].astype(F32)
    total = unpack_chunk(total.astype(BF16))
    to = lax.broadcasted_iota(jnp.int32, (ROWS, ROWS), 0)
    order = to % (ROWS // rows_dev) * rows_dev + to // (ROWS // rows_dev)
    order = (lax.broadcasted_iota(jnp.int32, (ROWS, ROWS), 1) == order).astype(BF16)
    hidden_ref[...] = jnp.dot(order, total, preferred_element_type=F32)
    hidden = total.astype(F32)
    square = jnp.sum(hidden * hidden, axis=1, keepdims=True)
    scaled = (hidden * gain_ref[...]).astype(BF16)
    logits = jnp.dot(scaled, router_ref[...], preferred_element_type=F32)
    expert = lax.broadcasted_iota(jnp.int32, logits.shape, 1)
    lane = lax.broadcasted_iota(jnp.int32, (ROWS, LANES - CHUNK), 1)
    top = ids_ref.shape[1]
    spare = jnp.zeros((ROWS, LANES - CHUNK), F32)
    for k in range(top + 1):
        value = square
        if k < top:
            value = jnp.sum(jnp.where(expert == ids_ref[:, k : k + 1], logits, 0.0), axis=1, keepdims=True)
        high = value.astype(BF16).astype(F32)
        at_high, at_low = (k, top + k) if k < top else (2 * top, 2 * top + 1)
        spare = jnp.where(lane == at_high, high, jnp.where(lane == at_low, value - high, spare))
    packed_ref[:, :CHUNK] = scaled
    packed_ref[:, CHUNK:] = spare.astype(BF16)


def pack_rows(part, gain, router, ids, rows_dev):
    return pl.pallas_call(
        functools.partial(rows_kernel, rows_dev),
        out_shape=[kept((ROWS, LANES), BF16), kept((ROWS, CHUNK), F32)],
        compiler_params=pltpu.CompilerParams(vmem_limit_bytes=SMALL),
        name="pack_rows",
    )(part, gain, router, ids)


def slot_kernel(after_ref, ranks_ref, *refs):
    packed_refs, out_ref, rows_ref = refs[:NZ], refs[NZ], refs[NZ + 1]
    for k in range(NZ):
        rows_ref[k * ROWS : (k + 1) * ROWS, :] = packed_refs[k][...]
    slot = lax.broadcasted_iota(jnp.int32, (CAP, ALL_ROWS), 0)
    for e in range(EXP_G):
        table = (ranks_ref[e : e + 1, :] == slot).astype(BF16)
        slotted = jnp.dot(table, rows_ref[...], preferred_element_type=F32).astype(BF16)
        out_ref[2 * e] = slotted
        out_ref[2 * e + 1] = slotted


def slot_rows(after, ranks, packed):
    return pl.pallas_call(
        slot_kernel,
        in_specs=[ANYWHERE] + [WHOLE] * (1 + NZ),
        out_specs=WHOLE,
        out_shape=kept((NXY, CAP, LANES), BF16),
        scratch_shapes=[pltpu.VMEM((ALL_ROWS, LANES), BF16)],
        compiler_params=pltpu.CompilerParams(vmem_limit_bytes=SMALL),
        name="slot_rows",
    )(after, ranks, *packed)


def combine_kernel(plane_ref, out_ref, ranks_ref, hidden_ref, rows_ref, acc_ref):
    slot = lax.broadcasted_iota(jnp.int32, (ALL_ROWS, CAP), 1)
    acc = jnp.zeros((ALL_ROWS, CHUNK), F32)
    for e in range(EXP_G):
        table = (ranks_ref[:, e : e + 1] == slot).astype(BF16)
        both = out_ref[2 * e].astype(F32) + out_ref[2 * e + 1].astype(F32)
        acc = acc + jnp.dot(table, unpack_chunk(both.astype(BF16)), preferred_element_type=F32)
    acc_ref[...] = acc
    span, count = rows_ref.shape[0], rows_ref.shape[1]
    own = ROWS // count
    for r in range(count):
        at = pl.multiple_of(r * span + plane_ref[0] * own, 8)
        acc_ref[pl.ds(at, own), :] += hidden_ref[r * own : (r + 1) * own, :]
    for r in range(count):
        rows_ref[:, r, :] = acc_ref[r * span : (r + 1) * span, :].astype(BF16)


def combine_rows(plane, out, ranks, hidden, count):
    vmem = pl.BlockSpec(memory_space=pltpu.VMEM)
    return pl.pallas_call(
        combine_kernel,
        in_specs=[pl.BlockSpec(memory_space=pltpu.SMEM), vmem, vmem, vmem],
        out_specs=vmem,
        out_shape=kept((ALL_ROWS // count, count, CHUNK), BF16),
        scratch_shapes=[pltpu.VMEM((ALL_ROWS, CHUNK), F32)],
        compiler_params=pltpu.CompilerParams(vmem_limit_bytes=SMALL),
        name="combine_rows",
    )(plane, out, ranks, hidden)


def give_kernel(
    half_ref, out_hbm, res_hbm, gate_hbm, up_hbm, down_hbm, to_out, to_in, to_down,
    out_ref, in_ref, down_ref, in_sems, out_sems,
):
    depth = out_hbm.shape[0]
    columns = pl.ds(pl.multiple_of(half_ref[0] * HALF, 128), HALF)
    rows = pl.ds(pl.multiple_of(half_ref[0] * HALF, 16), HALF)
    sources = (
        (out_hbm.at[:, columns], out_ref.at[pl.ds(0, depth), :], to_out.at[pl.ds(0, depth), :]),
        (res_hbm.at[:, columns], out_ref.at[pl.ds(depth, 16), :], to_out.at[pl.ds(depth, 16), :]),
        (gate_hbm.at[0, rows, :], in_ref.at[0], to_in.at[0]),
        (up_hbm.at[0, rows, :], in_ref.at[1], to_in.at[1]),
        (down_hbm.at[0, :, columns], down_ref, to_down),
    )
    arrive = [pltpu.make_async_copy(a, b, in_sems.at[n]) for n, (a, b, _) in enumerate(sources)]
    leave = [pltpu.make_async_copy(b, c, out_sems.at[n]) for n, (_, b, c) in enumerate(sources)]
    start_all(arrive)
    for first, second in zip(arrive, leave):
        first.wait()
        second.start()
    for copy in leave:
        copy.wait()


def give_weights(half, w_out, res, w_gate, w_up, w_down):
    hidden = w_gate.shape[2]
    arrays = (w_out, res, w_gate, w_up, w_down)
    return pl.pallas_call(
        give_kernel,
        in_specs=[SCALAR] + [ANYWHERE] * 5,
        out_specs=[ANYWHERE] * 3,
        out_shape=[
            pltpu.HBM((w_out.shape[0] + 16, HALF), BF16),
            pltpu.HBM((2, HALF, hidden), BF16),
            pltpu.HBM((hidden, HALF), BF16),
        ],
        scratch_shapes=[
            pltpu.VMEM((w_out.shape[0] + 16, HALF), BF16),
            pltpu.VMEM((2, HALF, hidden), BF16),
            pltpu.VMEM((hidden, HALF), BF16),
            pltpu.SemaphoreType.DMA((5,)),
            pltpu.SemaphoreType.DMA((5,)),
        ],
        compiler_params=pltpu.CompilerParams(vmem_limit_bytes=SMALL),
        name="give_weights",
    )(half, *[in_hbm(a) for a in arrays])


def fetch_kernel(
    after_ref, half_ref, gate_hbm, up_hbm, down_hbm, got_in_hbm, got_down_hbm, in_ref, down_ref, sems
):
    hidden = gate_hbm.shape[2]
    columns = pl.ds(pl.multiple_of(half_ref[0] * HALF, 128), HALF)
    rows = pl.ds(pl.multiple_of(half_ref[0] * HALF, 16), HALF)
    sources = (gate_hbm.at[0, rows, :], up_hbm.at[0, rows, :], got_in_hbm.at[0], got_in_hbm.at[1])
    copies = [
        pltpu.make_async_copy(source, in_ref.at[:, pl.ds(j * hidden, hidden)], sems.at[j])
        for j, source in enumerate(sources)
    ]
    copies.append(
        pltpu.make_async_copy(down_hbm.at[0, :, columns], down_ref.at[pl.ds(0, hidden), :], sems.at[4])
    )
    copies.append(pltpu.make_async_copy(got_down_hbm, down_ref.at[pl.ds(hidden, hidden), :], sems.at[5]))
    for copy in start_all(copies):
        copy.wait()


def fetch_experts(after, half, w_gate, w_up, w_down, got_in, got_down):
    hidden = w_gate.shape[2]
    return pl.pallas_call(
        fetch_kernel,
        in_specs=[ANYWHERE, SCALAR] + [ANYWHERE] * 5,
        out_specs=[ANYWHERE] * 2,
        out_shape=[kept((HALF, 4 * hidden), BF16), kept((2 * hidden, HALF), BF16)],
        scratch_shapes=[pltpu.SemaphoreType.DMA((6,))],
        compiler_params=pltpu.CompilerParams(vmem_limit_bytes=SMALL),
        cost_estimate=pl.CostEstimate(flops=0, bytes_accessed=12 * D * hidden, transcendentals=0),
        name="fetch_experts",
    )(after, half, *[in_hbm(a) for a in (w_gate, w_up, w_down, got_in, got_down)])


def gate_up_kernel(y_ref, w_ref, own_ref, send_ref):
    width = w_ref.shape[1]
    acc = jnp.zeros((CAP, width), F32)
    stats = jnp.zeros((CAP, LANES - CHUNK), F32)
    for p in range(NXY):
        acc = acc + jnp.dot(
            y_ref[p, :, :CHUNK], w_ref[p * CHUNK : (p + 1) * CHUNK, :], preferred_element_type=F32
        )
        stats = stats + y_ref[p, :, CHUNK:].astype(F32)
    own_ref[:, :width] = acc
    send_ref[:, :width] = acc.astype(BF16)
    high = stats.astype(BF16).astype(F32)
    spare = jnp.zeros((CAP, 128 - 2 * stats.shape[1]), F32)
    own_ref[:, width:] = jnp.concatenate([stats, jnp.zeros_like(stats), spare], axis=1)
    send_ref[:, width:] = jnp.concatenate([high, stats - high, spare], axis=1).astype(BF16)


def gate_up(y, w):
    width = w.shape[1] + 128
    return pl.pallas_call(
        gate_up_kernel,
        in_specs=[WHOLE] * 2,
        out_specs=[WHOLE] * 2,
        out_shape=[kept((CAP, width), F32), kept((CAP, width), BF16)],
        compiler_params=pltpu.CompilerParams(vmem_limit_bytes=SMALL),
        name="gate_up",
    )(y, w)


def down_kernel(own_ref, got_ref, mine_ref, w_ref, out_ref):
    slices = w_ref.shape[0]
    hidden = slices // 2
    width = 2 * slices
    lanes = LANES - CHUNK
    stats = own_ref[:, width : width + lanes]
    stats = stats + got_ref[:, width : width + lanes].astype(F32)
    stats = stats + got_ref[:, width + lanes : width + 2 * lanes].astype(F32)
    square = stats[:, 16:17] + stats[:, 17:18]
    scale = lax.rsqrt(square * (1.0 / D) + 1e-6)
    affinity = jax.nn.sigmoid((stats[:, 0:8] + stats[:, 8:16]) * scale)
    own = jnp.sum(affinity * mine_ref[...], axis=1, keepdims=True)
    gates = 2.5 * own / jnp.sum(affinity, axis=1, keepdims=True)
    gates = gates.astype(BF16).astype(F32)
    acts = []
    for j in range(2):
        here, there = j * slices, (1 - j) * slices
        both = own_ref[:, here : here + slices] + got_ref[:, there : there + slices].astype(F32)
        gate = both[:, :hidden] * scale
        acts.append((gate * jax.nn.sigmoid(gate) * (both[:, hidden:] * scale)).astype(BF16))
    act = jnp.concatenate(acts, axis=1)
    for i in range(STEPS):
        acc = jnp.dot(act, w_ref[:, i * BLK : (i + 1) * BLK], preferred_element_type=F32) * gates
        for g in range(GROUP):
            pack_chunk(out_ref, i * GROUP + g, acc[:, g * CHUNK : (g + 1) * CHUNK])


def down(own, got, mine, w):
    return pl.pallas_call(
        down_kernel,
        in_specs=[WHOLE] * 4,
        out_specs=WHOLE,
        out_shape=kept((NXY, CAP * CHUNK // 128, 128), BF16),
        compiler_params=pltpu.CompilerParams(vmem_limit_bytes=SMALL),
        name="down",
    )(own, got, mine, w)


def finish_kernel(total_ref, out_ref):
    for c in range(NC):
        for p in range(NXY):
            row = sum(total_ref[z * NDEV + p * NC + c].astype(F32) for z in range(NZ))
            at = (c * NXY + p) * CHUNK
            out_ref[:, at : at + CHUNK] = row.astype(BF16)


def finish(total):
    return pl.pallas_call(
        finish_kernel,
        in_specs=[WHOLE],
        out_specs=WHOLE,
        out_shape=jax.ShapeDtypeStruct((total.shape[1], D), BF16),
        compiler_params=pltpu.CompilerParams(vmem_limit_bytes=SMALL),
        name="finish",
    )(total)


def swap_cores(values):
    return lax.ppermute(values, "c", [(0, 1), (1, 0)])


def per_device(
    prompt_cache,
    assignment,
    resident_cache,
    resident_len,
    queries,
    new_latent,
    residual,
    w_uv,
    w_out,
    norm_gain,
    w_router,
    expert_ids,
    w_gate,
    w_up,
    w_down,
):
    plane = lax.axis_index("z")
    core = lax.axis_index("c")
    place_xy = lax.axis_index("x") * NY + lax.axis_index("y")
    rows_dev = queries.shape[0]
    own_half = jnp.reshape(core, (1,)).astype(jnp.int32)
    other_half = 1 - own_half
    plane_index = jnp.reshape(plane, (1,)).astype(jnp.int32)
    chunk = core * NXY + place_xy

    received = lax.all_to_all(spread(assignment, prompt_cache), ("x", "y", "c"), 0, 0, tiled=True)

    ids_plane = expert_ids - plane * EXP_G
    named = jnp.any(expert_ids[:, :, None] == jnp.arange(NZ * EXP_G, dtype=jnp.int32)[None, None, :], axis=1)
    lower = (jnp.arange(ALL_ROWS)[:, None] > jnp.arange(ALL_ROWS)[None, :]).astype(BF16)
    ranks = jnp.dot(lower, named.astype(BF16), preferred_element_type=F32).astype(jnp.int32)
    ranks = jnp.where(named, ranks, -1)
    plane_ranks = lax.dynamic_slice_in_dim(ranks, plane * EXP_G, EXP_G, 1)
    own_expert = place_xy // 2
    slot_iota = jnp.arange(CAP, dtype=jnp.int32)
    own_ranks = lax.dynamic_index_in_dim(plane_ranks, own_expert, 1, keepdims=False)
    own_slots = (own_ranks[None, :] == slot_iota[:, None]).astype(BF16)
    slot_ids = jnp.dot(own_slots, ids_plane.astype(BF16), preferred_element_type=F32)
    mine = (slot_ids == own_expert.astype(F32)).astype(F32)
    group_ids = lax.dynamic_slice_in_dim(expert_ids, plane * ROWS, ROWS, 0)
    by_group = plane_ranks.reshape(NZ, ROWS, EXP_G)
    step_order = (plane - jnp.arange(NZ, dtype=jnp.int32)) % NZ
    step_ranks = by_group.at[step_order].get(mode="promise_in_bounds").reshape(ALL_ROWS, EXP_G).T
    owner_ranks = plane_ranks.reshape(NZ * NDEV, rows_dev, EXP_G).transpose(1, 0, 2).reshape(ALL_ROWS, EXP_G)
    gain_chunk = lax.dynamic_slice_in_dim(norm_gain, chunk * CHUNK, CHUNK, 0).astype(F32)[None, :]
    router_chunk = lax.dynamic_slice_in_dim(w_router, chunk * CHUNK, CHUNK, 0)
    row_iota = jnp.arange(ROWS, dtype=jnp.int32)
    pair = jnp.arange(2, dtype=jnp.int32)
    first_rows = (place_xy * NC + core + pair * (1 - 2 * core)) * rows_dev
    place = row_iota[None, :, None] == (first_rows[:, None] + jnp.arange(16, dtype=jnp.int32)[None, :])[:, None, :]
    place = (place & (jnp.arange(16) < rows_dev)[None, None, :]).astype(BF16)
    res = jnp.pad(residual, ((0, 16 - rows_dev), (0, 0)))

    given = give_weights(other_half, w_out, res, w_gate, w_up, w_down)
    got_out, got_in, got_down = [swap_cores(a) for a in given]

    cache_iota = jnp.arange(resident_cache.shape[1], dtype=jnp.int32)
    old_masks = cache_iota[None, :] < resident_len[0][:, None]
    context_old = jax.vmap(attend)(queries[1:], resident_cache, old_masks, new_latent[1:])
    context_old = context_old.reshape(rows_dev - 1, NDEV, -1, LAT).transpose(1, 0, 2, 3)
    context_old = jnp.pad(context_old, ((0, 0), (1, 0), (0, 0), (0, 0))).reshape(-1, LAT)
    held = (
        received, context_old, queries[0].T, step_ranks, owner_ranks, mine, group_ids, gain_chunk,
        router_chunk, place, res, own_half, plane_index, got_out, got_in, got_down,
    )
    (
        received, context_old, first_query, step_ranks, owner_ranks, mine, group_ids, gain_chunk,
        router_chunk, place, res, own_half, plane_index, got_out, got_in, got_down,
    ) = lax.optimization_barrier(held)
    context, w_uv, w_out = prompt_attention(
        own_half, first_query, received, new_latent, context_old, w_uv, w_out, res, got_out
    )

    context = lax.all_to_all(context.reshape(NDEV, -1, LAT), ("x", "y", "c"), 0, 0, tiled=True)
    context = context.reshape(-1, LAT)

    attn = head_values(context, w_uv)
    partial = project(attn, swap_cores(attn), place, w_out)
    partial = lax.all_to_all(partial, ("x", "y"), 0, 0, tiled=True)

    packed, hidden = pack_rows(partial, gain_chunk, router_chunk, group_ids, rows_dev)

    groups = [packed]
    for k in range(1, NZ):
        groups.append(lax.ppermute(packed, "z", [(i, (i + k) % NZ) for i in range(NZ)]))
    w_in, w_down = fetch_experts(packed, own_half, w_gate, w_up, w_down, got_in, got_down)
    slotted = slot_rows(w_down, step_ranks, groups)
    slotted = lax.all_to_all(slotted, ("x", "y"), 0, 0, tiled=True)

    sums, to_send = gate_up(slotted, w_in)
    out = down(sums, swap_cores(to_send), mine, w_down)
    out = lax.all_to_all(out, ("x", "y"), 0, 0, tiled=True)

    total = combine_rows(plane_index, out, owner_ranks, hidden, rows_dev)
    total = lax.all_to_all(total, ("z", "x", "y", "c"), 0, 0, tiled=True)
    return finish(total)


def solution(mesh):
    grid = Mesh(mesh.devices.reshape(NZ, NX, NY, NC), ("z", "x", "y", "c"))
    dev = ("x", "y", "c")
    every = ("z", "x", "y", "c")
    return jax.shard_map(
        per_device,
        mesh=grid,
        in_specs=(
            P("z", dev, None),
            P("z", None),
            P(every, None, None),
            P(every, None),
            P(every, None, None),
            P(every, None),
            P(every, None),
            P(dev, None, None),
            P(dev, None),
            P(),
            P(),
            P(),
            P(every, None, None),
            P(every, None, None),
            P(every, None, None),
        ),
        out_specs=P(every, None),
        check_vma=False,
    )
```

```python
import functools

import jax
import jax.numpy as jnp
from jax import lax
from jax.experimental import pallas as pl
from jax.experimental.pallas import tpu as pltpu
from jax.sharding import Mesh, PartitionSpec as P

LAT = 512
ROPE = 64
NOPE = 128
D = 7168
CAP = 192
NZ, NX, NY, NC = 4, 4, 4, 2
NXY = NX * NY
NDEV = NXY * NC
EXP_G = 8
CHUNK = D // NDEV
HALF = D // 2
PARTS = 4
LANES = 256
GROUP = 4
BLK = CHUNK * GROUP
STEPS = NXY // GROUP
ROWS = 128
ALL_ROWS = ROWS * NZ
F32 = jnp.float32
BF16 = jnp.bfloat16
SMALL = 16 * 1024 * 1024
LARGE = 20 * 1024 * 1024


def kept(shape, dtype):
    return pltpu.VMEM(shape, dtype)


def in_hbm(array):
    return pltpu.with_memory_space_constraint(array, pltpu.HBM)


def start_all(copies):
    for copy in copies:
        copy.start()
    return copies


WHOLE = pl.BlockSpec(memory_space=pltpu.VMEM)
SCALAR = pl.BlockSpec(memory_space=pltpu.SMEM)
ANYWHERE = pl.BlockSpec(memory_space=pl.ANY)


def attend(query_row, cache_block, valid_mask, own_entry):
    scale_factor = (NOPE + ROPE) ** (-0.5)
    scores = jnp.einsum("hc,kc->hk", query_row, cache_block, preferred_element_type=F32) * scale_factor
    if valid_mask is not None:
        scores = jnp.where(valid_mask[None, :], scores, -jnp.inf)
    own_score = jnp.einsum("hc,c->h", query_row, own_entry, preferred_element_type=F32) * scale_factor
    maximum = jnp.maximum(jnp.max(scores, axis=1), own_score)
    exponent = jnp.exp(scores - maximum[:, None])
    own_exponent = jnp.exp(own_score - maximum)
    totals = jnp.sum(exponent, axis=1) + own_exponent
    weights = (exponent / totals[:, None]).astype(BF16)
    own_weight = (own_exponent / totals).astype(BF16)
    context = jnp.einsum("hk,kl->hl", weights, cache_block[:, :LAT], preferred_element_type=F32)
    context = context + own_weight.astype(F32)[:, None] * own_entry[:LAT].astype(F32)[None, :]
    return context.astype(BF16)


def pack_chunk(ref, at, part):
    rows, most = part.shape[0], part.shape[0] * 3 // 4
    rest = part[:, 128:]
    ref[at, :rows, :] = part[:, :128].astype(ref.dtype)
    ref[at, rows:, :96] = rest[:most].astype(ref.dtype)
    tail = jnp.concatenate([rest[most:, 32 * i : 32 * (i + 1)] for i in range(3)], axis=0)
    ref[at, rows:, 96:] = tail.astype(ref.dtype)


def unpack_chunk(packed):
    rows = packed.shape[0] * 4 // 7
    most, few = rows * 3 // 4, rows // 4
    rest = packed[rows:, :96]
    tail = [packed[rows + few * i : rows + few * (i + 1), 96:] for i in range(3)]
    rest = jnp.concatenate([rest, jnp.concatenate(tail, axis=1)], axis=0)
    return jnp.concatenate([packed[:rows], rest], axis=1)


def spread_kernel(owners_hbm, cache_ref, out_ref, owners_ref, held_ref, packed_ref, owner_sem, in_sem, out_sem):
    owners_copy = pltpu.make_async_copy(owners_hbm, owners_ref, owner_sem)
    owners_copy.start()
    batch = NDEV // in_sem.shape[0]
    tokens, half = cache_ref.shape[1], cache_ref.shape[1] // 2
    arrive = []
    for b in range(in_sem.shape[0]):
        at = pl.ds(b * batch, batch)
        arrive.append(pltpu.make_async_copy(cache_ref.at[at], held_ref.at[at], in_sem.at[b]))
    start_all(arrive)
    owners_copy.wait()
    leave = [
        pltpu.make_async_copy(packed_ref.at[p], out_ref.at[owners_ref[0, p]], out_sem.at[p])
        for p in range(NDEV)
    ]
    for p in range(NDEV):
        if p % batch == 0:
            arrive[p // batch].wait()
        for j in range(LAT // 128):
            packed_ref[p, j * tokens : (j + 1) * tokens, :] = held_ref[p, :, j * 128 : (j + 1) * 128]
        tail = jnp.concatenate([held_ref[p, :half, LAT:], held_ref[p, half:, LAT:]], axis=1)
        packed_ref[p, LAT // 128 * tokens :, :] = tail
        leave[p].start()
    for p in range(NDEV):
        leave[p].wait()


def spread(owners, cache):
    packed = (NDEV, cache.shape[1] * cache.shape[2] // 128, 128)
    return pl.pallas_call(
        spread_kernel,
        in_specs=[ANYWHERE, ANYWHERE],
        out_specs=ANYWHERE,
        scratch_shapes=[
            pltpu.SMEM(owners.shape, owners.dtype),
            pltpu.VMEM(cache.shape, cache.dtype),
            pltpu.VMEM(packed, cache.dtype),
            pltpu.SemaphoreType.DMA,
            pltpu.SemaphoreType.DMA((8,)),
            pltpu.SemaphoreType.DMA((NDEV,)),
        ],
        out_shape=pltpu.HBM(packed, cache.dtype),
        compiler_params=pltpu.CompilerParams(vmem_limit_bytes=SMALL),
        name="spread",
    )(in_hbm(owners), in_hbm(cache))


def prompt_kernel(
    half_ref, query_hbm, cache_ref, entry_ref, old_hbm, uv_hbm, w_hbm, res_hbm, got_hbm,
    out_ref, uv_ref, w_ref, old_ref, query_ref, sems,
):
    heads_all = query_hbm.shape[1]
    query_copy = pltpu.make_async_copy(query_hbm, query_ref, sems.at[0])
    old_copy = pltpu.make_async_copy(old_hbm, old_ref, sems.at[1])
    uv_copy = pltpu.make_async_copy(uv_hbm, uv_ref, sems.at[2])
    depth = w_hbm.shape[0]
    at = pl.ds(pl.multiple_of(half_ref[0] * HALF, 128), HALF)
    w_copies = [pltpu.make_async_copy(res_hbm.at[:, at], w_ref.at[pl.ds(2 * depth, 16), :], sems.at[3])]
    span = depth // PARTS
    for n in range(PARTS):
        rows = pl.ds(n * span, span)
        w_copies.append(pltpu.make_async_copy(w_hbm.at[rows, at], w_ref.at[rows, :], sems.at[4 + n]))
        w_copies.append(
            pltpu.make_async_copy(
                got_hbm.at[rows, :], w_ref.at[pl.ds(depth + n * span, span), :], sems.at[4 + PARTS + n]
            )
        )
    w_copies.append(
        pltpu.make_async_copy(
            got_hbm.at[pl.ds(depth, 16), :], w_ref.at[pl.ds(2 * depth + 16, 16), :], sems.at[4 + 2 * PARTS]
        )
    )
    start_all([query_copy, old_copy, uv_copy] + w_copies)
    scale_factor = (NOPE + ROPE) ** (-0.5)
    sources, tokens = cache_ref.shape[0], cache_ref.shape[1] * 128 // query_ref.shape[0]
    tiles = [cache_ref[:, j * tokens : (j + 1) * tokens, :].reshape(-1, 128) for j in range(LAT // 128)]
    cache = jnp.concatenate(tiles, axis=1)
    rope = cache_ref[:, LAT // 128 * tokens :, :].reshape(-1, 128)
    entry = entry_ref[:1, :]
    query_copy.wait()
    query = query_ref[...]
    tail = query[LAT:, :]
    blank = jnp.zeros_like(tail)
    tail = jnp.concatenate(
        [jnp.concatenate([tail, blank], axis=0), jnp.concatenate([blank, tail], axis=0)], axis=1
    )
    extra = jnp.dot(rope, tail, preferred_element_type=F32)
    extra = [extra[:, h * heads_all : (h + 1) * heads_all].reshape(sources, -1, heads_all) for h in range(2)]
    scores = jnp.dot(cache, query[:LAT, :], preferred_element_type=F32)
    scores = (scores + jnp.concatenate(extra, axis=1).reshape(scores.shape)) * scale_factor
    own_score = jnp.dot(entry, query, preferred_element_type=F32) * scale_factor
    maximum = jnp.maximum(jnp.max(scores, axis=0, keepdims=True), own_score)
    exponent = jnp.exp(scores - maximum)
    own_exponent = jnp.exp(own_score - maximum)
    totals = jnp.sum(exponent, axis=0, keepdims=True) + own_exponent
    inverse = 1.0 / totals
    weights = (exponent * inverse).astype(BF16)
    own_weight = (own_exponent * inverse).astype(BF16)
    over_rows = (((0,), (0,)), ((), ()))
    context = lax.dot_general(weights, cache, over_rows, preferred_element_type=F32)
    context = context + lax.dot_general(own_weight, entry[:, :LAT], over_rows, preferred_element_type=F32)
    rows, block = out_ref.shape[0], out_ref.shape[0] // NDEV
    heads = heads_all // NDEV
    to = lax.broadcasted_iota(jnp.int32, (rows, heads_all), 0)
    source = jnp.where(to % block < heads, to // block * heads + to % block, -1)
    order = (lax.broadcasted_iota(jnp.int32, (rows, heads_all), 1) == source).astype(BF16)
    placed = jnp.dot(order, context.astype(BF16), preferred_element_type=F32)
    old_copy.wait()
    out_ref[...] = (placed + old_ref[...].astype(F32)).astype(BF16)
    uv_copy.wait()
    for copy in w_copies:
        copy.wait()


def prompt_attention(half, query, cache, entry, old, w_uv, w_out, res, got):
    rows = old.shape[0]
    return pl.pallas_call(
        prompt_kernel,
        in_specs=[SCALAR, ANYWHERE, WHOLE, WHOLE] + [ANYWHERE] * 5,
        out_specs=[WHOLE, ANYWHERE, ANYWHERE],
        out_shape=[
            kept((rows, LAT), BF16), kept(w_uv.shape, BF16), kept((2 * got.shape[0], HALF), BF16),
        ],
        scratch_shapes=[
            pltpu.VMEM((rows, LAT), BF16),
            pltpu.VMEM(query.shape, BF16),
            pltpu.SemaphoreType.DMA((5 + 2 * PARTS,)),
        ],
        compiler_params=pltpu.CompilerParams(vmem_limit_bytes=LARGE),
        name="prompt_attention",
    )(half, in_hbm(query), cache, entry, *[in_hbm(a) for a in (old, w_uv, w_out, res, got)])


def values_kernel(context_ref, uv_ref, attn_ref):
    heads, rows = uv_ref.shape[0], context_ref.shape[0]
    context = context_ref[...]
    pick = lax.broadcasted_iota(jnp.int32, (ROWS, rows), 1) // heads
    pick = (pick == lax.broadcasted_iota(jnp.int32, (ROWS, rows), 0)).astype(BF16)
    width = uv_ref.shape[2]
    row_head = lax.broadcasted_iota(jnp.int32, (rows, 2 * width), 0) % heads
    lane_head = lax.broadcasted_iota(jnp.int32, (rows, 2 * width), 1) // width
    for h in range(0, heads, 2):
        values = jnp.concatenate([uv_ref[h], uv_ref[h + 1]], axis=1)
        values = jnp.dot(context, values, preferred_element_type=F32)
        values = jnp.where(row_head == lane_head + h, values, 0.0).astype(BF16)
        values = jnp.dot(pick, values, preferred_element_type=F32).astype(BF16)
        attn_ref[:, h * width : (h + 2) * width] = values


def head_values(context, w_uv):
    return pl.pallas_call(
        values_kernel,
        in_specs=[WHOLE, WHOLE],
        out_specs=WHOLE,
        out_shape=kept((ROWS, w_uv.shape[0] * w_uv.shape[2]), BF16),
        compiler_params=pltpu.CompilerParams(vmem_limit_bytes=SMALL),
        name="head_values",
    )(context, w_uv)


def project_kernel(own_ref, got_ref, place_ref, w_ref, out_ref):
    lhs = (own_ref[...], got_ref[...], jnp.concatenate([place_ref[0], place_ref[1]], axis=1))
    for i in range(STEPS):
        at, acc = 0, jnp.zeros((ROWS, BLK), F32)
        for left in lhs:
            acc = acc + jnp.dot(
                left, w_ref[at : at + left.shape[1], i * BLK : (i + 1) * BLK], preferred_element_type=F32
            )
            at += left.shape[1]
        for g in range(GROUP):
            pack_chunk(out_ref, i * GROUP + g, acc[:, g * CHUNK : (g + 1) * CHUNK])


def project(own, got, place, w_out):
    return pl.pallas_call(
        project_kernel,
        in_specs=[WHOLE] * 4,
        out_specs=WHOLE,
        out_shape=kept((NXY, ROWS * CHUNK // 128, 128), BF16),
        compiler_params=pltpu.CompilerParams(vmem_limit_bytes=SMALL),
        name="project",
    )(own, got, place, w_out)


def rows_kernel(rows_dev, part_ref, gain_ref, router_ref, ids_ref, packed_ref, hidden_ref):
    total = part_ref[0].astype(F32)
    for source in range(1, part_ref.shape[0]):
        total = total + part_ref[source].astype(F32)
    total = unpack_chunk(total.astype(BF16))
    to = lax.broadcasted_iota(jnp.int32, (ROWS, ROWS), 0)
    order = to % (ROWS // rows_dev) * rows_dev + to // (ROWS // rows_dev)
    order = (lax.broadcasted_iota(jnp.int32, (ROWS, ROWS), 1) == order).astype(BF16)
    hidden_ref[...] = jnp.dot(order, total, preferred_element_type=F32)
    hidden = total.astype(F32)
    square = jnp.sum(hidden * hidden, axis=1, keepdims=True)
    scaled = (hidden * gain_ref[...]).astype(BF16)
    logits = jnp.dot(scaled, router_ref[...], preferred_element_type=F32)
    expert = lax.broadcasted_iota(jnp.int32, logits.shape, 1)
    lane = lax.broadcasted_iota(jnp.int32, (ROWS, LANES - CHUNK), 1)
    top = ids_ref.shape[1]
    spare = jnp.zeros((ROWS, LANES - CHUNK), F32)
    for k in range(top + 1):
        value = square
        if k < top:
            value = jnp.sum(jnp.where(expert == ids_ref[:, k : k + 1], logits, 0.0), axis=1, keepdims=True)
        high = value.astype(BF16).astype(F32)
        at_high, at_low = (k, top + k) if k < top else (2 * top, 2 * top + 1)
        spare = jnp.where(lane == at_high, high, jnp.where(lane == at_low, value - high, spare))
    packed_ref[:, :CHUNK] = scaled
    packed_ref[:, CHUNK:] = spare.astype(BF16)


def pack_rows(part, gain, router, ids, rows_dev):
    return pl.pallas_call(
        functools.partial(rows_kernel, rows_dev),
        out_shape=[kept((ROWS, LANES), BF16), kept((ROWS, CHUNK), F32)],
        compiler_params=pltpu.CompilerParams(vmem_limit_bytes=SMALL),
        name="pack_rows",
    )(part, gain, router, ids)


def slot_kernel(after_ref, ranks_ref, *refs):
    packed_refs, out_ref, rows_ref = refs[:NZ], refs[NZ], refs[NZ + 1]
    for k in range(NZ):
        rows_ref[k * ROWS : (k + 1) * ROWS, :] = packed_refs[k][...]
    slot = lax.broadcasted_iota(jnp.int32, (CAP, ALL_ROWS), 0)
    for e in range(EXP_G):
        table = (ranks_ref[e : e + 1, :] == slot).astype(BF16)
        slotted = jnp.dot(table, rows_ref[...], preferred_element_type=F32).astype(BF16)
        out_ref[2 * e] = slotted
        out_ref[2 * e + 1] = slotted


def slot_rows(after, ranks, packed):
    return pl.pallas_call(
        slot_kernel,
        in_specs=[ANYWHERE] + [WHOLE] * (1 + NZ),
        out_specs=WHOLE,
        out_shape=kept((NXY, CAP, LANES), BF16),
        scratch_shapes=[pltpu.VMEM((ALL_ROWS, LANES), BF16)],
        compiler_params=pltpu.CompilerParams(vmem_limit_bytes=SMALL),
        name="slot_rows",
    )(after, ranks, *packed)


def combine_kernel(plane_ref, out_ref, ranks_ref, hidden_ref, rows_ref, acc_ref):
    slot = lax.broadcasted_iota(jnp.int32, (ALL_ROWS, CAP), 1)
    acc = jnp.zeros((ALL_ROWS, CHUNK), F32)
    for e in range(EXP_G):
        table = (ranks_ref[:, e : e + 1] == slot).astype(BF16)
        both = out_ref[2 * e].astype(F32) + out_ref[2 * e + 1].astype(F32)
        acc = acc + jnp.dot(table, unpack_chunk(both.astype(BF16)), preferred_element_type=F32)
    acc_ref[...] = acc
    span, count = rows_ref.shape[0], rows_ref.shape[1]
    own = ROWS // count
    for r in range(count):
        at = pl.multiple_of(r * span + plane_ref[0] * own, 8)
        acc_ref[pl.ds(at, own), :] += hidden_ref[r * own : (r + 1) * own, :]
    for r in range(count):
        rows_ref[:, r, :] = acc_ref[r * span : (r + 1) * span, :].astype(BF16)


def combine_rows(plane, out, ranks, hidden, count):
    vmem = pl.BlockSpec(memory_space=pltpu.VMEM)
    return pl.pallas_call(
        combine_kernel,
        in_specs=[pl.BlockSpec(memory_space=pltpu.SMEM), vmem, vmem, vmem],
        out_specs=vmem,
        out_shape=kept((ALL_ROWS // count, count, CHUNK), BF16),
        scratch_shapes=[pltpu.VMEM((ALL_ROWS, CHUNK), F32)],
        compiler_params=pltpu.CompilerParams(vmem_limit_bytes=SMALL),
        name="combine_rows",
    )(plane, out, ranks, hidden)


def give_kernel(
    half_ref, out_hbm, res_hbm, gate_hbm, up_hbm, down_hbm, to_out, to_in, to_down,
    out_ref, in_ref, down_ref, in_sems, out_sems,
):
    depth = out_hbm.shape[0]
    columns = pl.ds(pl.multiple_of(half_ref[0] * HALF, 128), HALF)
    rows = pl.ds(pl.multiple_of(half_ref[0] * HALF, 16), HALF)
    sources = (
        (out_hbm.at[:, columns], out_ref.at[pl.ds(0, depth), :], to_out.at[pl.ds(0, depth), :]),
        (res_hbm.at[:, columns], out_ref.at[pl.ds(depth, 16), :], to_out.at[pl.ds(depth, 16), :]),
        (gate_hbm.at[0, rows, :], in_ref.at[0], to_in.at[0]),
        (up_hbm.at[0, rows, :], in_ref.at[1], to_in.at[1]),
        (down_hbm.at[0, :, columns], down_ref, to_down),
    )
    arrive = [pltpu.make_async_copy(a, b, in_sems.at[n]) for n, (a, b, _) in enumerate(sources)]
    leave = [pltpu.make_async_copy(b, c, out_sems.at[n]) for n, (_, b, c) in enumerate(sources)]
    start_all(arrive)
    for first, second in zip(arrive, leave):
        first.wait()
        second.start()
    for copy in leave:
        copy.wait()


def give_weights(half, w_out, res, w_gate, w_up, w_down):
    hidden = w_gate.shape[2]
    arrays = (w_out, res, w_gate, w_up, w_down)
    return pl.pallas_call(
        give_kernel,
        in_specs=[SCALAR] + [ANYWHERE] * 5,
        out_specs=[ANYWHERE] * 3,
        out_shape=[
            pltpu.HBM((w_out.shape[0] + 16, HALF), BF16),
            pltpu.HBM((2, HALF, hidden), BF16),
            pltpu.HBM((hidden, HALF), BF16),
        ],
        scratch_shapes=[
            pltpu.VMEM((w_out.shape[0] + 16, HALF), BF16),
            pltpu.VMEM((2, HALF, hidden), BF16),
            pltpu.VMEM((hidden, HALF), BF16),
            pltpu.SemaphoreType.DMA((5,)),
            pltpu.SemaphoreType.DMA((5,)),
        ],
        compiler_params=pltpu.CompilerParams(vmem_limit_bytes=SMALL),
        name="give_weights",
    )(half, *[in_hbm(a) for a in arrays])


def fetch_kernel(
    after_ref, half_ref, gate_hbm, up_hbm, down_hbm, got_in_hbm, got_down_hbm, in_ref, down_ref, sems
):
    hidden = gate_hbm.shape[2]
    columns = pl.ds(pl.multiple_of(half_ref[0] * HALF, 128), HALF)
    rows = pl.ds(pl.multiple_of(half_ref[0] * HALF, 16), HALF)
    sources = (gate_hbm.at[0, rows, :], up_hbm.at[0, rows, :], got_in_hbm.at[0], got_in_hbm.at[1])
    copies = [
        pltpu.make_async_copy(source, in_ref.at[:, pl.ds(j * hidden, hidden)], sems.at[j])
        for j, source in enumerate(sources)
    ]
    copies.append(
        pltpu.make_async_copy(down_hbm.at[0, :, columns], down_ref.at[pl.ds(0, hidden), :], sems.at[4])
    )
    copies.append(pltpu.make_async_copy(got_down_hbm, down_ref.at[pl.ds(hidden, hidden), :], sems.at[5]))
    for copy in start_all(copies):
        copy.wait()


def fetch_experts(after, half, w_gate, w_up, w_down, got_in, got_down):
    hidden = w_gate.shape[2]
    return pl.pallas_call(
        fetch_kernel,
        in_specs=[ANYWHERE, SCALAR] + [ANYWHERE] * 5,
        out_specs=[ANYWHERE] * 2,
        out_shape=[kept((HALF, 4 * hidden), BF16), kept((2 * hidden, HALF), BF16)],
        scratch_shapes=[pltpu.SemaphoreType.DMA((6,))],
        compiler_params=pltpu.CompilerParams(vmem_limit_bytes=SMALL),
        cost_estimate=pl.CostEstimate(flops=0, bytes_accessed=12 * D * hidden, transcendentals=0),
        name="fetch_experts",
    )(after, half, *[in_hbm(a) for a in (w_gate, w_up, w_down, got_in, got_down)])


def gate_up_kernel(y_ref, w_ref, own_ref, send_ref):
    width = w_ref.shape[1]
    acc = jnp.zeros((CAP, width), F32)
    stats = jnp.zeros((CAP, LANES - CHUNK), F32)
    for p in range(NXY):
        acc = acc + jnp.dot(
            y_ref[p, :, :CHUNK], w_ref[p * CHUNK : (p + 1) * CHUNK, :], preferred_element_type=F32
        )
        stats = stats + y_ref[p, :, CHUNK:].astype(F32)
    own_ref[:, :width] = acc
    send_ref[:, :width] = acc.astype(BF16)
    high = stats.astype(BF16).astype(F32)
    spare = jnp.zeros((CAP, 128 - 2 * stats.shape[1]), F32)
    own_ref[:, width:] = jnp.concatenate([stats, jnp.zeros_like(stats), spare], axis=1)
    send_ref[:, width:] = jnp.concatenate([high, stats - high, spare], axis=1).astype(BF16)


def gate_up(y, w):
    width = w.shape[1] + 128
    return pl.pallas_call(
        gate_up_kernel,
        in_specs=[WHOLE] * 2,
        out_specs=[WHOLE] * 2,
        out_shape=[kept((CAP, width), F32), kept((CAP, width), BF16)],
        compiler_params=pltpu.CompilerParams(vmem_limit_bytes=SMALL),
        name="gate_up",
    )(y, w)


def down_kernel(own_ref, got_ref, mine_ref, w_ref, out_ref):
    slices = w_ref.shape[0]
    hidden = slices // 2
    width = 2 * slices
    lanes = LANES - CHUNK
    stats = own_ref[:, width : width + lanes]
    stats = stats + got_ref[:, width : width + lanes].astype(F32)
    stats = stats + got_ref[:, width + lanes : width + 2 * lanes].astype(F32)
    square = stats[:, 16:17] + stats[:, 17:18]
    scale = lax.rsqrt(square * (1.0 / D) + 1e-6)
    affinity = jax.nn.sigmoid((stats[:, 0:8] + stats[:, 8:16]) * scale)
    own = jnp.sum(affinity * mine_ref[...], axis=1, keepdims=True)
    gates = 2.5 * own / jnp.sum(affinity, axis=1, keepdims=True)
    gates = gates.astype(BF16).astype(F32)
    acts = []
    for j in range(2):
        here, there = j * slices, (1 - j) * slices
        both = own_ref[:, here : here + slices] + got_ref[:, there : there + slices].astype(F32)
        gate = both[:, :hidden] * scale
        acts.append((gate * jax.nn.sigmoid(gate) * (both[:, hidden:] * scale)).astype(BF16))
    act = jnp.concatenate(acts, axis=1)
    for i in range(STEPS):
        acc = jnp.dot(act, w_ref[:, i * BLK : (i + 1) * BLK], preferred_element_type=F32) * gates
        for g in range(GROUP):
            pack_chunk(out_ref, i * GROUP + g, acc[:, g * CHUNK : (g + 1) * CHUNK])


def down(own, got, mine, w):
    return pl.pallas_call(
        down_kernel,
        in_specs=[WHOLE] * 4,
        out_specs=WHOLE,
        out_shape=kept((NXY, CAP * CHUNK // 128, 128), BF16),
        compiler_params=pltpu.CompilerParams(vmem_limit_bytes=SMALL),
        name="down",
    )(own, got, mine, w)


def finish_kernel(total_ref, out_ref):
    for c in range(NC):
        for p in range(NXY):
            row = sum(total_ref[z * NDEV + p * NC + c].astype(F32) for z in range(NZ))
            at = (c * NXY + p) * CHUNK
            out_ref[:, at : at + CHUNK] = row.astype(BF16)


def finish(total):
    return pl.pallas_call(
        finish_kernel,
        in_specs=[WHOLE],
        out_specs=WHOLE,
        out_shape=jax.ShapeDtypeStruct((total.shape[1], D), BF16),
        compiler_params=pltpu.CompilerParams(vmem_limit_bytes=SMALL),
        name="finish",
    )(total)


def swap_cores(values):
    return lax.ppermute(values, "c", [(0, 1), (1, 0)])


def per_device(
    prompt_cache,
    assignment,
    resident_cache,
    resident_len,
    queries,
    new_latent,
    residual,
    w_uv,
    w_out,
    norm_gain,
    w_router,
    expert_ids,
    w_gate,
    w_up,
    w_down,
):
    plane = lax.axis_index("z")
    core = lax.axis_index("c")
    place_xy = lax.axis_index("x") * NY + lax.axis_index("y")
    rows_dev = queries.shape[0]
    own_half = jnp.reshape(core, (1,)).astype(jnp.int32)
    other_half = 1 - own_half
    plane_index = jnp.reshape(plane, (1,)).astype(jnp.int32)
    chunk = core * NXY + place_xy

    received = lax.all_to_all(spread(assignment, prompt_cache), ("x", "y", "c"), 0, 0, tiled=True)

    ids_plane = expert_ids - plane * EXP_G
    named = jnp.any(expert_ids[:, :, None] == jnp.arange(NZ * EXP_G, dtype=jnp.int32)[None, None, :], axis=1)
    lower = (jnp.arange(ALL_ROWS)[:, None] > jnp.arange(ALL_ROWS)[None, :]).astype(BF16)
    ranks = jnp.dot(lower, named.astype(BF16), preferred_element_type=F32).astype(jnp.int32)
    ranks = jnp.where(named, ranks, -1)
    plane_ranks = lax.dynamic_slice_in_dim(ranks, plane * EXP_G, EXP_G, 1)
    own_expert = place_xy // 2
    slot_iota = jnp.arange(CAP, dtype=jnp.int32)
    own_ranks = lax.dynamic_index_in_dim(plane_ranks, own_expert, 1, keepdims=False)
    own_slots = (own_ranks[None, :] == slot_iota[:, None]).astype(BF16)
    slot_ids = jnp.dot(own_slots, ids_plane.astype(BF16), preferred_element_type=F32)
    mine = (slot_ids == own_expert.astype(F32)).astype(F32)
    group_ids = lax.dynamic_slice_in_dim(expert_ids, plane * ROWS, ROWS, 0)
    by_group = plane_ranks.reshape(NZ, ROWS, EXP_G)
    step_order = (plane - jnp.arange(NZ, dtype=jnp.int32)) % NZ
    step_ranks = by_group.at[step_order].get(mode="promise_in_bounds").reshape(ALL_ROWS, EXP_G).T
    owner_ranks = plane_ranks.reshape(NZ * NDEV, rows_dev, EXP_G).transpose(1, 0, 2).reshape(ALL_ROWS, EXP_G)
    gain_chunk = lax.dynamic_slice_in_dim(norm_gain, chunk * CHUNK, CHUNK, 0).astype(F32)[None, :]
    router_chunk = lax.dynamic_slice_in_dim(w_router, chunk * CHUNK, CHUNK, 0)
    row_iota = jnp.arange(ROWS, dtype=jnp.int32)
    pair = jnp.arange(2, dtype=jnp.int32)
    first_rows = (place_xy * NC + core + pair * (1 - 2 * core)) * rows_dev
    place = row_iota[None, :, None] == (first_rows[:, None] + jnp.arange(16, dtype=jnp.int32)[None, :])[:, None, :]
    place = (place & (jnp.arange(16) < rows_dev)[None, None, :]).astype(BF16)
    res = jnp.pad(residual, ((0, 16 - rows_dev), (0, 0)))

    given = give_weights(other_half, w_out, res, w_gate, w_up, w_down)
    got_out, got_in, got_down = [swap_cores(a) for a in given]

    cache_iota = jnp.arange(resident_cache.shape[1], dtype=jnp.int32)
    old_masks = cache_iota[None, :] < resident_len[0][:, None]
    context_old = jax.vmap(attend)(queries[1:], resident_cache, old_masks, new_latent[1:])
    context_old = context_old.reshape(rows_dev - 1, NDEV, -1, LAT).transpose(1, 0, 2, 3)
    context_old = jnp.pad(context_old, ((0, 0), (1, 0), (0, 0), (0, 0))).reshape(-1, LAT)
    held = (
        received, context_old, queries[0].T, step_ranks, owner_ranks, mine, group_ids, gain_chunk,
        router_chunk, place, res, own_half, plane_index, got_out, got_in, got_down,
    )
    (
        received, context_old, first_query, step_ranks, owner_ranks, mine, group_ids, gain_chunk,
        router_chunk, place, res, own_half, plane_index, got_out, got_in, got_down,
    ) = lax.optimization_barrier(held)
    context, w_uv, w_out = prompt_attention(
        own_half, first_query, received, new_latent, context_old, w_uv, w_out, res, got_out
    )

    context = lax.all_to_all(context.reshape(NDEV, -1, LAT), ("x", "y", "c"), 0, 0, tiled=True)
    context = context.reshape(-1, LAT)

    attn = head_values(context, w_uv)
    partial = project(attn, swap_cores(attn), place, w_out)
    partial = lax.all_to_all(partial, ("x", "y"), 0, 0, tiled=True)

    packed, hidden = pack_rows(partial, gain_chunk, router_chunk, group_ids, rows_dev)

    groups = [packed]
    for k in range(1, NZ):
        groups.append(lax.ppermute(packed, "z", [(i, (i + k) % NZ) for i in range(NZ)]))
    w_in, w_down = fetch_experts(packed, own_half, w_gate, w_up, w_down, got_in, got_down)
    slotted = slot_rows(w_down, step_ranks, groups)
    slotted = lax.all_to_all(slotted, ("x", "y"), 0, 0, tiled=True)

    sums, to_send = gate_up(slotted, w_in)
    out = down(sums, swap_cores(to_send), mine, w_down)
    out = lax.all_to_all(out, ("x", "y"), 0, 0, tiled=True)

    total = combine_rows(plane_index, out, owner_ranks, hidden, rows_dev)
    total = lax.all_to_all(total, ("z", "x", "y", "c"), 0, 0, tiled=True)
    return finish(total)


def solution(mesh):
    grid = Mesh(mesh.devices.reshape(NZ, NX, NY, NC), ("z", "x", "y", "c"))
    dev = ("x", "y", "c")
    every = ("z", "x", "y", "c")
    return jax.shard_map(
        per_device,
        mesh=grid,
        in_specs=(
            P("z", dev, None),
            P("z", None),
            P(every, None, None),
            P(every, None),
            P(every, None, None),
            P(every, None),
            P(every, None),
            P(dev, None, None),
            P(dev, None),
            P(),
            P(),
            P(),
            P(every, None, None),
            P(every, None, None),
            P(every, None, None),
        ),
        out_specs=P(every, None),
        check_vma=False,
    )
```
